32 devices in a mesh: nodes: 8 (over z, x), rep: 4 (over y, core).
Axes of the slice: x: 2, y: 2, z: 4, core: 2. Of those that a mesh axis runs over, the one named last changes fastest.
Arguments:
- features: bfloat16 [16384, 128], P(('nodes', 'rep')), may hold values from -12 to 12
- node_count: int32 [32], P(('nodes', 'rep')), may hold values from 256 to 512, as said below
- neighbours: int32 [16384, 16], P(('nodes', 'rep')), may hold values from -1 to 16383, as said below
- neighbour_count: int32 [16384], P(('nodes', 'rep')), may hold values from 1 to 16
- label_mask: int32 [16384], P(('nodes', 'rep')), may hold values from 0 to 1, as said below
- labels: int32 [16384], P(('nodes', 'rep')), may hold values from 0 to 46
- encoder_weight: float32 [128, 256], P('nodes'), may hold values from -1 to 1
- layer_weights: float32 [3, 512, 256], P(None, 'nodes'), may hold values from -1 to 1
- head_weight: float32 [256, 47], P('nodes'), may hold values from -0.375 to 0.375
- biases: float32 [4, 256], P(None, 'nodes'), may hold values from -1.75 to 1.75
- class_bias: float32 [47], replicated, may hold values from -3 to 3
- mean_encoder: float32 [128, 256], P('nodes'), may hold values from -0.0029296875 to 0.0029296875
- mean_layers: float32 [3, 512, 256], P(None, 'nodes'), may hold values from -0.009765625 to 0.009765625
- mean_head: float32 [256, 47], P('nodes'), may hold values from -0.009765625 to 0.009765625
- mean_biases: float32 [4, 256], P(None, 'nodes'), may hold values from -0.0390625 to 0.0390625
- mean_class: float32 [47], replicated, may hold values from -0.0390625 to 0.0390625
- square_encoder: float32 [128, 256], P('nodes'), may hold values from 6.832359e-08 to 2.7329435e-07
- square_layers: float32 [3, 512, 256], P(None, 'nodes'), may hold values from 2.277453e-06 to 9.109812e-06
- square_head: float32 [256, 47], P('nodes'), may hold values from 2.277453e-06 to 9.109812e-06
- square_biases: float32 [4, 256], P(None, 'nodes'), may hold values from 3.6439247e-05 to 0.00014575699
- square_class: float32 [47], replicated, may hold values from 3.6439247e-05 to 0.00014575699
Outputs:
- updated_encoder: float32 [128, 256], P('nodes')
- updated_layers: float32 [3, 512, 256], P(None, 'nodes')
- updated_head: float32 [256, 47], P('nodes')
- updated_biases: float32 [4, 256], P(None, 'nodes')
- updated_class: float32 [47], replicated
- drift_encoder: float32 [128, 256], P('nodes')
- drift_layers: float32 [3, 512, 256], P(None, 'nodes')
- drift_head: float32 [256, 47], P('nodes')
- drift_biases: float32 [4, 256], P(None, 'nodes')
- drift_class: float32 [47], replicated
- spread_encoder: float32 [128, 256], P('nodes')
- spread_layers: float32 [3, 512, 256], P(None, 'nodes')
- spread_head: float32 [256, 47], P('nodes')
- spread_biases: float32 [4, 256], P(None, 'nodes')
- spread_class: float32 [47], replicated
- copied_encoder: bfloat16 [128, 256], P('nodes')
- copied_layers: bfloat16 [3, 512, 256], P(None, 'nodes')
- copied_head: bfloat16 [256, 47], P('nodes')
- copied_biases: bfloat16 [4, 256], P(None, 'nodes')
- loss_sum: float32 [], replicated
- label_total: float32 [], replicated
- grad_norm: float32 [], replicated
The draws below stay inside these ranges and needn't reach their ends.
Inputs may be any that keep to these rules, and one draw needn't show every extreme that they name: `node_count`: slots below a device's count hold valid nodes; some device is full. `neighbours`: a live entry is a global slot number (device times 512 plus slot) of a valid node on a device whose nodes index differs by at most one from the node's own, with wrap-around; entries at or beyond the node's neighbour count are -1. `label_mask`: zero on slots that are not valid nodes; some node counts.
All inputs are finite; a program needn't handle non-finite values.
Results may differ from the reference program's by a relative error of at most 0.0094.
Values may be sent and summed in bfloat16 or wider, within the bound.
No kernel may reach another device: no remote copies, remote signals or barrier semaphores. Data moves between devices by JAX's collectives and lax.ppermute only.
A program may use at most 64 MiB of HBM per device.

```python
import math
import jax
import jax.numpy as jnp
from jax import lax

NPD = 512
IN = 128
H = 256
C = 47
FAN = 16
LAYERS = 3
STEP = 5
NODES = 16384
NPARAM = 439087
N_NODES = 8
N_REP = 4
DEVICES = 32


def node_totals(key):
    key = jax.random.fold_in(key, 11)
    totals = jax.random.randint(key, (DEVICES,), NPD // 2, NPD + 1)
    fullest = jax.random.randint(jax.random.fold_in(key, 1), (), 0, DEVICES)
    return jnp.where(jnp.arange(DEVICES) == fullest, NPD, totals).astype(jnp.int32)


def edge_totals(key):
    key = jax.random.fold_in(key, 12)
    totals = jax.random.randint(key, (NODES,), 1, FAN + 1)
    places = jnp.arange(NODES)
    totals = jnp.where(places == 0, FAN, totals)
    return jnp.where(places == 1, 1, totals).astype(jnp.int32)


def draw_node_count(key, part):
    return node_totals(key)


def draw_neighbour_count(key, part):
    return edge_totals(key)


def draw_neighbours(key, part):
    totals = node_totals(key)
    counts = edge_totals(key)
    key = jax.random.fold_in(key, 2)
    places = jnp.arange(NODES)
    group = places // NPD // N_REP
    step = jax.random.randint(jax.random.fold_in(key, 1), (NODES, FAN), -1, 2)
    member = jax.random.randint(jax.random.fold_in(key, 2), (NODES, FAN), 0, N_REP)
    owner = (group[:, None] + step) % N_NODES * N_REP + member
    slot = jax.random.randint(jax.random.fold_in(key, 3), (NODES, FAN), 0, totals[owner])
    targets = owner * NPD + slot
    used = jnp.arange(FAN)[None, :] < counts[:, None]
    return jnp.where(used, targets, -1).astype(jnp.int32)


def draw_label_mask(key, part):
    totals = node_totals(key)
    key = jax.random.fold_in(key, 3)
    places = jnp.arange(NODES)
    device = places // NPD
    limit = 250 + 500 * device // max(DEVICES - 1, 1)
    coin = jax.random.randint(key, (NODES,), 0, 1000)
    marked = (coin < limit) & (places % NPD < totals[device])
    return jnp.where(places == 0, 1, marked.astype(jnp.int32)).astype(jnp.int32)


def draw_features(key, part):
    key = jax.random.fold_in(key, 4)
    ramp = jnp.linspace(0.0, 1.0, IN)
    values = jnp.clip(jax.random.normal(key, (NODES, IN), jnp.float32), -4.0, 4.0)
    scales = 1.0 + 2.0 * ramp
    return (values * scales[None, :]).astype(jnp.bfloat16)


def draw_encoder_weight(key, part):
    key = jax.random.fold_in(key, 5)
    ramp = jnp.linspace(0.0, 1.0, H)
    values = jnp.clip(jax.random.normal(key, (IN, H), jnp.float32), -4.0, 4.0)
    scales = 0.5 + ramp
    return values * scales[None, :] * IN ** (-0.5)


def draw_layer_weights(key, part):
    key = jax.random.fold_in(key, 6)
    ramp = jnp.linspace(0.0, 1.0, H)
    values = jnp.clip(jax.random.normal(key, (LAYERS, 2 * H, H), jnp.float32), -4.0, 4.0)
    scales = 0.5 + ramp
    return values * scales[None, None, :] * (2 * H) ** (-0.5)


def with_ends(result, stream_key, least, high):
    index_at = [jax.random.randint(jax.random.fold_in(stream_key, axis), (), 0, length) for axis, length in enumerate(result.shape)]
    main_axis = result.shape.index(max(result.shape))
    neighbour = index_at[:main_axis] + [(index_at[main_axis] + 1) % result.shape[main_axis]] + index_at[main_axis + 1:]
    return result.at[tuple(index_at)].set(least).at[tuple(neighbour)].set(high)


def block_scale(rng, shape, cuts, smallest, top_value):
    gain, own = 1.0, jax.random.fold_in(rng, 6)
    for axis_at, blocks in cuts:
        steps = jnp.exp(jax.random.uniform(jax.random.fold_in(own, axis_at), (blocks,), jnp.float32, smallest / len(cuts), top_value / len(cuts)))
        gain = gain * jnp.repeat(steps, shape[axis_at] // blocks).reshape([-1 if axis == axis_at else 1 for axis in range(len(shape))])
    return gain


def noise(key, extent, deviation, bound, split=(), kind=jnp.bfloat16):
    drawn = jax.random.normal(key, extent, jnp.float32) * deviation
    if len(split) > 0:
        drawn = block_scale(key, extent, split, -0.22, 0.18) * drawn
    return jnp.clip(drawn, min=-bound, max=bound).astype(kind)


def setup_inputs(seed: int = 0) -> dict:
    key_of = jax.random.split(jax.random.key(seed), 22)
    return {
        "features": draw_features(jax.random.fold_in(key_of[21], 71), 0),
        "node_count": draw_node_count(jax.random.fold_in(key_of[21], 71), 0),
        "neighbours": draw_neighbours(jax.random.fold_in(key_of[21], 71), 0),
        "neighbour_count": draw_neighbour_count(jax.random.fold_in(key_of[21], 71), 0),
        "label_mask": draw_label_mask(jax.random.fold_in(key_of[21], 71), 0),
        "labels": with_ends(jax.random.randint(key_of[5], (NODES,), 0, C), jax.random.fold_in(key_of[5], 1), 0, C - 1).astype(jnp.int32),
        "encoder_weight": draw_encoder_weight(jax.random.fold_in(key_of[21], 71), 0),
        "layer_weights": draw_layer_weights(jax.random.fold_in(key_of[21], 71), 0),
        "head_weight": noise(key_of[8], (H, C), H ** -0.5, 0.375, ((0, 8),), jnp.float32),
        "biases": noise(key_of[9], (LAYERS + 1, H), 0.3, 1.75, ((1, 8),), jnp.float32),
        "class_bias": noise(key_of[10], (C,), 0.5, 3.0, (), jnp.float32),
        "mean_encoder": noise(key_of[11], (IN, H), (0.3 * NPARAM ** -0.5), 0.0029296875, ((0, 8),), jnp.float32),
        "mean_layers": noise(key_of[12], (LAYERS, 2 * H, H), (NPARAM ** -0.5), 0.009765625, ((1, 8),), jnp.float32),
        "mean_head": noise(key_of[13], (H, C), (NPARAM ** -0.5), 0.009765625, ((0, 8),), jnp.float32),
        "mean_biases": noise(key_of[14], (LAYERS + 1, H), (4 * NPARAM ** -0.5), 0.0390625, ((1, 8),), jnp.float32),
        "mean_class": noise(key_of[15], (C,), (4 * NPARAM ** -0.5), 0.0390625, (), jnp.float32),
        "square_encoder": jnp.clip(jnp.exp(math.log(2.732943471528415e-07) - 1.3862944 * jax.random.uniform(key_of[16], (IN, H), jnp.float32) ** block_scale(key_of[16], (IN, H), ((0, 8),), -0.2, 0.2)), 6.832358678821038e-08, 2.732943471528415e-07),
        "square_layers": jnp.clip(jnp.exp(math.log(9.109811799135059e-06) - 1.3862944 * jax.random.uniform(key_of[17], (LAYERS, 2 * H, H), jnp.float32) ** block_scale(key_of[17], (LAYERS, 2 * H, H), ((1, 8),), -0.2, 0.2)), 2.2774529497837648e-06, 9.109811799135059e-06),
        "square_head": jnp.clip(jnp.exp(math.log(9.109811799135059e-06) - 1.3862944 * jax.random.uniform(key_of[18], (H, C), jnp.float32) ** block_scale(key_of[18], (H, C), ((0, 8),), -0.2, 0.2)), 2.2774529497837648e-06, 9.109811799135059e-06),
        "square_biases": jnp.clip(jnp.exp(math.log(0.00014575699) - 1.3862944 * jax.random.uniform(key_of[19], (LAYERS + 1, H), jnp.float32) ** block_scale(key_of[19], (LAYERS + 1, H), ((1, 8),), -0.2, 0.2)), 3.6439247196540236e-05, 0.00014575699),
        "square_class": jnp.clip(jnp.exp(jax.random.uniform(key_of[20], (C,), jnp.float32, math.log(3.6439247196540236e-05), math.log(0.00014575699))), 3.6439247196540236e-05, 0.00014575699),
    }


beta_one = 0.5
beta_two = 0.5
rate = 0.05
decay = 0.01
epsilon = 1e-08

@jax.custom_vjp
def low(v):
    return lax.optimization_barrier(v.astype(jnp.bfloat16)).astype(jnp.float32)

@jax.custom_vjp
def low_back(v):
    return v

def low_keep(v):
    return (low(v), None)

def low_pass(kept, grad):
    return (grad,)

def back_keep(v):
    return (v, None)

def back_low(kept, grad):
    return (low(grad),)
low.defvjp(low_keep, low_pass)
low_back.defvjp(back_keep, back_low)

def matmul(left, right):
    return jnp.dot(left, right, precision=lax.Precision.HIGHEST, preferred_element_type=jnp.float32)

def act_norm(before):
    active = jax.nn.gelu(before)
    return active * lax.rsqrt(lax.optimization_barrier(jnp.mean(active * active, axis=-1, keepdims=True)) + 1e-06)

def forward(params, inputs, neighbours, valid_edge, inverse_count, valid_node, weight_mask, labels):
    encoder, layers, head, biases, class_bias = params
    biases_low = low(biases)
    hidden = (low_back(matmul(inputs, low(encoder))) + biases_low[0]) * valid_node[:, None]
    clamped = jnp.maximum(neighbours, 0)
    for layer in range(LAYERS):
        rounded = low(hidden)
        summed = jnp.zeros_like(rounded)
        for column in range(FAN):
            summed = summed + rounded[clamped[:, column]] * valid_edge[:, column:column + 1]
        summed = low_back(summed)
        averaged = low(summed * inverse_count[:, None])
        joined = jnp.concatenate([rounded, averaged], axis=1)
        before = low_back(matmul(joined, low(layers[layer]))) + biases_low[layer + 1]
        hidden = act_norm(before)
    logits = low_back(matmul(low(hidden), low(head))) + class_bias
    total_exp = jax.nn.logsumexp(logits, axis=1)
    picked = jnp.take_along_axis(logits, labels[:, None], axis=1)[:, 0]
    return jnp.sum(weight_mask * (total_exp - picked))

def adamw(weight, first, second, grad, scale):
    scaled = grad * scale
    drift = beta_one * first + (1.0 - beta_one) * scaled
    spread = beta_two * second + (1.0 - beta_two) * scaled * scaled
    corrected = drift / (1.0 - beta_one ** STEP)
    denominator = jnp.sqrt(spread / (1.0 - beta_two ** STEP)) + epsilon
    return (weight - rate * (corrected / denominator + decay * weight), drift, spread)

def reference(features, node_count, neighbours, neighbour_count, label_mask, labels, encoder_weight, layer_weights, head_weight, biases, class_bias, mean_encoder, mean_layers, mean_head, mean_biases, mean_class, square_encoder, square_layers, square_head, square_biases, square_class):
    places = jnp.arange(NODES, dtype=jnp.int32)
    owner = places // NPD
    valid_node = (places % NPD < node_count[owner]).astype(jnp.float32)
    slots = jnp.arange(FAN, dtype=jnp.int32)
    valid_edge = (slots[None, :] < neighbour_count[:, None]).astype(jnp.float32)
    inverse_count = 1.0 / neighbour_count.astype(jnp.float32)
    weight_mask = label_mask.astype(jnp.float32) * valid_node
    inputs = features.astype(jnp.float32)
    params = (encoder_weight, layer_weights, head_weight, biases, class_bias)
    loss_sum, pullback = jax.vjp(lambda chosen: forward(chosen, inputs, neighbours, valid_edge, inverse_count, valid_node, weight_mask, labels), params)
    grads = pullback(jnp.ones((), jnp.float32))[0]
    squares = jnp.zeros((), jnp.float32)
    for entry in grads:
        squares = squares + jnp.sum(entry * entry)
    grad_norm = jnp.sqrt(squares)
    scale = jnp.minimum(1.0, 1.0 / (grad_norm + 1e-06))
    firsts = (mean_encoder, mean_layers, mean_head, mean_biases, mean_class)
    seconds = (square_encoder, square_layers, square_head, square_biases, square_class)
    results = [adamw(params[index], firsts[index], seconds[index], grads[index], scale) for index in range(5)]
    updated = [entry[0] for entry in results]
    drifts = [entry[1] for entry in results]
    spreads = [entry[2] for entry in results]
    copies = [updated[index].astype(jnp.bfloat16) for index in range(4)]
    return (updated[0], updated[1], updated[2], updated[3], updated[4], drifts[0], drifts[1], drifts[2], drifts[3], drifts[4], spreads[0], spreads[1], spreads[2], spreads[3], spreads[4], copies[0], copies[1], copies[2], copies[3], loss_sum, jnp.sum(weight_mask), grad_norm)
```

```python
import functools

import jax
import jax.numpy as jnp
from jax import lax
from jax.experimental import pallas as pl
from jax.experimental.pallas import tpu as pltpu
from jax.sharding import PartitionSpec as P

LAYERS = 3
STEP = 5

beta_one = 0.5
beta_two = 0.5
rate = 0.05
decay = 0.01
epsilon = 1e-08

LANES = 128
BATCH = 256
PAD_AT = 64
VMEM_LIMIT = 14 << 20

bf16 = jnp.bfloat16
f32 = jnp.float32


def swap(array, axis, bit):
    return lax.ppermute(array, axis, [(i, i ^ bit) for i in range(lax.axis_size(axis))])


def shifted(array, axis, step):
    count = lax.axis_size(axis)
    return lax.ppermute(array, axis, [(i, (i + step) % count) for i in range(count)])


def bits_of(axis):
    return [1 << b for b in range(lax.axis_size(axis).bit_length() - 1)]


def act_norm(before):
    active = jax.nn.gelu(before)
    return active * lax.rsqrt(jnp.mean(active * active, axis=-1, keepdims=True) + 1e-06)


def dot(left, right):
    return jnp.dot(left, right, preferred_element_type=f32)


def dot_rows(left, right):
    return lax.dot_general(left, right, (((0,), (0,)), ((), ())), preferred_element_type=f32)


def dot_columns(left, right):
    return lax.dot_general(left, right, (((1,), (1,)), ((), ())), preferred_element_type=f32)


def table_kernel(base_ref, codes_ref, table_ref, *, groups, fan):
    batch_rows = BATCH // fan
    base = base_ref[0]
    lane = lax.broadcasted_iota(jnp.int32, (1, BATCH), 1)
    row_id = lax.broadcasted_iota(jnp.int32, (groups * batch_rows, BATCH), 0).astype(bf16)
    lane_id = lax.broadcasted_iota(jnp.int32, (LANES, BATCH), 0).astype(bf16)
    one, zero = jnp.ones((), bf16), jnp.zeros((), bf16)

    def step(batch, carry):
        code = codes_ref[pl.ds(batch, 1), :] - base
        inside = (code >= 0) & (code < groups * LANES)
        key = jnp.where(inside, (code // LANES) * batch_rows + lane // fan, -1).astype(bf16)
        low = (code & (LANES - 1)).astype(bf16)
        left = jnp.where(key == row_id, one, zero)
        right = jnp.where(low == lane_id, one, zero)
        counts = dot_columns(left, right).astype(bf16)
        at = pl.ds(pl.multiple_of(batch * batch_rows, batch_rows), batch_rows)
        for group in range(groups):
            table_ref[at, group * LANES : (group + 1) * LANES] = counts[
                group * batch_rows : (group + 1) * batch_rows
            ]
        return carry

    lax.fori_loop(0, codes_ref.shape[0], step, 0, unroll=32)


def build_table(codes, base, rows, slots, fan):
    return pl.pallas_call(
        functools.partial(table_kernel, groups=slots // LANES, fan=fan),
        out_shape=jax.ShapeDtypeStruct((rows, slots), bf16),
        in_specs=[
            pl.BlockSpec(memory_space=pltpu.SMEM),
            pl.BlockSpec(memory_space=pltpu.VMEM),
        ],
        out_specs=pl.BlockSpec(memory_space=pltpu.VMEM),
        compiler_params=pltpu.CompilerParams(vmem_limit_bytes=VMEM_LIMIT),
        name="count_table",
    )(base, codes)


def gather_kernel(table_ref, before_ref, own_ref, after_ref, mine_ref, kept_ref, sent_ref):
    rows = own_ref.shape[0]
    for block in range(table_ref.shape[0] // rows):
        at = slice(block * rows, (block + 1) * rows)
        total = dot(table_ref[at, :rows], before_ref[...])
        total += dot(table_ref[at, rows : 2 * rows], own_ref[...])
        total += dot(table_ref[at, 2 * rows :], after_ref[...])
        if block == 0:
            mine_ref[...] = total
        elif block % 2 == 0:
            place = block // 2 - 1
            kept_ref[place * rows : (place + 1) * rows] = total
        else:
            place = block // 2
            sent_ref[place * rows : (place + 1) * rows] = total.astype(bf16)


def gather_products(table, before, own, after):
    rows, width = own.shape
    members = table.shape[0] // rows
    vmem = pl.BlockSpec(memory_space=pltpu.VMEM)
    return pl.pallas_call(
        gather_kernel,
        out_shape=(
            jax.ShapeDtypeStruct((rows, width), f32),
            jax.ShapeDtypeStruct(((members // 2 - 1) * rows, width), f32),
            jax.ShapeDtypeStruct((members // 2 * rows, width), bf16),
        ),
        in_specs=[vmem] * 4,
        out_specs=(vmem,) * 3,
        compiler_params=pltpu.CompilerParams(vmem_limit_bytes=VMEM_LIMIT),
        name="neighbour_sums",
    )(table, before, own, after)


def spread_kernel(table_ref, *refs):
    *grads, to_before, own, to_after = refs
    rows = own.shape[0]
    for place, out in enumerate((to_before, own, to_after)):
        total = None
        for block, grad in enumerate(grads):
            part = dot_rows(
                table_ref[block * rows : (block + 1) * rows, place * rows : (place + 1) * rows],
                grad[...],
            )
            total = part if total is None else total + part
        out[...] = total.astype(out.dtype)


def spread_products(table, grads):
    rows, width = grads[0].shape
    vmem = pl.BlockSpec(memory_space=pltpu.VMEM)
    return pl.pallas_call(
        spread_kernel,
        out_shape=tuple(jax.ShapeDtypeStruct((rows, width), kind) for kind in (bf16, f32, bf16)),
        in_specs=[vmem] * (1 + len(grads)),
        out_specs=(vmem,) * 3,
        compiler_params=pltpu.CompilerParams(vmem_limit_bytes=VMEM_LIMIT),
        name="neighbour_grads",
    )(table, *grads)


def neighbour_sums(table, own):
    rows = own.shape[0]
    before = shifted(own, "nodes", 1)
    after = shifted(own, "nodes", -1)
    mine, kept, sent = gather_products(table, before, own, after)
    for bit in bits_of("rep"):
        received = swap(sent, "rep", bit).astype(f32)
        mine = mine + received[:rows]
        rest = kept + received[rows:]
        left = rest.shape[0] // rows
        if left == 0:
            break
        blocks = [rest[i * rows : (i + 1) * rows] for i in range(left)]
        sent = jnp.concatenate(blocks[0::2], axis=0).astype(bf16)
        kept = jnp.concatenate(blocks[1::2], axis=0) if left > 1 else rest[:0]
    return mine


def neighbour_grads(table, low_grad):
    grads = [low_grad]
    for bit in reversed(bits_of("rep")):
        held = jnp.concatenate(grads, axis=0) if len(grads) > 1 else grads[0]
        received = swap(held, "rep", bit)
        rows = low_grad.shape[0]
        new = [received[i * rows : (i + 1) * rows] for i in range(len(grads))]
        grads = [block for pair in zip(grads, new) for block in pair]
    to_before, own, to_after = spread_products(table, grads)
    from_after = shifted(to_before, "nodes", -1)
    from_before = shifted(to_after, "nodes", 1)
    return own + from_after.astype(f32) + from_before.astype(f32)


def halves(array):
    half = array.shape[1] // 2
    return array[:, :half], array[:, half:]


def adamw(weight, first, second, grad, scale):
    scaled = grad * scale
    drift = beta_one * first + (1.0 - beta_one) * scaled
    spread = beta_two * second + (1.0 - beta_two) * scaled * scaled
    corrected = drift / (1.0 - beta_one**STEP)
    denominator = jnp.sqrt(spread / (1.0 - beta_two**STEP)) + epsilon
    return (weight - rate * (corrected / denominator + decay * weight), drift, spread)


def packed(encoder, layers, head, biases):
    lead = encoder.shape[:-2]
    width = encoder.shape[-1]
    rows, classes = head.shape[-2:]
    flat_layers = layers.reshape(lead + (layers.shape[-3] * layers.shape[-2], width))
    head = jnp.pad(head, [(0, 0)] * len(lead) + [(0, 0), (0, PAD_AT - classes)])
    bias = jnp.pad(
        biases,
        [(0, 0)] * len(lead) + [(0, rows - biases.shape[-2]), (0, LANES - PAD_AT - biases.shape[-1])],
    )
    tail = jnp.concatenate([head, bias], axis=-1)
    tail = jnp.concatenate([tail[..., : rows // 2, :], tail[..., rows // 2 :, :]], axis=-1)
    return jnp.concatenate([encoder, flat_layers, tail], axis=-2)


def unpacked(rows, encoder_rows, layer_rows, classes, bias_columns):
    lead = rows.shape[:-2]
    width = rows.shape[-1]
    encoder = rows[..., :encoder_rows, :]
    ends = encoder_rows + LAYERS * layer_rows
    layers = rows[..., encoder_rows:ends, :].reshape(lead + (LAYERS, layer_rows, width))
    tail = rows[..., ends:, :]
    tail = jnp.concatenate([tail[..., :LANES], tail[..., LANES:]], axis=-2)
    head = tail[..., :classes]
    biases = tail[..., : LAYERS + 1, PAD_AT : PAD_AT + bias_columns]
    return encoder, layers, head, biases


def per_device(
    features,
    node_count,
    neighbours,
    neighbour_count,
    label_mask,
    labels,
    encoder_weight,
    layer_weights,
    head_weight,
    biases,
    class_bias,
    mean_encoder,
    mean_layers,
    mean_head,
    mean_biases,
    mean_class,
    square_encoder,
    square_layers,
    square_head,
    square_biases,
    square_class,
):
    node_rows = features.shape[0]
    fan = neighbours.shape[1]
    width = encoder_weight.shape[1]
    classes = class_bias.shape[0]
    groups = lax.axis_size("nodes")
    copies = lax.axis_size("rep")
    here_node = lax.axis_index("nodes")
    member = lax.axis_index("rep")
    encoder_rows, layer_rows, bias_columns = (
        encoder_weight.shape[0],
        layer_weights.shape[1],
        biases.shape[1],
    )

    own_weights = packed(
        encoder_weight.astype(bf16), layer_weights.astype(bf16), head_weight.astype(bf16), biases.astype(bf16)
    )
    all_weights = lax.all_gather(own_weights, "nodes", axis=0)

    owner = jnp.floor_divide(neighbours, node_rows)
    offset = jnp.mod(jnp.floor_divide(owner, copies) - here_node + 1, groups)
    codes = (
        jnp.mod(owner, copies) * (3 * node_rows)
        + offset * node_rows
        + jnp.mod(neighbours, node_rows)
    )
    edge_live = lax.broadcasted_iota(jnp.int32, neighbours.shape, 1) < neighbour_count[:, None]
    codes = jnp.where(edge_live, codes, -1).reshape(node_rows * fan // BATCH, BATCH)
    for bit in bits_of("rep"):
        codes = jnp.concatenate([codes, swap(codes, "rep", bit)], axis=0)
    base = jnp.reshape(member * (3 * node_rows), (1,)).astype(jnp.int32)
    table = build_table(codes, base, copies * node_rows, 3 * node_rows, fan)

    local_rows = lax.broadcasted_iota(jnp.int32, (node_rows,), 0)
    valid_node = (local_rows < node_count[0]).astype(f32)[:, None]
    inverse_count = (1.0 / neighbour_count.astype(f32))[:, None]
    weight_mask = label_mask.astype(f32)[:, None] * valid_node

    feature_mean = (neighbour_sums(table, features) * inverse_count).astype(bf16)

    encoder, layers, head, bias_parts = unpacked(
        all_weights, encoder_rows, layer_rows, classes, bias_columns
    )
    encoder = encoder.reshape(groups * encoder_rows, width)
    layers = jnp.swapaxes(layers, 0, 1).reshape(LAYERS, groups * layer_rows, width)
    head = head.reshape(width, classes)
    bias_rows = jnp.swapaxes(bias_parts, 0, 1).reshape(LAYERS + 1, width).astype(f32)

    rounded = ((dot(features, encoder) + bias_rows[0]) * valid_node).astype(bf16)
    averaged = (dot(feature_mean, encoder) + bias_rows[0]).astype(bf16)
    kept_joined = []
    kept_before = []
    for layer in range(LAYERS):
        if layer > 0:
            parts = [neighbour_sums(table, part) for part in halves(rounded)]
            averaged = (jnp.concatenate(parts, axis=1) * inverse_count).astype(bf16)
        joined = jnp.concatenate([rounded, averaged], axis=1)
        before = dot(joined, layers[layer]) + bias_rows[layer + 1]
        kept_joined.append(joined)
        kept_before.append(before)
        rounded = act_norm(before).astype(bf16)

    logits = dot(rounded, head) + class_bias
    total_exp = jax.nn.logsumexp(logits, axis=1, keepdims=True)
    class_ids = lax.broadcasted_iota(jnp.int32, logits.shape, 1)
    target = (class_ids == labels[:, None]).astype(f32)
    picked = jnp.sum(logits * target, axis=1, keepdims=True)
    loss_local = jnp.sum(weight_mask * (total_exp - picked))
    count_local = jnp.sum(weight_mask)
    grad_logits = (jnp.exp(logits - total_exp) - target) * weight_mask
    grad_class_local = jnp.sum(grad_logits, axis=0)
    low_logits = grad_logits.astype(bf16)
    grad_head = dot_rows(rounded, low_logits)
    grad_hidden = dot_columns(low_logits, head)

    grad_weights = [None] * LAYERS
    grad_bias_rows = [None] * (LAYERS + 1)
    for layer in reversed(range(LAYERS)):
        _, pullback = jax.vjp(act_norm, kept_before[layer])
        grad_before = pullback(grad_hidden)[0]
        grad_bias_rows[layer + 1] = jnp.sum(grad_before, axis=0)
        low_grad = grad_before.astype(bf16)
        grad_weights[layer] = dot_rows(kept_joined[layer], low_grad)
        grad_joined = dot_columns(low_grad, layers[layer])
        grad_self, grad_mean = halves(grad_joined)
        if layer > 0:
            low_grad_sum = (grad_mean * inverse_count).astype(bf16)
            parts = [neighbour_grads(table, part) for part in halves(low_grad_sum)]
            grad_hidden = grad_self + jnp.concatenate(parts, axis=1)
    grad_self = grad_self * valid_node
    grad_bias_rows[0] = jnp.sum(grad_self + grad_mean, axis=0)
    grad_encoder = dot_rows(
        jnp.concatenate([features, feature_mean], axis=0),
        jnp.concatenate([grad_self, grad_mean], axis=0).astype(bf16),
    )

    grads = packed(
        grad_encoder.reshape(groups, encoder_rows, width),
        jnp.swapaxes(jnp.stack(grad_weights).reshape(LAYERS, groups, layer_rows, width), 0, 1),
        grad_head.reshape(groups, width // groups, classes),
        jnp.swapaxes(jnp.stack(grad_bias_rows).reshape(LAYERS + 1, groups, bias_columns), 0, 1),
    )
    splits = []
    for index, bit in enumerate(bits_of("rep")):
        dim = 2 if index == 0 else 1
        half = grads.shape[dim] // 2
        low_part = lax.slice_in_dim(grads, 0, half, axis=dim)
        high_part = lax.slice_in_dim(grads, half, 2 * half, axis=dim)
        high = (member & bit) != 0
        away = jnp.where(high, low_part, high_part).astype(bf16)
        grads = jnp.where(high, high_part, low_part) + swap(away, "rep", bit).astype(f32)
        splits.append((bit, dim, high))
    for bit in reversed(bits_of("nodes")):
        half = grads.shape[0] // 2
        high = (here_node & bit) != 0
        away = jnp.where(high, grads[:half], grads[half:]).astype(bf16)
        grads = jnp.where(high, grads[half:], grads[:half]) + swap(away, "nodes", bit).astype(f32)

    squares = jnp.sum(grads * grads)
    row = jnp.concatenate(
        [grad_class_local, loss_local[None], count_local[None], squares[None]]
    )
    tile = jnp.pad(row[None, :], ((0, 7), (0, LANES - row.shape[0])))
    for bit in bits_of("nodes"):
        tile = tile + swap(tile, "nodes", bit)
    for bit in bits_of("rep"):
        tile = tile + swap(tile, "rep", bit)
    grad_class = tile[0, :classes]
    loss_sum = tile[0, classes]
    label_total = tile[0, classes + 1]
    grad_norm = jnp.sqrt(tile[0, classes + 2] + jnp.sum(grad_class * grad_class))
    for bit, dim, high in reversed(splits):
        other = swap(grads, "rep", bit)
        grads = jnp.concatenate(
            [jnp.where(high, other, grads), jnp.where(high, grads, other)], axis=dim
        )

    scale = jnp.minimum(1.0, 1.0 / (grad_norm + 1e-06))
    params = (encoder_weight, layer_weights, head_weight, biases, class_bias)
    firsts = (mean_encoder, mean_layers, mean_head, mean_biases, mean_class)
    seconds = (square_encoder, square_layers, square_head, square_biases, square_class)
    shards = unpacked(grads[0], encoder_rows, layer_rows, classes, bias_columns) + (grad_class,)
    results = [
        adamw(params[index], firsts[index], seconds[index], shards[index], scale)
        for index in range(5)
    ]
    updated = tuple(entry[0] for entry in results)
    drifts = tuple(entry[1] for entry in results)
    spreads = tuple(entry[2] for entry in results)
    copied = tuple(updated[index].astype(bf16) for index in range(4))
    return updated + drifts + spreads + copied + (loss_sum, label_total, grad_norm)


def solution(mesh):
    node_arrays = (
        P(("nodes", "rep"), None),
        P(("nodes", "rep")),
        P(("nodes", "rep"), None),
        P(("nodes", "rep")),
        P(("nodes", "rep")),
        P(("nodes", "rep")),
    )
    weights = (P("nodes", None), P(None, "nodes", None), P("nodes", None), P(None, "nodes"), P())
    return jax.shard_map(
        per_device,
        mesh=mesh,
        in_specs=node_arrays + weights * 3,
        out_specs=weights * 3 + weights[:4] + (P(), P(), P()),
        check_vma=False,
    )
```

```python
import functools

import jax
import jax.numpy as jnp
from jax import lax
from jax.experimental import pallas as pl
from jax.experimental.pallas import tpu as pltpu
from jax.sharding import PartitionSpec as P

LAYERS = 3
STEP = 5

beta_one = 0.5
beta_two = 0.5
rate = 0.05
decay = 0.01
epsilon = 1e-08

LANES = 128
LANE_BITS = 7
BATCH = 256
PAD_AT = 64
VMEM_LIMIT = 14 << 20
COST = 1

bf16 = jnp.bfloat16
f32 = jnp.float32
VMEM = pl.BlockSpec(memory_space=pltpu.VMEM)


def swap(array, axis, mask):
    return lax.ppermute(array, axis, [(i, i ^ mask) for i in range(lax.axis_size(axis))])


def swap_both(array, node_mask, rep_mask):
    copies = lax.axis_size("rep")
    count = lax.axis_size("nodes") * copies
    mask = node_mask * copies + rep_mask
    return lax.ppermute(array, ("nodes", "rep"), [(i, i ^ mask) for i in range(count)])


def shifted(array, axis, step):
    count = lax.axis_size(axis)
    return lax.ppermute(array, axis, [(i, (i + step) % count) for i in range(count)])


def bits_of(axis):
    return [1 << b for b in range(lax.axis_size(axis).bit_length() - 1)]


def masks_of(bits):
    masks = [0]
    for bit in bits:
        masks = masks + [mask | bit for mask in masks]
    return masks


def paired(bits):
    return [bits[at : at + 2] for at in range(0, len(bits), 2)]


def act_norm(before):
    active = jax.nn.gelu(before)
    return active * lax.rsqrt(jnp.mean(active * active, axis=-1, keepdims=True) + 1e-06)


def dot(left, right):
    return jnp.dot(left, right, preferred_element_type=f32)


def dot_rows(left, right):
    return lax.dot_general(left, right, (((0,), (0,)), ((), ())), preferred_element_type=f32)


def dot_columns(left, right):
    return lax.dot_general(left, right, (((1,), (1,)), ((), ())), preferred_element_type=f32)


def split_codes(codes):
    parts = jnp.concatenate([codes >> LANE_BITS, codes & (LANES - 1)], axis=0).astype(bf16)
    return jnp.concatenate([parts[:, :LANES], parts[:, LANES:]], axis=0)


def table_kernel(codes_ref, table_ref, keys, lows, *, fan, slot_bits, member_bits, by_rows):
    batch_rows = BATCH // fan
    batches = keys.shape[0]
    groups = table_ref.shape[1] // LANES
    mine = lax.axis_index("rep")
    row_id = lax.broadcasted_iota(jnp.int32, (groups * batch_rows, BATCH), 0).astype(bf16)
    lane_id = lax.broadcasted_iota(jnp.int32, (LANES, BATCH), 0).astype(bf16)
    one, zero = jnp.ones((), bf16), jnp.zeros((), bf16)
    group_bits = slot_bits - LANE_BITS
    for half in range(2):
        columns = slice(half * LANES, (half + 1) * LANES)
        start = half * 2 * batches
        upper = codes_ref[start : start + batches].astype(f32).astype(jnp.int32)
        if by_rows is not None:
            inside = (upper >> (member_bits + group_bits)) == by_rows
            group = (upper & ((1 << (member_bits + group_bits)) - 1)) ^ (mine << group_bits)
        else:
            inside = ((upper >> group_bits) & ((1 << member_bits) - 1)) == mine
            group = ((upper >> (member_bits + group_bits)) << group_bits) | (upper & ((1 << group_bits) - 1))
        row = (lax.broadcasted_iota(jnp.int32, upper.shape, 1) + half * LANES) // fan
        keys[:, columns] = jnp.where(inside & (upper >= 0), group * batch_rows + row, -1).astype(f32)
        lows[:, columns] = codes_ref[start + batches : start + 2 * batches].astype(f32)

    def step(batch, carry):
        left = jnp.where(keys[pl.ds(batch, 1), :].astype(bf16) == row_id, one, zero)
        right = jnp.where(lows[pl.ds(batch, 1), :].astype(bf16) == lane_id, one, zero)
        counts = dot_columns(left, right).astype(bf16)
        at = pl.ds(pl.multiple_of(batch * batch_rows, batch_rows), batch_rows)
        for group in range(groups):
            table_ref[at, group * LANES : (group + 1) * LANES] = counts[
                group * batch_rows : (group + 1) * batch_rows
            ]
        return carry

    lax.fori_loop(0, batches, step, 0, unroll=min(32, batches))


def build_table(codes, by_rows, slots, members, fan):
    batches = codes.shape[0] // 4
    columns = (3 if by_rows is None else members) * slots
    return kernel_call(
        functools.partial(
            table_kernel,
            fan=fan,
            slot_bits=slots.bit_length() - 1,
            member_bits=members.bit_length() - 1,
            by_rows=by_rows,
        ),
        "column_table" if by_rows is None else "row_table",
        jax.ShapeDtypeStruct((batches * (BATCH // fan), columns), bf16),
        (codes,),
        (pltpu.VMEM((batches, BATCH), f32), pltpu.VMEM((batches, BATCH), f32)),
    )


def blocks_of(tables, rows):
    return [
        table.at[place * rows : (place + 1) * rows]
        for table in tables
        for place in range(table.shape[0] // rows)
    ]


def first_sums_kernel(*refs):
    *tables, before_ref, own_ref, after_ref, mine_ref, kept_ref, sent_ref = refs
    rows = own_ref.shape[0]
    for block, table in enumerate(blocks_of(tables, rows)):
        total = dot(table[:, :rows], before_ref[...])
        total += dot(table[:, rows : 2 * rows], own_ref[...])
        total += dot(table[:, 2 * rows :], after_ref[...])
        if block == 0:
            mine_ref[...] = total
        elif block % 2 == 0:
            kept_ref[(block // 2 - 1) * rows : block // 2 * rows] = total
        else:
            sent_ref[block // 2 * rows : (block // 2 + 1) * rows] = total.astype(bf16)


def sums_kernel(*refs, count):
    tables, parts, outs = refs[:count], refs[count:-count], refs[-count:]
    rows = parts[0].shape[0]
    for table, out in zip(tables, outs):
        total = None
        for place, part in enumerate(parts):
            one = dot(table[:, place * rows : (place + 1) * rows], part[...])
            total = one if total is None else total + one
        out[...] = total.astype(out.dtype)


def grads_kernel(*refs, count):
    tables, grads, outs = refs[:count], refs[count:-3], refs[-3:]
    rows = grads[0].shape[0]
    blocks = blocks_of(tables, rows)
    for place, out in enumerate(outs):
        total = None
        for block, grad in zip(blocks, grads):
            one = dot_rows(block[:, place * rows : (place + 1) * rows], grad[...])
            total = one if total is None else total + one
        out[...] = total.astype(out.dtype)


def table_call(body, name, tables, operands, out_shape):
    return pl.pallas_call(
        body,
        out_shape=out_shape,
        in_specs=[VMEM] * (len(tables) + len(operands)),
        out_specs=(VMEM,) * len(out_shape),
        compiler_params=pltpu.CompilerParams(vmem_limit_bytes=VMEM_LIMIT),
        cost_estimate=pl.CostEstimate(flops=COST, bytes_accessed=COST, transcendentals=0),
        name=name,
    )(*tables, *operands)


def first_sums(tables, around, later):
    rows, width = around[1].shape
    bits = bits_of("rep")
    members = 1 << len(bits)
    mine, kept, sent = table_call(
        first_sums_kernel,
        "first_sums",
        tables,
        around,
        (
            jax.ShapeDtypeStruct((rows, width), f32),
            jax.ShapeDtypeStruct(((members // 2 - 1) * rows, width), f32),
            jax.ShapeDtypeStruct((members // 2 * rows, width), bf16),
        ),
    )
    terms = []
    for bit in bits[:-1]:
        received = swap(sent, "rep", bit)
        terms.append(received[:rows])
        left = kept.shape[0] // rows
        rest = [
            kept[i * rows : (i + 1) * rows] + received[(i + 1) * rows : (i + 2) * rows].astype(f32)
            for i in range(left)
        ]
        sent = jnp.concatenate(rest[0::2], axis=0).astype(bf16)
        kept = jnp.concatenate(rest[1::2], axis=0) if left > 1 else kept[:0]
    work, *given = later
    sent, *given = tied(sent, *given)
    last, *given = tied(swap(sent, "rep", bits[-1]), *work(*given))
    return sum([term.astype(f32) for term in terms + [last]], mine), given


def over_group(own):
    blocks = [own]
    for bit in reversed(bits_of("rep")):
        blocks = [part for block in blocks for part in (block, swap(block, "rep", bit))]
    return blocks


def exchanged(kernel, name, tables, parts):
    everywhere = [over_group(part) for part in parts]
    totals = []
    for blocks in everywhere:
        shapes = tuple(jax.ShapeDtypeStruct(blocks[0].shape, kind) for kind in (bf16, f32, bf16))
        to_before, own, to_after = table_call(
            functools.partial(kernel, count=len(tables)), name, tables, blocks, shapes
        )
        totals.append((own, shifted(to_before, "nodes", -1), shifted(to_after, "nodes", 1)))
    return [own + one.astype(f32) + other.astype(f32) for own, one, other in totals]


def tied(*arrays):
    return lax.optimization_barrier(arrays)


def halves(array):
    half = array.shape[1] // 2
    return array[:, :half], array[:, half:]


def kernel_call(body, name, out_shape, operands, scratch=(), given=VMEM):
    many = isinstance(out_shape, tuple)
    return pl.pallas_call(
        body,
        out_shape=out_shape,
        in_specs=[given] * len(operands),
        out_specs=(VMEM,) * len(out_shape) if many else VMEM,
        scratch_shapes=list(scratch),
        compiler_params=pltpu.CompilerParams(vmem_limit_bytes=VMEM_LIMIT),
        name=name,
    )(*operands)


def pack_kernel(*refs):
    given, (first, later, tail), held, done = refs[:4], refs[4:7], refs[7:11], refs[11]
    copies = [pltpu.make_async_copy(given[at], held[at], done.at[at]) for at in range(4)]
    for copy in copies:
        copy.start()
    for copy in copies:
        copy.wait()
    encoder, layers, head, biases = held
    encoder_rows, layer_rows, rows = encoder.shape[0], layers.shape[1], head.shape[0]
    tail[...] = jnp.zeros_like(tail)
    tail[:, : head.shape[1]] = head[...]
    tail[: biases.shape[0], PAD_AT : PAD_AT + biases.shape[1]] = biases[...]
    for odd in range(2):

        @pl.when((lax.axis_index("rep") & 1) == odd)
        def _(columns=slice(odd * LANES, (odd + 1) * LANES), half=slice(odd * rows // 2, (odd + 1) * rows // 2)):
            first[:encoder_rows] = encoder[:, columns].astype(bf16)
            first[encoder_rows : encoder_rows + layer_rows] = layers[0, :, columns].astype(bf16)
            first[encoder_rows + layer_rows :] = tail[half].astype(bf16)
            for layer in range(1, LAYERS):
                at = slice((layer - 1) * layer_rows, layer * layer_rows)
                later[at] = layers[layer, :, columns].astype(bf16)


def assemble_kernel(mine, theirs, *outs, sizes, order):
    for odd in range(2):

        @pl.when((lax.axis_index("rep") & 1) == odd)
        def _(low=(mine, theirs)[odd], high=(theirs, mine)[odd]):
            bias_total = None
            for shard in range(mine.shape[0]):
                node = lax.axis_index("nodes") ^ order[shard]
                start = 0
                for out, rows in zip(outs, sizes):
                    at = pl.ds(pl.multiple_of(node * rows, rows), rows)
                    part = slice(start, start + rows)
                    out[at, :LANES] = low[shard, part]
                    out[at, LANES:] = high[shard, part]
                    start += rows
                if len(outs) == len(sizes):
                    continue
                head, bias_rows = outs[len(sizes) :]
                rows = head.shape[0] // mine.shape[0]
                half = rows // 2
                at = pl.multiple_of(node * rows, rows)
                head[pl.ds(at, half)] = low[shard, start:]
                head[pl.ds(pl.multiple_of(at + half, half), half)] = high[shard, start:]
                columns = bias_rows.shape[1] // mine.shape[0]
                bias = low[shard, start:].astype(f32)
                if half < 8:
                    bias = jnp.concatenate([bias, high[shard, start:].astype(f32)], axis=0)
                bias = bias[: bias_rows.shape[0]]
                lane = lax.broadcasted_iota(jnp.int32, bias.shape, 1)
                bias = jnp.where((lane >= PAD_AT) & (lane < PAD_AT + columns), bias, 0.0)
                wide = jnp.concatenate([bias, jnp.zeros_like(bias)], axis=1)
                wide = pltpu.roll(wide, (node * columns + bias_rows.shape[1] - PAD_AT) % bias_rows.shape[1], 1)
                bias_total = wide if bias_total is None else bias_total + wide
            if bias_total is not None:
                outs[-1][...] = bias_total


def gradient_kernel(
    rounded, averaged, low_grad, features, means, low_self, low_mean, *refs, groups
):
    *others, head, away, kept, encoder_grad, layer_grad = refs
    width = low_grad.shape[1]
    encoder_grad[...] = dot_rows(features[...], low_self[...]) + dot_rows(means[...], low_mean[...])
    layer_grad[:width] = dot_rows(rounded[...], low_grad[...])
    layer_grad[width:] = dot_rows(averaged[...], low_grad[...])
    sources = [encoder_grad, layer_grad] + list(others)
    for odd in range(2):

        @pl.when((lax.axis_index("rep") & 1) == odd)
        def _(odd=odd):
            mine = slice(odd * LANES, (odd + 1) * LANES)
            other = slice((1 - odd) * LANES, (2 - odd) * LANES)
            for node in range(groups):
                start = 0
                for source in sources:
                    rows = source.shape[0] // groups
                    at, put = slice(node * rows, (node + 1) * rows), slice(start, start + rows)
                    kept[node, put] = source[at, mine]
                    away[node, put] = source[at, other].astype(bf16)
                    start += rows
                half = head.shape[0] // groups // 2
                low, high = (2 * node + odd) * half, (2 * node + 1 - odd) * half
                kept[node, start:] = head[low : low + half]
                away[node, start:] = head[high : high + half].astype(bf16)


def total_at(parts, *index):
    sums = [part[index].astype(f32) for part in parts]
    while len(sums) > 1:
        sums = [one + other for one, other in zip(sums[0::2], sums[1::2])]
    return sums[0]


def first_cut_kernel(kept, received, own, *sent):
    half = own.shape[1]
    for place in range(own.shape[0]):
        for mask, out in enumerate((own, *sent)):
            node = 2 * place + ((lax.axis_index("nodes") & 1) ^ (mask & 1))
            rows = ((lax.axis_index("rep") >> 1) & 1) ^ (mask >> 1)
            rows = pl.ds(pl.multiple_of(rows * half, half), half)
            out[place] = total_at((kept, received), node, rows).astype(out.dtype)


def cut_kernel(*refs, count, bit, ways):
    parts, outs = refs[:count], refs[count:]
    mine = lax.axis_index("nodes") // bit & (ways - 1)
    for place in range(outs[0].shape[0]):
        for mask, out in enumerate(outs):
            out[place] = total_at(parts, ways * place + (mine ^ mask)).astype(out.dtype)


def last_kernel(own, *refs):
    *received, class_row, out = refs[: -(LAYERS + 2)] + refs[-2:]
    bias_rows = refs[-(LAYERS + 3) : -2]
    rows = own.shape[1]
    grad = total_at((own, *received), 0)
    out[:rows] = grad
    out[rows : rows + 8] = jnp.sum((grad * grad).reshape(rows // 8, 8, LANES), axis=0)
    out[rows + 8 : rows + 16] = jnp.broadcast_to(class_row[...], (8, LANES))
    out[rows + 16 :] = jnp.concatenate(
        [row[:, side * LANES : (side + 1) * LANES] for side in range(2) for row in bias_rows], axis=0
    )


def update_kernel(*refs):
    (mine_ref, theirs), rest = refs[:2], refs[2:]
    params, firsts, seconds = rest[:5], rest[5:10], rest[10:15]
    updated, drifts, spreads, copied, scalars, grad = (
        rest[15:20], rest[20:25], rest[25:30], rest[30:34], rest[34], rest[35],
    )
    quarter = (mine_ref.shape[0] - 24) // 2
    tile = mine_ref[2 * quarter :] + theirs[2 * quarter :]
    high, odd = (lax.axis_index("rep") >> 1) & 1, lax.axis_index("rep") & 1
    upper = pl.multiple_of(high * quarter, quarter)
    lower = pl.multiple_of((1 - high) * quarter, quarter)
    mine = pl.ds(pl.multiple_of(odd * LANES, LANES), LANES)
    other = pl.ds(pl.multiple_of((1 - odd) * LANES, LANES), LANES)
    grad[pl.ds(upper, quarter), mine] = mine_ref[:quarter]
    grad[pl.ds(lower, quarter), mine] = mine_ref[quarter : 2 * quarter]
    grad[pl.ds(upper, quarter), other] = theirs[:quarter]
    grad[pl.ds(lower, quarter), other] = theirs[quarter : 2 * quarter]

    classes = params[4].shape[1]
    lane = lax.broadcasted_iota(jnp.int32, (1, LANES), 1)
    class_row = tile[8:9]
    class_grad = jnp.where(lane < classes, class_row, 0.0)
    bias_low, bias_high = tile[16:20], tile[20:24]
    squares = (
        jnp.sum(tile[:8], keepdims=True)
        + jnp.sum(class_grad * class_grad, keepdims=True)
        + jnp.sum(bias_low * bias_low, keepdims=True)
        + jnp.sum(bias_high * bias_high, keepdims=True)
    )
    norm = jnp.sqrt(squares)
    scale = jnp.minimum(1.0, 1.0 / (norm + 1e-06))
    scalars[0:1] = jnp.sum(jnp.where(lane == classes, class_row, 0.0), axis=1, keepdims=True)
    scalars[1:2] = jnp.sum(jnp.where(lane == classes + 1, class_row, 0.0), axis=1, keepdims=True)
    scalars[2:3] = norm

    encoder_rows, layer_rows = params[0].shape[0], params[1].shape[1]
    ends = encoder_rows + LAYERS * layer_rows
    head_half = params[2].shape[0] // 2
    columns = params[3].shape[1]
    width = 2 * LANES
    biases = jnp.concatenate([bias_low, bias_high], axis=1)
    biases = pltpu.roll(biases, (width - lax.axis_index("nodes") * columns) % width, 1)[:, :columns]

    def step(index, at, gradient):
        new, drift, spread = adamw(params[index][at], firsts[index][at], seconds[index][at], gradient, scale)
        updated[index][at] = new
        drifts[index][at] = drift
        spreads[index][at] = spread
        if index < 4:
            copied[index][at] = new.astype(bf16)

    step(0, slice(None), grad[:encoder_rows])
    for layer in range(LAYERS):
        start = encoder_rows + layer * layer_rows
        step(1, layer, grad[start : start + layer_rows])
    step(2, slice(0, head_half), grad[ends:, :LANES][:, :classes])
    step(2, slice(head_half, 2 * head_half), grad[ends:, LANES:][:, :classes])
    step(3, slice(None), biases)
    step(4, slice(None), class_grad[:, :classes])


def adamw(weight, first, second, grad, scale):
    scaled = grad * scale
    drift = beta_one * first + (1.0 - beta_one) * scaled
    spread = beta_two * second + (1.0 - beta_two) * scaled * scaled
    corrected = drift / (1.0 - beta_one**STEP)
    denominator = jnp.sqrt(spread / (1.0 - beta_two**STEP)) + epsilon
    return (weight - rate * (corrected / denominator + decay * weight), drift, spread)


def plain_pack(encoder, layers, head, biases):
    head = jnp.pad(head, ((0, 0), (0, PAD_AT - head.shape[1])))
    bias = jnp.pad(biases, ((0, head.shape[0] - biases.shape[0]), (0, LANES - PAD_AT - biases.shape[1])))
    tail = jnp.concatenate([head, bias], axis=1)
    half = tail.shape[0] // 2
    tail = jnp.concatenate([tail[:half], tail[half:]], axis=1)
    odd = (lax.axis_index("rep") & 1) == 1
    first, later = jnp.concatenate([encoder, layers[0], tail], axis=0), jnp.concatenate(list(layers[1:]), axis=0)
    return [jnp.where(odd, part[:, LANES:], part[:, :LANES]).astype(bf16) for part in (first, later)]


def plain_assemble(mine, theirs, order, sizes):
    places = [0] * len(order)
    for place, node in enumerate(order):
        places[node] = place
    places = jnp.asarray(places)[lax.axis_index("nodes") ^ jnp.arange(len(order))]
    mine, theirs = jnp.take(mine, places, axis=0), jnp.take(theirs, places, axis=0)
    odd = (lax.axis_index("rep") & 1) == 1
    rows = jnp.concatenate([jnp.where(odd, theirs, mine), jnp.where(odd, mine, theirs)], axis=2)
    outs, start = [], 0
    for size in sizes:
        outs.append(rows[:, start : start + size].reshape(-1, rows.shape[2]))
        start += size
    if start < rows.shape[1]:
        tail = rows[:, start:]
        tail = jnp.concatenate([tail[..., :LANES], tail[..., LANES:]], axis=1)
        columns = rows.shape[2] // len(order)
        bias = tail[:, : LAYERS + 1, PAD_AT : PAD_AT + columns].astype(f32)
        outs += [tail.reshape(-1, LANES), jnp.swapaxes(bias, 0, 1).reshape(LAYERS + 1, rows.shape[2])]
    return outs


def plain_gradients(rounded, averaged, low_grad, features, means, low_self, low_mean, *rest, groups):
    *others, head = rest
    encoder = dot_rows(features, low_self) + dot_rows(means, low_mean)
    layer = jnp.concatenate([dot_rows(rounded, low_grad), dot_rows(averaged, low_grad)], axis=0)
    parts = [part.reshape(groups, -1, part.shape[1]) for part in (encoder, layer, *others, head)]
    half = parts[-1].shape[1] // 2
    parts[-1] = jnp.concatenate([parts[-1][:, :half], parts[-1][:, half:]], axis=2)
    rows = jnp.concatenate(parts, axis=1)
    odd = (lax.axis_index("rep") & 1) == 1
    low, high = rows[..., :LANES], rows[..., LANES:]
    return jnp.where(odd, low, high).astype(bf16), jnp.where(odd, high, low)


def plain_first_cut(kept, received):
    total = kept + received.astype(f32)
    half = total.shape[1] // 2
    total = total.reshape(total.shape[0] // 2, 2, 2, half, LANES)
    outs = []
    for mask in range(4):
        node = (lax.axis_index("nodes") & 1) ^ (mask & 1)
        rows = ((lax.axis_index("rep") >> 1) & 1) ^ (mask >> 1)
        part = lax.dynamic_slice(total, (0, node, rows, 0, 0), (total.shape[0], 1, 1, half, LANES))
        outs.append(part.reshape(-1, half, LANES).astype(bf16 if mask else f32))
    return outs


def plain_last(own, *refs):
    received, bias_rows, class_row = refs[: -(LAYERS + 2)], refs[-(LAYERS + 2) : -1], refs[-1]
    grad = total_at((own, *received), 0)
    squares = jnp.pad(jnp.sum(grad * grad, axis=0, keepdims=True), ((0, 7), (0, 0)))
    bias = [row[:, side * LANES : (side + 1) * LANES] for side in range(2) for row in bias_rows]
    return jnp.concatenate([grad, squares, jnp.broadcast_to(class_row, (8, LANES)), *bias], axis=0)


def plain_update(mine, theirs, *rest):
    params, firsts, seconds = rest[:5], rest[5:10], rest[10:15]
    quarter = (mine.shape[0] - 24) // 2
    tile = mine[2 * quarter :] + theirs[2 * quarter :]
    high, odd = (lax.axis_index("rep") >> 1) & 1 == 1, lax.axis_index("rep") & 1 == 1
    sides = []
    for part in (mine, theirs):
        one, other = part[:quarter], part[quarter : 2 * quarter]
        sides.append(jnp.concatenate([jnp.where(high, other, one), jnp.where(high, one, other)], axis=0))
    rows = jnp.concatenate([jnp.where(odd, *sides[::-1]), jnp.where(odd, *sides)], axis=1)
    classes = params[4].shape[1]
    class_grad = tile[8:9, :classes]
    biases = jnp.concatenate([tile[16:20], tile[20:24]], axis=1)
    norm = jnp.sqrt(jnp.sum(tile[:8]) + jnp.sum(class_grad * class_grad) + jnp.sum(biases * biases))
    scale = jnp.minimum(1.0, 1.0 / (norm + 1e-06))
    encoder_rows, layer_rows = params[0].shape[0], params[1].shape[1]
    ends = encoder_rows + LAYERS * layer_rows
    columns = params[3].shape[1]
    grads = (
        rows[:encoder_rows],
        rows[encoder_rows:ends].reshape(LAYERS, layer_rows, -1),
        jnp.concatenate([rows[ends:, :LANES], rows[ends:, LANES:]], axis=0)[:, :classes],
        lax.dynamic_slice_in_dim(biases, lax.axis_index("nodes") * columns, columns, axis=1),
        class_grad,
    )
    results = [adamw(params[at], firsts[at], seconds[at], grads[at], scale) for at in range(5)]
    new = [entry[0] for entry in results]
    scalars = jnp.stack([tile[8, classes], tile[8, classes + 1], norm])[:, None]
    return (
        *new, *[entry[1] for entry in results], *[entry[2] for entry in results],
        *[entry.astype(bf16) for entry in new[:4]], scalars,
    )


def per_device(
    features,
    node_count,
    neighbours,
    neighbour_count,
    label_mask,
    labels,
    encoder_weight,
    layer_weights,
    head_weight,
    biases,
    class_bias,
    mean_encoder,
    mean_layers,
    mean_head,
    mean_biases,
    mean_class,
    square_encoder,
    square_layers,
    square_head,
    square_biases,
    square_class,
):
    node_rows = features.shape[0]
    fan = neighbours.shape[1]
    width = encoder_weight.shape[1]
    classes = class_bias.shape[0]
    groups = lax.axis_size("nodes")
    copies = lax.axis_size("rep")
    here_node = lax.axis_index("nodes")
    member = lax.axis_index("rep")
    encoder_rows, layer_rows, bias_columns = (
        encoder_weight.shape[0],
        layer_weights.shape[1],
        biases.shape[1],
    )

    owner = jnp.floor_divide(neighbours, node_rows)
    offset = jnp.mod(jnp.floor_divide(owner, copies) - here_node + 1, groups)
    codes = (offset * copies + jnp.mod(owner, copies)) * node_rows + jnp.mod(neighbours, node_rows)
    edge_live = lax.broadcasted_iota(jnp.int32, neighbours.shape, 1) < neighbour_count[:, None]
    codes = jnp.where(edge_live, codes, -1).reshape(node_rows * fan // BATCH, BATCH)
    codes = split_codes(codes)
    to_around = jnp.concatenate([features, codes], axis=0)
    around = (shifted(to_around, "nodes", 1), shifted(to_around, "nodes", -1))
    blocks = [codes]
    for bit in bits_of("rep"):
        blocks = blocks + [swap(block, "rep", bit) for block in blocks]
    column_tables = [build_table(block, None, node_rows, copies, fan) for block in blocks]

    head_rows = head_weight.shape[0]
    aligned = encoder_rows % 16 == 0 and layer_rows % 16 == 0 and head_rows % 32 == 0
    first_rows = encoder_rows + layer_rows + head_rows // 2
    weights = (encoder_weight, layer_weights, head_weight, biases)
    own_first, own_later = plain_pack(*weights) if not aligned else kernel_call(
        pack_kernel,
        "pack_weights",
        (
            jax.ShapeDtypeStruct((first_rows, LANES), bf16),
            jax.ShapeDtypeStruct(((LAYERS - 1) * layer_rows, LANES), bf16),
        ),
        weights,
        (
            pltpu.VMEM((head_rows, LANES), f32),
            *[pltpu.VMEM(weight.shape, f32) for weight in weights],
            pltpu.SemaphoreType.DMA((4,)),
        ),
        pl.BlockSpec(memory_space=pltpu.HBM),
    )
    def over_nodes(part, beside):
        part, order = part[None], [0]
        for bit in bits_of("nodes")[::-1]:
            part = jnp.concatenate([part, swap(part, "nodes", bit)], axis=0)
            order = order + [node ^ bit for node in order]
            if beside:
                part, beside[0] = tied(part, beside[0])
                done.append(beside.pop(0))
        return (part, swap(part, "rep", 1)), order

    done = []
    gathered, order = over_nodes(own_first, column_tables)
    column_tables = done + column_tables
    sizes = (encoder_rows, layer_rows)
    encoder, first_layer, head, bias_rows = plain_assemble(*gathered, order, sizes) if not aligned else kernel_call(
        functools.partial(assemble_kernel, sizes=sizes, order=order),
        "first_weights",
        (
            jax.ShapeDtypeStruct((groups * encoder_rows, width), bf16),
            jax.ShapeDtypeStruct((groups * layer_rows, width), bf16),
            jax.ShapeDtypeStruct((groups * head_rows, LANES), bf16),
            jax.ShapeDtypeStruct((min(8, head_rows), width), f32),
        ),
        gathered,
    )
    local_rows = lax.broadcasted_iota(jnp.int32, (node_rows,), 0)
    valid_node = (local_rows < node_count[0]).astype(f32)[:, None]
    inverse_count = (1.0 / neighbour_count.astype(f32))[:, None]
    weight_mask = label_mask.astype(f32)[:, None] * valid_node

    def row_tables_of(*blocks):
        return [build_table(block, place, node_rows, copies, fan) for block, place in zip(blocks, (2, 1, 0))] + [
            blocks[-1]
        ]

    feature_sums, (*row_tables, own_later) = first_sums(
        column_tables,
        (around[0][:node_rows], features, around[1][:node_rows]),
        (row_tables_of, around[0][node_rows:], codes, around[1][node_rows:], own_later),
    )
    gathered, order = over_nodes(own_later, [])
    sizes = (layer_rows,) * (LAYERS - 1)
    layers = [first_layer] + list(
        plain_assemble(*gathered, order, sizes) if not aligned else kernel_call(
            functools.partial(assemble_kernel, sizes=sizes, order=order),
            "later_weights",
            (jax.ShapeDtypeStruct((groups * layer_rows, width), bf16),) * (LAYERS - 1),
            gathered,
            )
    )
    feature_mean = (feature_sums * inverse_count).astype(bf16)

    rounded = ((dot(features, encoder) + bias_rows[0:1]) * valid_node).astype(bf16)
    averaged = (dot(feature_mean, encoder) + bias_rows[0:1]).astype(bf16)
    low_self_input = (rounded, averaged)
    kept_joined = []
    kept_before = []
    for layer in range(LAYERS):
        if layer > 0:
            parts = exchanged(sums_kernel, "neighbour_sums", row_tables, halves(rounded))
            averaged = (jnp.concatenate(parts, axis=1) * inverse_count).astype(bf16)
        joined = jnp.concatenate([rounded, averaged], axis=1)
        before = dot(joined, layers[layer]) + bias_rows[layer + 1 : layer + 2]
        kept_joined.append(joined)
        kept_before.append(before)
        rounded = act_norm(before).astype(bf16)

    class_ids = lax.broadcasted_iota(jnp.int32, (1, LANES), 1)
    padded_bias = jnp.pad(class_bias, (0, LANES - classes))
    logits = jnp.where(class_ids < classes, dot(rounded, head) + padded_bias, -1e30)
    total_exp = jax.nn.logsumexp(logits, axis=1, keepdims=True)
    target = (class_ids == labels[:, None]).astype(f32)
    picked = jnp.sum(logits * target, axis=1, keepdims=True)
    loss_local = jnp.sum(weight_mask * (total_exp - picked))
    count_local = jnp.sum(weight_mask)
    grad_logits = (jnp.exp(logits - total_exp) - target) * weight_mask
    class_tile = jnp.sum(grad_logits, axis=0, keepdims=True)
    class_tile = jnp.where(class_ids == classes, loss_local, class_tile)
    class_tile = jnp.where(class_ids == classes + 1, count_local, class_tile)
    low_logits = grad_logits.astype(bf16)
    grad_head = dot_rows(rounded, low_logits)
    grad_hidden = dot_columns(low_logits, head)

    grad_weights = [None] * LAYERS
    grad_bias_rows = [None] * (LAYERS + 1)
    for layer in reversed(range(LAYERS)):
        _, pullback = jax.vjp(act_norm, kept_before[layer])
        grad_before = pullback(grad_hidden)[0]
        grad_bias_rows[layer + 1] = jnp.sum(grad_before, axis=0, keepdims=True)
        low_grad = grad_before.astype(bf16)
        if layer > 0:
            grad_weights[layer] = dot_rows(kept_joined[layer], low_grad)
        grad_joined = dot_columns(low_grad, layers[layer])
        grad_self, grad_mean = halves(grad_joined)
        if layer > 0:
            low_grad_sum = (grad_mean * inverse_count).astype(bf16)
            parts = exchanged(grads_kernel, "neighbour_grads", column_tables, halves(low_grad_sum))
            grad_hidden = grad_self + jnp.concatenate(parts, axis=1)
    grad_self = grad_self * valid_node
    grad_bias_rows[0] = jnp.sum(grad_self + grad_mean, axis=0, keepdims=True)
    rows = first_rows + (LAYERS - 1) * layer_rows
    inputs = (
        *low_self_input,
        low_grad,
        features,
        feature_mean,
        grad_self.astype(bf16),
        grad_mean.astype(bf16),
        *grad_weights[1:],
        grad_head,
    )
    away, grads = plain_gradients(*inputs, groups=groups) if not aligned else kernel_call(
        functools.partial(gradient_kernel, groups=groups),
        "gradients",
        (
            jax.ShapeDtypeStruct((groups, rows, LANES), bf16),
            jax.ShapeDtypeStruct((groups, rows, LANES), f32),
        ),
        inputs,
        (pltpu.VMEM((features.shape[1], width), f32), pltpu.VMEM((2 * width, width), f32)),
    )

    received = swap(away, "rep", 1)
    half = rows // 2
    own, *sent = plain_first_cut(grads, received) if not aligned else kernel_call(
        first_cut_kernel,
        "first_cut",
        tuple(jax.ShapeDtypeStruct((groups // 2, half, LANES), kind) for kind in (f32, bf16, bf16, bf16)),
        (grads, received),
    )
    received = [swap_both(part, mask & 1, (mask >> 1) * 2) for mask, part in enumerate(sent, 1)]
    for bits in paired(bits_of("nodes")[1:]):
        masks = masks_of(bits)
        parts = (own, *received)
        left = own.shape[0] // len(masks)
        own, *sent = kernel_call(
            functools.partial(cut_kernel, count=len(parts), bit=bits[0], ways=len(masks)),
            "cut",
            tuple(
                jax.ShapeDtypeStruct((left, half, LANES), bf16 if mask else f32) for mask in masks
            ),
            parts,
        )
        received = [swap(part, "nodes", mask) for mask, part in zip(masks[1:], sent)]
    inputs = (own, *received, *grad_bias_rows, class_tile)
    grads = plain_last(*inputs) if not aligned else pl.pallas_call(
        last_kernel,
        out_shape=jax.ShapeDtypeStruct((half + 24, LANES), f32),
        in_specs=[VMEM] * (len(received) + LAYERS + 3),
        out_specs=VMEM,
        compiler_params=pltpu.CompilerParams(vmem_limit_bytes=VMEM_LIMIT),
        name="last_sum",
    )(*inputs)

    tile = grads[half:]
    for bits in paired(bits_of("nodes")[1:]):
        parts = [tile] + [swap(tile, "nodes", mask) for mask in masks_of(bits)[1:]]
        tile = total_at(parts, slice(None))
    across, other, both = (
        swap_both(tile, 1, 0),
        swap(jnp.concatenate([grads[:half], tile], axis=0), "rep", 2),
        swap_both(tile, 1, 2),
    )
    tile = total_at((tile, across, other[half:], both), slice(None))
    grads = jnp.concatenate([grads[:half], other[:half], tile], axis=0)
    received = swap(grads, "rep", 1)

    params = (encoder_weight, layer_weights, head_weight, biases, class_bias[None])
    firsts = (mean_encoder, mean_layers, mean_head, mean_biases, mean_class[None])
    seconds = (square_encoder, square_layers, square_head, square_biases, square_class[None])
    shapes = tuple(jax.ShapeDtypeStruct(param.shape, f32) for param in params)
    lows = tuple(jax.ShapeDtypeStruct(param.shape, bf16) for param in params[:4])
    inputs = (grads, received, *params, *firsts, *seconds)
    results = plain_update(*inputs) if not aligned else pl.pallas_call(
        update_kernel,
        out_shape=shapes * 3 + lows + (jax.ShapeDtypeStruct((3, 1), f32),),
        in_specs=[VMEM] * 17,
        out_specs=(VMEM,) * 20,
        scratch_shapes=[pltpu.VMEM((rows, width), f32)],
        compiler_params=pltpu.CompilerParams(vmem_limit_bytes=VMEM_LIMIT),
        name="adamw",
    )(*inputs)
    results, scalars = list(results[:19]), results[19]
    for index in (4, 9, 14):
        results[index] = results[index][0]
    return tuple(results) + tuple(scalars[index, 0] for index in range(3))


def solution(mesh):
    node_arrays = (
        P(("nodes", "rep"), None),
        P(("nodes", "rep")),
        P(("nodes", "rep"), None),
        P(("nodes", "rep")),
        P(("nodes", "rep")),
        P(("nodes", "rep")),
    )
    weights = (P("nodes", None), P(None, "nodes", None), P("nodes", None), P(None, "nodes"), P())
    return jax.shard_map(
        per_device,
        mesh=mesh,
        in_specs=node_arrays + weights * 3,
        out_specs=weights * 3 + weights[:4] + (P(), P(), P()),
        check_vma=False,
    )
```

```python
import functools

import jax
import jax.numpy as jnp
from jax import lax
from jax.experimental import pallas as pl
from jax.experimental.pallas import tpu as pltpu
from jax.sharding import PartitionSpec as P

LAYERS = 3
STEP = 5

beta_one = 0.5
beta_two = 0.5
rate = 0.05
decay = 0.01
epsilon = 1e-08

LANES = 128
LANE_BITS = 7
BATCH = 256
PAD_AT = 64
VMEM_LIMIT = 14 << 20

bf16 = jnp.bfloat16
f32 = jnp.float32
VMEM = pl.BlockSpec(memory_space=pltpu.VMEM)


def swap(array, axis, mask):
    return lax.ppermute(array, axis, [(i, i ^ mask) for i in range(lax.axis_size(axis))])


def swap_both(array, node_mask, rep_mask):
    copies = lax.axis_size("rep")
    count = lax.axis_size("nodes") * copies
    mask = node_mask * copies + rep_mask
    return lax.ppermute(array, ("nodes", "rep"), [(i, i ^ mask) for i in range(count)])


def other_side(array):
    count = lax.axis_size("nodes")
    return lax.ppermute(array, "nodes", [(i, (i + (1 if i % 2 else -1)) % count) for i in range(count)])


def around_of(array):
    other = other_side(array)
    return swap(array, "nodes", 1), array, other


def bits_of(axis):
    return [1 << b for b in range(lax.axis_size(axis).bit_length() - 1)]


def masks_of(bits):
    masks = [0]
    for bit in bits:
        masks = masks + [mask | bit for mask in masks]
    return masks


def paired(bits):
    return [bits[at : at + 2] for at in range(0, len(bits), 2)]


def act_norm(before):
    active = jax.nn.gelu(before)
    return active * lax.rsqrt(jnp.mean(active * active, axis=-1, keepdims=True) + 1e-06)


def dot(left, right):
    return jnp.dot(left, right, preferred_element_type=f32)


def dot_rows(left, right):
    return lax.dot_general(left, right, (((0,), (0,)), ((), ())), preferred_element_type=f32)


def dot_columns(left, right):
    return lax.dot_general(left, right, (((1,), (1,)), ((), ())), preferred_element_type=f32)


def split_codes(codes):
    parts = jnp.concatenate([codes >> LANE_BITS, codes & (LANES - 1)], axis=0).astype(bf16)
    return jnp.concatenate([parts[:, :LANES], parts[:, LANES:]], axis=0)


def table_kernel(codes_ref, table_ref, keys, lows, *, fan, slot_bits, member_bits, by_rows):
    batch_rows = BATCH // fan
    batches = keys.shape[0]
    groups = table_ref.shape[1] // LANES
    mine = lax.axis_index("rep")
    row_id = lax.broadcasted_iota(jnp.int32, (groups * batch_rows, BATCH), 0).astype(bf16)
    lane_id = lax.broadcasted_iota(jnp.int32, (LANES, BATCH), 0).astype(bf16)
    one, zero = jnp.ones((), bf16), jnp.zeros((), bf16)
    group_bits = slot_bits - LANE_BITS
    for half in range(2):
        columns = slice(half * LANES, (half + 1) * LANES)
        start = half * 2 * batches
        upper = codes_ref[start : start + batches].astype(f32).astype(jnp.int32)
        if by_rows is not None:
            inside = (upper >> (member_bits + group_bits)) == by_rows
            group = (upper & ((1 << (member_bits + group_bits)) - 1)) ^ (mine << group_bits)
        else:
            inside = ((upper >> group_bits) & ((1 << member_bits) - 1)) == mine
            group = ((upper >> (member_bits + group_bits)) << group_bits) | (upper & ((1 << group_bits) - 1))
        row = (lax.broadcasted_iota(jnp.int32, upper.shape, 1) + half * LANES) // fan
        keys[:, columns] = jnp.where(inside & (upper >= 0), group * batch_rows + row, -1).astype(f32)
        lows[:, columns] = codes_ref[start + batches : start + 2 * batches].astype(f32)

    def step(batch, carry):
        left = jnp.where(keys[pl.ds(batch, 1), :].astype(bf16) == row_id, one, zero)
        right = jnp.where(lows[pl.ds(batch, 1), :].astype(bf16) == lane_id, one, zero)
        counts = dot_columns(left, right).astype(bf16)
        at = pl.ds(pl.multiple_of(batch * batch_rows, batch_rows), batch_rows)
        for group in range(groups):
            table_ref[at, group * LANES : (group + 1) * LANES] = counts[
                group * batch_rows : (group + 1) * batch_rows
            ]
        return carry

    lax.fori_loop(0, batches, step, 0, unroll=min(16, batches))


def build_table(codes, by_rows, slots, members, fan):
    batches = codes.shape[0] // 4
    columns = (3 if by_rows is None else members) * slots
    return kernel_call(
        functools.partial(
            table_kernel,
            fan=fan,
            slot_bits=slots.bit_length() - 1,
            member_bits=members.bit_length() - 1,
            by_rows=by_rows,
        ),
        "column_table" if by_rows is None else "row_table",
        jax.ShapeDtypeStruct((batches * (BATCH // fan), columns), bf16),
        (codes,),
        (pltpu.VMEM((batches, BATCH), f32), pltpu.VMEM((batches, BATCH), f32)),
    )


def products_kernel(*refs, tables, plan, transposed):
    outs = {entry[0] for entry in plan}
    given, outs = refs[: -len(outs)], refs[-len(outs) :]
    multiply = dot_rows if transposed else dot
    rows = given[-1].shape[0]
    for out, place, terms in plan:
        total = None
        for table, columns, operand in terms:
            one = multiply(given[table][:, columns * rows : (columns + 1) * rows], given[tables + operand][...])
            total = one if total is None else total + one
        outs[out][place * rows : (place + 1) * rows] = total.astype(outs[out].dtype)


def products(name, tables, operands, plan, kinds, transposed):
    rows, width = operands[0].shape
    sizes = [1 + max(place for out, place, _ in plan if out == at) for at in range(len(kinds))]
    outs = kernel_call(
        functools.partial(products_kernel, tables=len(tables), plan=plan, transposed=transposed),
        name,
        tuple(jax.ShapeDtypeStruct((size * rows, width), kind) for size, kind in zip(sizes, kinds)),
        (*tables, *operands),
    )
    return outs if len(kinds) > 1 else outs[0]


def nodes_first_products(column_tables, row_tables, around, members, transposed, after=()):
    sums = []
    for odd, kinds in ((1, (bf16,)), (0, (f32, f32))):
        if not odd and after:
            around = tied(*around, *after)[: len(around)]
        blocks = range(odd, members, 2)
        put = [(0, at) if odd or at == 0 else (1, at - 1) for at in range(len(blocks))]
        if transposed:
            tables = row_tables
            plan = [(*to, [(p, block, p) for p in range(3)]) for to, block in zip(put, blocks)]
        else:
            tables = [column_tables[block] for block in blocks]
            plan = [(*to, [(at, p, p) for p in range(3)]) for at, to in enumerate(put)]
        sums.append(products("nodes_first", tables, around, plan, kinds, transposed))
    return sums[1][0], sums[1][1], sums[0]


def rep_first_products(column_tables, row_tables, blocks, transposed):
    sums = []
    for place, kind in ((2, bf16), (0, bf16), (1, f32)):
        if transposed:
            tables, plan = column_tables, [(0, 0, [(at, place, at) for at in range(len(blocks))])]
        else:
            tables, plan = [row_tables[place]], [(0, 0, [(0, at, at) for at in range(len(blocks))])]
        sums.append(products("rep_first", tables, blocks, plan, (kind,), transposed))
    return sums[1], sums[2], sums[0]


def added_over_group(mine, kept, sent, later=None):
    rows = mine.shape[0]
    bits = bits_of("rep")
    terms = []
    for bit in bits[:-1]:
        received = swap(sent, "rep", bit)
        terms.append(received[:rows])
        left = kept.shape[0] // rows
        rest = [
            kept[i * rows : (i + 1) * rows] + received[(i + 1) * rows : (i + 2) * rows].astype(f32)
            for i in range(left)
        ]
        sent = jnp.concatenate(rest[0::2], axis=0).astype(bf16)
        kept = jnp.concatenate(rest[1::2], axis=0) if left > 1 else kept[:0]
    given = []
    if later is not None:
        work, *given = later
        sent, *given = tied(sent, *given)
        given = work(*given)
    last, *given = tied(swap(sent, "rep", bits[-1]), *given)
    return sum([term.astype(f32) for term in terms + [last]], mine), given


def over_group(own):
    blocks = [own]
    for bit in reversed(bits_of("rep")):
        blocks = [part for block in blocks for part in (block, swap(block, "rep", bit))]
    return blocks


def exchanged(array, column_tables, row_tables, transposed):
    one, other = halves(array)
    blocks = over_group(other)
    partner, own, far = around_of(one)
    to_partner, mine, to_far = rep_first_products(column_tables, row_tables, blocks, transposed)
    from_far, from_partner = other_side(to_far), swap(to_partner, "nodes", 1)
    one = nodes_first_products(column_tables, row_tables, (partner, own, far), len(blocks), transposed)
    one, _ = added_over_group(*one)
    other = mine + from_partner.astype(f32) + from_far.astype(f32)
    return jnp.concatenate([one, other], axis=1)


def tied(*arrays):
    return lax.optimization_barrier(arrays)


def halves(array):
    half = array.shape[1] // 2
    return array[:, :half], array[:, half:]


def kernel_call(body, name, out_shape, operands, scratch=(), given=VMEM):
    many = isinstance(out_shape, tuple)
    return pl.pallas_call(
        body,
        out_shape=out_shape,
        in_specs=[given] * len(operands),
        out_specs=(VMEM,) * len(out_shape) if many else VMEM,
        scratch_shapes=list(scratch),
        compiler_params=pltpu.CompilerParams(vmem_limit_bytes=VMEM_LIMIT),
        name=name,
    )(*operands)


def pack_kernel(*refs):
    given, (packed, tail), held, done = refs[:4], refs[5:7], refs[7:11], refs[11]
    copies = [pltpu.make_async_copy(given[at], held[at], done.at[at]) for at in range(4)]
    for copy in copies:
        copy.start()
    for copy in copies:
        copy.wait()
    encoder, layers, head, biases = held
    encoder_rows, layer_rows, rows = encoder.shape[0], layers.shape[1], head.shape[0]
    tail[...] = jnp.zeros_like(tail)
    tail[:, : head.shape[1]] = head[...]
    tail[: biases.shape[0], PAD_AT : PAD_AT + biases.shape[1]] = biases[...]
    for odd in range(2):

        @pl.when((lax.axis_index("rep") & 1) == odd)
        def _(columns=slice(odd * LANES, (odd + 1) * LANES), half=slice(odd * rows // 2, (odd + 1) * rows // 2)):
            packed[:encoder_rows] = encoder[:, columns].astype(bf16)
            for layer in range(LAYERS):
                start = encoder_rows + layer * layer_rows
                packed[start : start + layer_rows] = layers[layer, :, columns].astype(bf16)
            packed[encoder_rows + LAYERS * layer_rows :] = tail[half].astype(bf16)


def assemble_kernel(mine, theirs, *outs, sizes, order):
    for odd in range(2):

        @pl.when((lax.axis_index("rep") & 1) == odd)
        def _(low=(mine, theirs)[odd], high=(theirs, mine)[odd]):
            bias_total = None
            for shard in range(mine.shape[0]):
                node = lax.axis_index("nodes") ^ order[shard]
                start = 0
                for out, rows in zip(outs, sizes):
                    at = pl.ds(pl.multiple_of(node * rows, rows), rows)
                    part = slice(start, start + rows)
                    out[at, :LANES] = low[shard, part]
                    out[at, LANES:] = high[shard, part]
                    start += rows
                if len(outs) == len(sizes):
                    continue
                head, bias_rows = outs[len(sizes) :]
                rows = head.shape[0] // mine.shape[0]
                half = rows // 2
                at = pl.multiple_of(node * rows, rows)
                head[pl.ds(at, half)] = low[shard, start:]
                head[pl.ds(pl.multiple_of(at + half, half), half)] = high[shard, start:]
                columns = bias_rows.shape[1] // mine.shape[0]
                bias = low[shard, start:].astype(f32)
                if half < 8:
                    bias = jnp.concatenate([bias, high[shard, start:].astype(f32)], axis=0)
                bias = bias[: bias_rows.shape[0]]
                lane = lax.broadcasted_iota(jnp.int32, bias.shape, 1)
                bias = jnp.where((lane >= PAD_AT) & (lane < PAD_AT + columns), bias, 0.0)
                wide = jnp.concatenate([bias, jnp.zeros_like(bias)], axis=1)
                wide = pltpu.roll(wide, (node * columns + bias_rows.shape[1] - PAD_AT) % bias_rows.shape[1], 1)
                bias_total = wide if bias_total is None else bias_total + wide
            if bias_total is not None:
                outs[-1][...] = bias_total


def gradient_kernel(
    rounded, averaged, low_grad, features, means, low_self, low_mean, *refs, groups
):
    *others, head, away, kept, encoder_grad, layer_grad = refs
    width = low_grad.shape[1]
    encoder_grad[...] = dot_rows(features[...], low_self[...]) + dot_rows(means[...], low_mean[...])
    layer_grad[:width] = dot_rows(rounded[...], low_grad[...])
    layer_grad[width:] = dot_rows(averaged[...], low_grad[...])
    sources = [encoder_grad, layer_grad] + list(others)
    for odd in range(2):

        @pl.when((lax.axis_index("rep") & 1) == odd)
        def _(odd=odd):
            mine = slice(odd * LANES, (odd + 1) * LANES)
            other = slice((1 - odd) * LANES, (2 - odd) * LANES)
            for node in range(groups):
                start = 0
                for source in sources:
                    rows = source.shape[0] // groups
                    at, put = slice(node * rows, (node + 1) * rows), slice(start, start + rows)
                    kept[node, put] = source[at, mine]
                    away[node, put] = source[at, other].astype(bf16)
                    start += rows
                half = head.shape[0] // groups // 2
                low, high = (2 * node + odd) * half, (2 * node + 1 - odd) * half
                kept[node, start:] = head[low : low + half]
                away[node, start:] = head[high : high + half].astype(bf16)


def total_at(parts, *index):
    sums = [part[index].astype(f32) for part in parts]
    while len(sums) > 1:
        sums = [one + other for one, other in zip(sums[0::2], sums[1::2])]
    return sums[0]


def first_cut_kernel(kept, received, own, *sent):
    half = own.shape[1]
    for place in range(own.shape[0]):
        for mask, out in enumerate((own, *sent)):
            node = 2 * place + ((lax.axis_index("nodes") & 1) ^ (mask & 1))
            rows = ((lax.axis_index("rep") >> 1) & 1) ^ (mask >> 1)
            rows = pl.ds(pl.multiple_of(rows * half, half), half)
            out[place] = total_at((kept, received), node, rows).astype(out.dtype)


def cut_kernel(*refs, count, bit, ways):
    parts, outs = refs[:count], refs[count:]
    mine = lax.axis_index("nodes") // bit & (ways - 1)
    for place in range(outs[0].shape[0]):
        for mask, out in enumerate(outs):
            out[place] = total_at(parts, ways * place + (mine ^ mask)).astype(out.dtype)


def last_kernel(own, *refs):
    *received, class_row, out = refs[: -(LAYERS + 2)] + refs[-2:]
    bias_rows = refs[-(LAYERS + 3) : -2]
    rows = own.shape[1]
    grad = total_at((own, *received), 0)
    out[:rows] = grad
    out[rows : rows + 8] = jnp.sum((grad * grad).reshape(rows // 8, 8, LANES), axis=0)
    out[rows + 8 : rows + 16] = jnp.broadcast_to(class_row[...], (8, LANES))
    out[rows + 16 :] = jnp.concatenate(
        [row[:, side * LANES : (side + 1) * LANES] for side in range(2) for row in bias_rows], axis=0
    )


def update_kernel(*refs):
    (mine_ref, theirs), rest = refs[:2], refs[2:]
    params, firsts, seconds = rest[:5], rest[5:10], rest[10:15]
    updated, drifts, spreads, copied = rest[15:20], rest[20:25], rest[25:30], rest[30:34]
    loss_ref, count_ref, norm_ref, grad = rest[34:]
    quarter = (mine_ref.shape[0] - 24) // 2
    tile = mine_ref[2 * quarter :] + theirs[2 * quarter :]
    high, odd = (lax.axis_index("rep") >> 1) & 1, lax.axis_index("rep") & 1
    upper = pl.multiple_of(high * quarter, quarter)
    lower = pl.multiple_of((1 - high) * quarter, quarter)
    mine = pl.ds(pl.multiple_of(odd * LANES, LANES), LANES)
    other = pl.ds(pl.multiple_of((1 - odd) * LANES, LANES), LANES)
    grad[pl.ds(upper, quarter), mine] = mine_ref[:quarter]
    grad[pl.ds(lower, quarter), mine] = mine_ref[quarter : 2 * quarter]
    grad[pl.ds(upper, quarter), other] = theirs[:quarter]
    grad[pl.ds(lower, quarter), other] = theirs[quarter : 2 * quarter]

    classes = params[4].shape[1]
    lane = lax.broadcasted_iota(jnp.int32, (1, LANES), 1)
    class_row = tile[8:9]
    class_grad = jnp.where(lane < classes, class_row, 0.0)
    bias_low, bias_high = tile[16:20], tile[20:24]
    squares = (
        jnp.sum(tile[:8], keepdims=True)
        + jnp.sum(class_grad * class_grad, keepdims=True)
        + jnp.sum(bias_low * bias_low, keepdims=True)
        + jnp.sum(bias_high * bias_high, keepdims=True)
    )
    norm = jnp.sqrt(squares)
    scale = jnp.minimum(1.0, 1.0 / (norm + 1e-06))
    loss_ref[...] = jnp.sum(jnp.where(lane == classes, class_row, 0.0), axis=1, keepdims=True)
    count_ref[...] = jnp.sum(jnp.where(lane == classes + 1, class_row, 0.0), axis=1, keepdims=True)
    norm_ref[...] = norm

    encoder_rows, layer_rows = params[0].shape[0], params[1].shape[1]
    ends = encoder_rows + LAYERS * layer_rows
    head_half = params[2].shape[0] // 2
    columns = params[3].shape[1]
    width = 2 * LANES
    biases = jnp.concatenate([bias_low, bias_high], axis=1)
    biases = pltpu.roll(biases, (width - lax.axis_index("nodes") * columns) % width, 1)[:, :columns]

    def step(index, at, gradient):
        new, drift, spread = adamw(params[index][at], firsts[index][at], seconds[index][at], gradient, scale)
        updated[index][at] = new
        drifts[index][at] = drift
        spreads[index][at] = spread
        if index < 4:
            copied[index][at] = new.astype(bf16)

    step(0, slice(None), grad[:encoder_rows])
    for layer in range(LAYERS):
        start = encoder_rows + layer * layer_rows
        step(1, layer, grad[start : start + layer_rows])
    step(2, slice(0, head_half), grad[ends:, :LANES][:, :classes])
    step(2, slice(head_half, 2 * head_half), grad[ends:, LANES:][:, :classes])
    step(3, slice(None), biases)
    step(4, slice(None), class_grad[:, :classes])


def adamw(weight, first, second, grad, scale):
    scaled = grad * scale
    drift = beta_one * first + (1.0 - beta_one) * scaled
    spread = beta_two * second + (1.0 - beta_two) * scaled * scaled
    corrected = drift / (1.0 - beta_one**STEP)
    denominator = jnp.sqrt(spread / (1.0 - beta_two**STEP)) + epsilon
    return (weight - rate * (corrected / denominator + decay * weight), drift, spread)


def plain_pack(encoder, layers, head, biases):
    head = jnp.pad(head, ((0, 0), (0, PAD_AT - head.shape[1])))
    bias = jnp.pad(biases, ((0, head.shape[0] - biases.shape[0]), (0, LANES - PAD_AT - biases.shape[1])))
    tail = jnp.concatenate([head, bias], axis=1)
    half = tail.shape[0] // 2
    tail = jnp.concatenate([tail[:half], tail[half:]], axis=1)
    odd = (lax.axis_index("rep") & 1) == 1
    rows = jnp.concatenate([encoder, *layers, tail], axis=0)
    return jnp.where(odd, rows[:, LANES:], rows[:, :LANES]).astype(bf16)


def plain_assemble(mine, theirs, order, sizes):
    places = [0] * len(order)
    for place, node in enumerate(order):
        places[node] = place
    places = jnp.asarray(places)[lax.axis_index("nodes") ^ jnp.arange(len(order))]
    mine, theirs = jnp.take(mine, places, axis=0), jnp.take(theirs, places, axis=0)
    odd = (lax.axis_index("rep") & 1) == 1
    rows = jnp.concatenate([jnp.where(odd, theirs, mine), jnp.where(odd, mine, theirs)], axis=2)
    outs, start = [], 0
    for size in sizes:
        outs.append(rows[:, start : start + size].reshape(-1, rows.shape[2]))
        start += size
    if start < rows.shape[1]:
        tail = rows[:, start:]
        tail = jnp.concatenate([tail[..., :LANES], tail[..., LANES:]], axis=1)
        columns = rows.shape[2] // len(order)
        bias = tail[:, : LAYERS + 1, PAD_AT : PAD_AT + columns].astype(f32)
        outs += [tail.reshape(-1, LANES), jnp.swapaxes(bias, 0, 1).reshape(LAYERS + 1, rows.shape[2])]
    return outs


def plain_gradients(rounded, averaged, low_grad, features, means, low_self, low_mean, *rest, groups):
    *others, head = rest
    encoder = dot_rows(features, low_self) + dot_rows(means, low_mean)
    layer = jnp.concatenate([dot_rows(rounded, low_grad), dot_rows(averaged, low_grad)], axis=0)
    parts = [part.reshape(groups, -1, part.shape[1]) for part in (encoder, layer, *others, head)]
    half = parts[-1].shape[1] // 2
    parts[-1] = jnp.concatenate([parts[-1][:, :half], parts[-1][:, half:]], axis=2)
    rows = jnp.concatenate(parts, axis=1)
    odd = (lax.axis_index("rep") & 1) == 1
    low, high = rows[..., :LANES], rows[..., LANES:]
    return jnp.where(odd, low, high).astype(bf16), jnp.where(odd, high, low)


def plain_first_cut(kept, received):
    total = kept + received.astype(f32)
    half = total.shape[1] // 2
    total = total.reshape(total.shape[0] // 2, 2, 2, half, LANES)
    outs = []
    for mask in range(4):
        node = (lax.axis_index("nodes") & 1) ^ (mask & 1)
        rows = ((lax.axis_index("rep") >> 1) & 1) ^ (mask >> 1)
        part = lax.dynamic_slice(total, (0, node, rows, 0, 0), (total.shape[0], 1, 1, half, LANES))
        outs.append(part.reshape(-1, half, LANES).astype(bf16 if mask else f32))
    return outs


def plain_last(own, *refs):
    received, bias_rows, class_row = refs[: -(LAYERS + 2)], refs[-(LAYERS + 2) : -1], refs[-1]
    grad = total_at((own, *received), 0)
    squares = jnp.pad(jnp.sum(grad * grad, axis=0, keepdims=True), ((0, 7), (0, 0)))
    bias = [row[:, side * LANES : (side + 1) * LANES] for side in range(2) for row in bias_rows]
    return jnp.concatenate([grad, squares, jnp.broadcast_to(class_row, (8, LANES)), *bias], axis=0)


def plain_update(mine, theirs, *rest):
    params, firsts, seconds = rest[:5], rest[5:10], rest[10:15]
    quarter = (mine.shape[0] - 24) // 2
    tile = mine[2 * quarter :] + theirs[2 * quarter :]
    high, odd = (lax.axis_index("rep") >> 1) & 1 == 1, lax.axis_index("rep") & 1 == 1
    sides = []
    for part in (mine, theirs):
        one, other = part[:quarter], part[quarter : 2 * quarter]
        sides.append(jnp.concatenate([jnp.where(high, other, one), jnp.where(high, one, other)], axis=0))
    rows = jnp.concatenate([jnp.where(odd, *sides[::-1]), jnp.where(odd, *sides)], axis=1)
    classes = params[4].shape[1]
    class_grad = tile[8:9, :classes]
    biases = jnp.concatenate([tile[16:20], tile[20:24]], axis=1)
    norm = jnp.sqrt(jnp.sum(tile[:8]) + jnp.sum(class_grad * class_grad) + jnp.sum(biases * biases))
    scale = jnp.minimum(1.0, 1.0 / (norm + 1e-06))
    encoder_rows, layer_rows = params[0].shape[0], params[1].shape[1]
    ends = encoder_rows + LAYERS * layer_rows
    columns = params[3].shape[1]
    grads = (
        rows[:encoder_rows],
        rows[encoder_rows:ends].reshape(LAYERS, layer_rows, -1),
        jnp.concatenate([rows[ends:, :LANES], rows[ends:, LANES:]], axis=0)[:, :classes],
        lax.dynamic_slice_in_dim(biases, lax.axis_index("nodes") * columns, columns, axis=1),
        class_grad,
    )
    results = [adamw(params[at], firsts[at], seconds[at], grads[at], scale) for at in range(5)]
    new = [entry[0] for entry in results]
    scalars = (tile[8, classes], tile[8, classes + 1], norm)
    return (
        *new, *[entry[1] for entry in results], *[entry[2] for entry in results],
        *[entry.astype(bf16) for entry in new[:4]], *scalars,
    )


def per_device(
    features,
    node_count,
    neighbours,
    neighbour_count,
    label_mask,
    labels,
    encoder_weight,
    layer_weights,
    head_weight,
    biases,
    class_bias,
    mean_encoder,
    mean_layers,
    mean_head,
    mean_biases,
    mean_class,
    square_encoder,
    square_layers,
    square_head,
    square_biases,
    square_class,
):
    node_rows = features.shape[0]
    fan = neighbours.shape[1]
    width = encoder_weight.shape[1]
    classes = class_bias.shape[0]
    groups = lax.axis_size("nodes")
    copies = lax.axis_size("rep")
    here_node = lax.axis_index("nodes")
    member = lax.axis_index("rep")
    encoder_rows, layer_rows, bias_columns = (
        encoder_weight.shape[0],
        layer_weights.shape[1],
        biases.shape[1],
    )

    owner = jnp.floor_divide(neighbours, node_rows)
    group = jnp.floor_divide(owner, copies)
    offset = jnp.where(group == here_node, 1, jnp.where(group == here_node ^ 1, 0, 2))
    codes = (offset * copies + jnp.mod(owner, copies)) * node_rows + jnp.mod(neighbours, node_rows)
    edge_live = lax.broadcasted_iota(jnp.int32, neighbours.shape, 1) < neighbour_count[:, None]
    codes = jnp.where(edge_live, codes, -1).reshape(node_rows * fan // BATCH, BATCH)
    codes = split_codes(codes)
    to_around = jnp.concatenate([features, codes], axis=0)
    partner, _, other = around_of(to_around)
    blocks = [codes]
    for bit in bits_of("rep"):
        blocks = blocks + [swap(block, "rep", bit) for block in blocks]
    own_rows = build_table(codes, 1, node_rows, copies, fan)
    partner, other, own_rows, *blocks[1:] = tied(partner, other, own_rows, *blocks[1:])
    column_tables = [build_table(block, None, node_rows, copies, fan) for block in blocks]

    head_rows = head_weight.shape[0]
    aligned = encoder_rows % 16 == 0 and layer_rows % 16 == 0 and head_rows % 32 == 0
    rows = encoder_rows + LAYERS * layer_rows + head_rows // 2
    weights = (encoder_weight, layer_weights, head_weight, biases)
    in_hbm = [pltpu.with_memory_space_constraint(weight, pltpu.HBM) for weight in weights] if aligned else []
    own_weights = plain_pack(*weights) if not aligned else kernel_call(
        pack_kernel,
        "pack_weights",
        jax.ShapeDtypeStruct((rows, LANES), bf16),
        (*in_hbm, codes),
        (
            pltpu.VMEM((head_rows, LANES), f32),
            *[pltpu.VMEM(weight.shape, f32) for weight in weights],
            pltpu.SemaphoreType.DMA((4,)),
        ),
        pl.BlockSpec(memory_space=pltpu.HBM),
    )
    def over_nodes(part, beside):
        part, order = part[None], [0]
        for bit in bits_of("nodes")[::-1]:
            part = jnp.concatenate([part, swap(part, "nodes", bit)], axis=0)
            order = order + [node ^ bit for node in order]
            if beside:
                part, beside[0] = tied(part, beside[0])
                done.append(beside.pop(0))
        return part, order

    done = []
    own_weights, order = over_nodes(own_weights, column_tables)
    column_tables = done + column_tables
    *feature_products, sent = nodes_first_products(
        column_tables, None, (partner[:node_rows], features, other[:node_rows]), copies, False
    )
    own_weights, sent = tied(own_weights, sent)
    local_rows = lax.broadcasted_iota(jnp.int32, (node_rows,), 0)
    valid_node = (local_rows < node_count[0]).astype(f32)[:, None]
    inverse_count = (1.0 / neighbour_count.astype(f32))[:, None]
    weight_mask = label_mask.astype(f32)[:, None] * valid_node

    def meanwhile(partner, other, held):
        return (
            build_table(partner, 0, node_rows, copies, fan),
            build_table(other, 2, node_rows, copies, fan),
            held,
            swap(held, "rep", 1),
        )

    feature_sums, (*row_tables, mine, theirs) = added_over_group(
        *feature_products, sent, (meanwhile, partner[node_rows:], other[node_rows:], own_weights)
    )
    row_tables.insert(1, own_rows)
    gathered = (mine, theirs)
    sizes = (encoder_rows,) + (layer_rows,) * LAYERS
    encoder, *layers, head, bias_rows = plain_assemble(*gathered, order, sizes) if not aligned else kernel_call(
        functools.partial(assemble_kernel, sizes=sizes, order=order),
        "assemble_weights",
        tuple(jax.ShapeDtypeStruct((groups * size, width), bf16) for size in sizes)
        + (
            jax.ShapeDtypeStruct((groups * head_rows, LANES), bf16),
            jax.ShapeDtypeStruct((min(8, head_rows), width), f32),
        ),
        gathered,
    )
    feature_mean = (feature_sums * inverse_count).astype(bf16)

    rounded = ((dot(features, encoder) + bias_rows[0:1]) * valid_node).astype(bf16)
    averaged = (dot(feature_mean, encoder) + bias_rows[0:1]).astype(bf16)
    low_self_input = (rounded, averaged)
    kept_joined = []
    kept_before = []
    for layer in range(LAYERS):
        if layer > 0:
            sums = exchanged(rounded, column_tables, row_tables, False)
            averaged = (sums * inverse_count).astype(bf16)
        joined = jnp.concatenate([rounded, averaged], axis=1)
        before = dot(joined, layers[layer]) + bias_rows[layer + 1 : layer + 2]
        kept_joined.append(joined)
        kept_before.append(before)
        rounded = act_norm(before).astype(bf16)

    class_ids = lax.broadcasted_iota(jnp.int32, (1, LANES), 1)
    padded_bias = jnp.pad(class_bias, (0, LANES - classes))
    logits = jnp.where(class_ids < classes, dot(rounded, head) + padded_bias, -1e30)
    total_exp = jax.nn.logsumexp(logits, axis=1, keepdims=True)
    target = (class_ids == labels[:, None]).astype(f32)
    picked = jnp.sum(logits * target, axis=1, keepdims=True)
    loss_local = jnp.sum(weight_mask * (total_exp - picked))
    count_local = jnp.sum(weight_mask)
    grad_logits = (jnp.exp(logits - total_exp) - target) * weight_mask
    class_tile = jnp.sum(grad_logits, axis=0, keepdims=True)
    class_tile = jnp.where(class_ids == classes, loss_local, class_tile)
    class_tile = jnp.where(class_ids == classes + 1, count_local, class_tile)
    low_logits = grad_logits.astype(bf16)
    grad_head = dot_rows(rounded, low_logits)
    grad_hidden = dot_columns(low_logits, head)

    grad_weights = [None] * LAYERS
    grad_bias_rows = [None] * (LAYERS + 1)
    for layer in reversed(range(LAYERS)):
        _, pullback = jax.vjp(act_norm, kept_before[layer])
        grad_before = pullback(grad_hidden)[0]
        grad_bias_rows[layer + 1] = jnp.sum(grad_before, axis=0, keepdims=True)
        low_grad = grad_before.astype(bf16)
        if layer > 0:
            grad_weights[layer] = dot_rows(kept_joined[layer], low_grad)
        grad_joined = dot_columns(low_grad, layers[layer])
        grad_self, grad_mean = halves(grad_joined)
        if layer > 0:
            low_grad_sum = (grad_mean * inverse_count).astype(bf16)
            grad_hidden = grad_self + exchanged(low_grad_sum, column_tables, row_tables, True)
            grad_hidden, class_tile = tied(grad_hidden, class_tile)
    grad_self = grad_self * valid_node
    grad_bias_rows[0] = jnp.sum(grad_self + grad_mean, axis=0, keepdims=True)
    inputs = (
        *low_self_input,
        low_grad,
        features,
        feature_mean,
        grad_self.astype(bf16),
        grad_mean.astype(bf16),
        *grad_weights[1:],
        grad_head,
    )
    away, grads = plain_gradients(*inputs, groups=groups) if not aligned else kernel_call(
        functools.partial(gradient_kernel, groups=groups),
        "gradients",
        (
            jax.ShapeDtypeStruct((groups, rows, LANES), bf16),
            jax.ShapeDtypeStruct((groups, rows, LANES), f32),
        ),
        inputs,
        (pltpu.VMEM((features.shape[1], width), f32), pltpu.VMEM((2 * width, width), f32)),
    )

    received = swap(away, "rep", 1)
    half = rows // 2
    own, *sent = plain_first_cut(grads, received) if not aligned else kernel_call(
        first_cut_kernel,
        "first_cut",
        tuple(jax.ShapeDtypeStruct((groups // 2, half, LANES), kind) for kind in (f32, bf16, bf16, bf16)),
        (grads, received),
    )
    received = [swap_both(part, mask & 1, (mask >> 1) * 2) for mask, part in enumerate(sent, 1)]
    for bits in paired(bits_of("nodes")[1:]):
        masks = masks_of(bits)
        parts = (own, *received)
        left = own.shape[0] // len(masks)
        own, *sent = kernel_call(
            functools.partial(cut_kernel, count=len(parts), bit=bits[0], ways=len(masks)),
            "cut",
            tuple(
                jax.ShapeDtypeStruct((left, half, LANES), bf16 if mask else f32) for mask in masks
            ),
            parts,
        )
        received = [swap(part, "nodes", mask) for mask, part in zip(masks[1:], sent)]
    inputs = (own, *received, *grad_bias_rows, class_tile)
    grads = plain_last(*inputs) if not aligned else pl.pallas_call(
        last_kernel,
        out_shape=jax.ShapeDtypeStruct((half + 24, LANES), f32),
        in_specs=[VMEM] * (len(received) + LAYERS + 3),
        out_specs=VMEM,
        compiler_params=pltpu.CompilerParams(vmem_limit_bytes=VMEM_LIMIT),
        name="last_sum",
    )(*inputs)

    tile = grads[half:]
    for bits in paired(bits_of("nodes")[1:]):
        parts = [tile] + [swap(tile, "nodes", mask) for mask in masks_of(bits)[1:]]
        tile = total_at(parts, slice(None))
    across, other, both = (
        swap_both(tile, 1, 0),
        swap(jnp.concatenate([grads[:half], tile], axis=0), "rep", 2),
        swap_both(tile, 1, 2),
    )
    tile = total_at((tile, across, other[half:], both), slice(None))
    grads = jnp.concatenate([grads[:half], other[:half], tile], axis=0)
    received = swap(grads, "rep", 1)

    params = (encoder_weight, layer_weights, head_weight, biases, class_bias[None])
    firsts = (mean_encoder, mean_layers, mean_head, mean_biases, mean_class[None])
    seconds = (square_encoder, square_layers, square_head, square_biases, square_class[None])
    shapes = tuple(jax.ShapeDtypeStruct(param.shape, f32) for param in params)
    lows = tuple(jax.ShapeDtypeStruct(param.shape, bf16) for param in params[:4])
    inputs = (grads, received, *params, *firsts, *seconds)
    results = plain_update(*inputs) if not aligned else pl.pallas_call(
        update_kernel,
        out_shape=shapes * 3 + lows + (jax.ShapeDtypeStruct((1, 1), f32),) * 3,
        in_specs=[VMEM] * 17,
        out_specs=(VMEM,) * 22,
        scratch_shapes=[pltpu.VMEM((rows, width), f32)],
        compiler_params=pltpu.CompilerParams(vmem_limit_bytes=VMEM_LIMIT),
        name="adamw",
    )(*inputs)
    results, scalars = list(results[:19]), results[19:]
    for index in (4, 9, 14):
        results[index] = results[index][0]
    return tuple(results) + tuple(scalar.reshape(()) for scalar in scalars)


def solution(mesh):
    node_arrays = (
        P(("nodes", "rep"), None),
        P(("nodes", "rep")),
        P(("nodes", "rep"), None),
        P(("nodes", "rep")),
        P(("nodes", "rep")),
        P(("nodes", "rep")),
    )
    weights = (P("nodes", None), P(None, "nodes", None), P("nodes", None), P(None, "nodes"), P())
    return jax.shard_map(
        per_device,
        mesh=mesh,
        in_specs=node_arrays + weights * 3,
        out_specs=weights * 3 + weights[:4] + (P(), P(), P()),
        check_vma=False,
    )
```

```python
import functools

import jax
import jax.numpy as jnp
from jax import lax
from jax.experimental import pallas as pl
from jax.experimental.pallas import tpu as pltpu
from jax.sharding import PartitionSpec as P

LAYERS = 3
STEP = 5

beta_one = 0.5
beta_two = 0.5
rate = 0.05
decay = 0.01
epsilon = 1e-08

LANES = 128
LANE_BITS = 7
BATCH = 256
PAD_AT = 64
VMEM_LIMIT = 14 << 20

bf16 = jnp.bfloat16
f32 = jnp.float32
VMEM = pl.BlockSpec(memory_space=pltpu.VMEM)


def swap(array, axis, mask):
    return lax.ppermute(array, axis, [(i, i ^ mask) for i in range(lax.axis_size(axis))])


def swap_both(array, node_mask, rep_mask):
    copies = lax.axis_size("rep")
    count = lax.axis_size("nodes") * copies
    mask = node_mask * copies + rep_mask
    return lax.ppermute(array, ("nodes", "rep"), [(i, i ^ mask) for i in range(count)])


def other_side(array):
    count = lax.axis_size("nodes")
    return lax.ppermute(array, "nodes", [(i, (i + (1 if i % 2 else -1)) % count) for i in range(count)])


def around_of(array):
    other = other_side(array)
    return swap(array, "nodes", 1), array, other


def bits_of(axis):
    return [1 << b for b in range(lax.axis_size(axis).bit_length() - 1)]


def masks_of(bits):
    masks = [0]
    for bit in bits:
        masks = masks + [mask | bit for mask in masks]
    return masks


def paired(bits):
    return [bits[at : at + 2] for at in range(0, len(bits), 2)]


def act_norm(before):
    active = jax.nn.gelu(before)
    return active * lax.rsqrt(jnp.mean(active * active, axis=-1, keepdims=True) + 1e-06)


def dot(left, right):
    return jnp.dot(left, right, preferred_element_type=f32)


def dot_rows(left, right):
    return lax.dot_general(left, right, (((0,), (0,)), ((), ())), preferred_element_type=f32)


def dot_columns(left, right):
    return lax.dot_general(left, right, (((1,), (1,)), ((), ())), preferred_element_type=f32)


def split_codes(codes):
    parts = jnp.concatenate([codes >> LANE_BITS, codes & (LANES - 1)], axis=0).astype(bf16)
    return jnp.concatenate([parts[:, :LANES], parts[:, LANES:]], axis=0)


def table_kernel(codes_ref, table_ref, keys, lows, *, fan, slot_bits, member_bits, by_rows):
    batch_rows = BATCH // fan
    batches = keys.shape[0]
    groups = table_ref.shape[1] // LANES
    mine = lax.axis_index("rep")
    row_id = lax.broadcasted_iota(jnp.int32, (groups * batch_rows, BATCH), 0).astype(bf16)
    lane_id = lax.broadcasted_iota(jnp.int32, (LANES, BATCH), 0).astype(bf16)
    one, zero = jnp.ones((), bf16), jnp.zeros((), bf16)
    group_bits = slot_bits - LANE_BITS
    for half in range(2):
        columns = slice(half * LANES, (half + 1) * LANES)
        start = half * 2 * batches
        upper = codes_ref[start : start + batches].astype(f32).astype(jnp.int32)
        if by_rows is not None:
            inside = (upper >> (member_bits + group_bits)) == by_rows
            group = (upper & ((1 << (member_bits + group_bits)) - 1)) ^ (mine << group_bits)
        else:
            inside = ((upper >> group_bits) & ((1 << member_bits) - 1)) == mine
            group = ((upper >> (member_bits + group_bits)) << group_bits) | (upper & ((1 << group_bits) - 1))
        row = (lax.broadcasted_iota(jnp.int32, upper.shape, 1) + half * LANES) // fan
        keys[:, columns] = jnp.where(inside & (upper >= 0), group * batch_rows + row, -1).astype(f32)
        lows[:, columns] = codes_ref[start + batches : start + 2 * batches].astype(f32)

    def step(batch, carry):
        left = jnp.where(keys[pl.ds(batch, 1), :].astype(bf16) == row_id, one, zero)
        right = jnp.where(lows[pl.ds(batch, 1), :].astype(bf16) == lane_id, one, zero)
        counts = dot_columns(left, right).astype(bf16)
        at = pl.ds(pl.multiple_of(batch * batch_rows, batch_rows), batch_rows)
        for group in range(groups):
            table_ref[at, group * LANES : (group + 1) * LANES] = counts[
                group * batch_rows : (group + 1) * batch_rows
            ]
        return carry

    lax.fori_loop(0, batches, step, 0, unroll=min(16, batches))


def build_table(codes, by_rows, slots, members, fan):
    batches = codes.shape[0] // 4
    columns = (3 if by_rows is None else members) * slots
    return kernel_call(
        functools.partial(
            table_kernel,
            fan=fan,
            slot_bits=slots.bit_length() - 1,
            member_bits=members.bit_length() - 1,
            by_rows=by_rows,
        ),
        "column_table" if by_rows is None else "row_table",
        jax.ShapeDtypeStruct((batches * (BATCH // fan), columns), bf16),
        (codes,),
        (pltpu.VMEM((batches, BATCH), f32), pltpu.VMEM((batches, BATCH), f32)),
    )


def products_kernel(*refs, tables, plan, transposed):
    outs = {entry[0] for entry in plan}
    given, outs = refs[: -len(outs)], refs[-len(outs) :]
    multiply = dot_rows if transposed else dot
    rows = given[-1].shape[0]
    for out, place, terms in plan:
        total = None
        for table, columns, operand in terms:
            one = multiply(given[table][:, columns * rows : (columns + 1) * rows], given[tables + operand][...])
            total = one if total is None else total + one
        outs[out][place * rows : (place + 1) * rows] = total.astype(outs[out].dtype)


def products(name, tables, operands, plan, kinds, transposed):
    rows, width = operands[0].shape
    sizes = [1 + max(place for out, place, _ in plan if out == at) for at in range(len(kinds))]
    outs = kernel_call(
        functools.partial(products_kernel, tables=len(tables), plan=plan, transposed=transposed),
        name,
        tuple(jax.ShapeDtypeStruct((size * rows, width), kind) for size, kind in zip(sizes, kinds)),
        (*tables, *operands),
    )
    return outs if len(kinds) > 1 else outs[0]


def nodes_first_products(column_tables, row_tables, around, members, transposed, after=()):
    sums = []
    for odd, kinds in ((1, (bf16,)), (0, (f32, f32))):
        if not odd and after:
            around = tied(*around, *after)[: len(around)]
        blocks = range(odd, members, 2)
        put = [(0, at) if odd or at == 0 else (1, at - 1) for at in range(len(blocks))]
        if transposed:
            tables = row_tables
            plan = [(*to, [(p, block, p) for p in range(3)]) for to, block in zip(put, blocks)]
        else:
            tables = [column_tables[block] for block in blocks]
            plan = [(*to, [(at, p, p) for p in range(3)]) for at, to in enumerate(put)]
        sums.append(products("nodes_first", tables, around, plan, kinds, transposed))
    return sums[1][0], sums[1][1], sums[0]


def rep_first_products(column_tables, row_tables, blocks, transposed):
    def product(places, blocks):
        kinds = tuple(f32 if place == 1 else bf16 for place in places)
        if transposed:
            tables = column_tables
            plan = [(out, 0, [(at, place, at) for at in range(len(blocks))]) for out, place in enumerate(places)]
        else:
            tables = [row_tables[place] for place in places]
            plan = [(out, 0, [(out, at, at) for at in range(len(blocks))]) for out in range(len(places))]
        return products("rep_first", tables, blocks, plan, kinds, transposed)

    to_far = product((2,), blocks)
    to_partner = product((0,), blocks)
    mine = product((1,), blocks)
    return to_partner, mine, to_far


def added_over_group(mine, kept, sent, later=None, after=None):
    rows = mine.shape[0]
    bits = bits_of("rep")
    terms = []
    for bit in bits[:-1]:
        received = swap(sent, "rep", bit)
        terms.append(received[:rows])
        left = kept.shape[0] // rows
        rest = [
            kept[i * rows : (i + 1) * rows] + received[(i + 1) * rows : (i + 2) * rows].astype(f32)
            for i in range(left)
        ]
        sent = jnp.concatenate(rest[0::2], axis=0).astype(bf16)
        kept = jnp.concatenate(rest[1::2], axis=0) if left > 1 else kept[:0]
    given = []
    if later is not None:
        work, *given = later
        given = work(*[tied(sent, array)[1] for array in given])
    if after is not None:
        given = [*given, *after(sent)]
    last, *given = tied(swap(sent, "rep", bits[-1]), *given)
    return sum([term.astype(f32) for term in terms + [last]], mine), given


def over_group(own):
    blocks = [own]
    for bit in reversed(bits_of("rep")):
        blocks = [part for block in blocks for part in (block, swap(block, "rep", bit))]
    return blocks


def exchanged(array, column_tables, row_tables, transposed, pair=None):
    one, other = halves(array)
    blocks = over_group(other)
    partner, own, far = around_of(one)
    far, partner = tied(far, partner)
    to_partner, mine, to_far = rep_first_products(column_tables, row_tables, blocks, transposed)
    from_far = other_side(to_far)
    from_partner = swap(to_partner, "nodes", 1)
    one = nodes_first_products(column_tables, row_tables, (partner, own, far), len(blocks), transposed)
    one, made = added_over_group(*one, after=lambda sent: (*(() if pair is None else (dot_rows(*tied(*pair, sent)[:2]),)),))
    other = mine + from_partner.astype(f32) + from_far.astype(f32)
    return jnp.concatenate([one, other], axis=1), made


def tied(*arrays):
    return lax.optimization_barrier(arrays)


def halves(array):
    half = array.shape[1] // 2
    return array[:, :half], array[:, half:]


def kernel_call(body, name, out_shape, operands, scratch=(), given=VMEM):
    many = isinstance(out_shape, tuple)
    return pl.pallas_call(
        body,
        out_shape=out_shape,
        in_specs=[given] * len(operands),
        out_specs=(VMEM,) * len(out_shape) if many else VMEM,
        scratch_shapes=list(scratch),
        compiler_params=pltpu.CompilerParams(vmem_limit_bytes=VMEM_LIMIT),
        name=name,
    )(*operands)


def pack_kernel(*refs):
    given, (packed, tail), held, done = refs[:4], refs[5:7], refs[7:11], refs[11]
    copies = [pltpu.make_async_copy(given[at], held[at], done.at[at]) for at in range(4)]
    for copy in copies:
        copy.start()
    for copy in copies:
        copy.wait()
    encoder, layers, head, biases = held
    encoder_rows, layer_rows, rows = encoder.shape[0], layers.shape[1], head.shape[0]
    tail[...] = jnp.zeros_like(tail)
    tail[:, : head.shape[1]] = head[...]
    tail[: biases.shape[0], PAD_AT : PAD_AT + biases.shape[1]] = biases[...]
    for odd in range(2):

        @pl.when((lax.axis_index("rep") & 1) == odd)
        def _(columns=slice(odd * LANES, (odd + 1) * LANES), half=slice(odd * rows // 2, (odd + 1) * rows // 2)):
            packed[:encoder_rows] = encoder[:, columns].astype(bf16)
            for layer in range(LAYERS):
                start = encoder_rows + layer * layer_rows
                packed[start : start + layer_rows] = layers[layer, :, columns].astype(bf16)
            packed[encoder_rows + LAYERS * layer_rows :] = tail[half].astype(bf16)


def assemble_kernel(mine, theirs, *outs, sizes, order):
    for odd in range(2):

        @pl.when((lax.axis_index("rep") & 1) == odd)
        def _(low=(mine, theirs)[odd], high=(theirs, mine)[odd]):
            bias_total = None
            for shard in range(mine.shape[0]):
                node = lax.axis_index("nodes") ^ order[shard]
                start = 0
                for out, rows in zip(outs, sizes):
                    at = pl.ds(pl.multiple_of(node * rows, rows), rows)
                    part = slice(start, start + rows)
                    out[at, :LANES] = low[shard, part]
                    out[at, LANES:] = high[shard, part]
                    start += rows
                if len(outs) == len(sizes):
                    continue
                head, bias_rows = outs[len(sizes) :]
                rows = head.shape[0] // mine.shape[0]
                half = rows // 2
                at = pl.multiple_of(node * rows, rows)
                head[pl.ds(at, half)] = low[shard, start:]
                head[pl.ds(pl.multiple_of(at + half, half), half)] = high[shard, start:]
                columns = bias_rows.shape[1] // mine.shape[0]
                bias = low[shard, start:].astype(f32)
                if half < 8:
                    bias = jnp.concatenate([bias, high[shard, start:].astype(f32)], axis=0)
                bias = bias[: bias_rows.shape[0]]
                lane = lax.broadcasted_iota(jnp.int32, bias.shape, 1)
                bias = jnp.where((lane >= PAD_AT) & (lane < PAD_AT + columns), bias, 0.0)
                wide = jnp.concatenate([bias, jnp.zeros_like(bias)], axis=1)
                wide = pltpu.roll(wide, (node * columns + bias_rows.shape[1] - PAD_AT) % bias_rows.shape[1], 1)
                bias_total = wide if bias_total is None else bias_total + wide
            if bias_total is not None:
                outs[-1][...] = bias_total


def gradient_kernel(
    rounded, averaged, low_grad, features, means, low_self, low_mean, *refs, groups
):
    *others, head, away, kept, encoder_grad, layer_grad = refs
    width = low_grad.shape[1]
    encoder_grad[...] = dot_rows(features[...], low_self[...]) + dot_rows(means[...], low_mean[...])
    layer_grad[:width] = dot_rows(rounded[...], low_grad[...])
    layer_grad[width:] = dot_rows(averaged[...], low_grad[...])
    sources = [encoder_grad, layer_grad] + list(others)
    for odd in range(2):

        @pl.when((lax.axis_index("rep") & 1) == odd)
        def _(odd=odd):
            mine = slice(odd * LANES, (odd + 1) * LANES)
            other = slice((1 - odd) * LANES, (2 - odd) * LANES)
            for node in range(groups):
                start = 0
                for source in sources:
                    rows = source.shape[0] // groups
                    at, put = slice(node * rows, (node + 1) * rows), slice(start, start + rows)
                    kept[node, put] = source[at, mine]
                    away[node, put] = source[at, other].astype(bf16)
                    start += rows
                half = head.shape[0] // groups // 2
                low, high = (2 * node + odd) * half, (2 * node + 1 - odd) * half
                kept[node, start:] = head[low : low + half]
                away[node, start:] = head[high : high + half].astype(bf16)


def total_at(parts, *index):
    sums = [part[index].astype(f32) for part in parts]
    while len(sums) > 1:
        sums = [one + other for one, other in zip(sums[0::2], sums[1::2])]
    return sums[0]


def first_cut_kernel(kept, received, own, *sent):
    half = own.shape[1]
    for place in range(own.shape[0]):
        for mask, out in enumerate((own, *sent)):
            node = 2 * place + ((lax.axis_index("nodes") & 1) ^ (mask & 1))
            rows = ((lax.axis_index("rep") >> 1) & 1) ^ (mask >> 1)
            rows = pl.ds(pl.multiple_of(rows * half, half), half)
            out[place] = total_at((kept, received), node, rows).astype(out.dtype)


def cut_kernel(*refs, count, bit, ways):
    parts, outs = refs[:count], refs[count:]
    mine = lax.axis_index("nodes") // bit & (ways - 1)
    for place in range(outs[0].shape[0]):
        for mask, out in enumerate(outs):
            out[place] = total_at(parts, ways * place + (mine ^ mask)).astype(out.dtype)


def last_kernel(own, received, sums, other_sums, out):
    owners, rows = own.shape[:2]
    mine = lax.axis_index("nodes") // (lax.axis_size("nodes") // owners)
    out[:rows] = total_at((own, received), mine)
    squares = None
    for owner in range(owners):
        grad = total_at((own, received), owner)
        one = jnp.sum((grad * grad).reshape(rows // 8, 8, LANES), axis=0)
        squares = one if squares is None else squares + one
    out[rows : rows + 8] = squares
    out[rows + 8 :] = sums[...] + other_sums[...]


def update_kernel(*refs):
    (mine_ref, theirs), rest = refs[:2], refs[2:]
    params, firsts, seconds = rest[:5], rest[5:10], rest[10:15]
    updated, drifts, spreads, copied = rest[15:20], rest[20:25], rest[25:30], rest[30:34]
    loss_ref, count_ref, norm_ref, grad = rest[34:]
    quarter = (mine_ref.shape[0] - 24) // 2
    tile = mine_ref[2 * quarter :] + theirs[2 * quarter :]
    high, odd = (lax.axis_index("rep") >> 1) & 1, lax.axis_index("rep") & 1
    upper = pl.multiple_of(high * quarter, quarter)
    lower = pl.multiple_of((1 - high) * quarter, quarter)
    mine = pl.ds(pl.multiple_of(odd * LANES, LANES), LANES)
    other = pl.ds(pl.multiple_of((1 - odd) * LANES, LANES), LANES)
    grad[pl.ds(upper, quarter), mine] = mine_ref[:quarter]
    grad[pl.ds(lower, quarter), mine] = mine_ref[quarter : 2 * quarter]
    grad[pl.ds(upper, quarter), other] = theirs[:quarter]
    grad[pl.ds(lower, quarter), other] = theirs[quarter : 2 * quarter]

    classes = params[4].shape[1]
    lane = lax.broadcasted_iota(jnp.int32, (1, LANES), 1)
    class_row = tile[8:9]
    class_grad = jnp.where(lane < classes, class_row, 0.0)
    bias_low, bias_high = tile[16:20], tile[20:24]
    squares = (
        jnp.sum(tile[:8], keepdims=True)
        + jnp.sum(class_grad * class_grad, keepdims=True)
        + jnp.sum(bias_low * bias_low, keepdims=True)
        + jnp.sum(bias_high * bias_high, keepdims=True)
    )
    norm = jnp.sqrt(squares)
    scale = jnp.minimum(1.0, 1.0 / (norm + 1e-06))
    loss_ref[...] = jnp.sum(jnp.where(lane == classes, class_row, 0.0), axis=1, keepdims=True)
    count_ref[...] = jnp.sum(jnp.where(lane == classes + 1, class_row, 0.0), axis=1, keepdims=True)
    norm_ref[...] = norm

    encoder_rows, layer_rows = params[0].shape[0], params[1].shape[1]
    ends = encoder_rows + LAYERS * layer_rows
    head_half = params[2].shape[0] // 2
    columns = params[3].shape[1]
    width = 2 * LANES
    biases = jnp.concatenate([bias_low, bias_high], axis=1)
    biases = pltpu.roll(biases, (width - lax.axis_index("nodes") * columns) % width, 1)[:, :columns]

    def step(index, at, gradient):
        new, drift, spread = adamw(params[index][at], firsts[index][at], seconds[index][at], gradient, scale)
        updated[index][at] = new
        drifts[index][at] = drift
        spreads[index][at] = spread
        if index < 4:
            copied[index][at] = new.astype(bf16)

    step(0, slice(None), grad[:encoder_rows])
    for layer in range(LAYERS):
        start = encoder_rows + layer * layer_rows
        step(1, layer, grad[start : start + layer_rows])
    step(2, slice(0, head_half), grad[ends:, :LANES][:, :classes])
    step(2, slice(head_half, 2 * head_half), grad[ends:, LANES:][:, :classes])
    step(3, slice(None), biases)
    step(4, slice(None), class_grad[:, :classes])


def adamw(weight, first, second, grad, scale):
    scaled = grad * scale
    drift = beta_one * first + (1.0 - beta_one) * scaled
    spread = beta_two * second + (1.0 - beta_two) * scaled * scaled
    corrected = drift / (1.0 - beta_one**STEP)
    denominator = jnp.sqrt(spread / (1.0 - beta_two**STEP)) + epsilon
    return (weight - rate * (corrected / denominator + decay * weight), drift, spread)


def plain_pack(encoder, layers, head, biases):
    head = jnp.pad(head, ((0, 0), (0, PAD_AT - head.shape[1])))
    bias = jnp.pad(biases, ((0, head.shape[0] - biases.shape[0]), (0, LANES - PAD_AT - biases.shape[1])))
    tail = jnp.concatenate([head, bias], axis=1)
    half = tail.shape[0] // 2
    tail = jnp.concatenate([tail[:half], tail[half:]], axis=1)
    odd = (lax.axis_index("rep") & 1) == 1
    rows = jnp.concatenate([encoder, *layers, tail], axis=0)
    return jnp.where(odd, rows[:, LANES:], rows[:, :LANES]).astype(bf16)


def plain_assemble(mine, theirs, order, sizes):
    places = [0] * len(order)
    for place, node in enumerate(order):
        places[node] = place
    places = jnp.asarray(places)[lax.axis_index("nodes") ^ jnp.arange(len(order))]
    mine, theirs = jnp.take(mine, places, axis=0), jnp.take(theirs, places, axis=0)
    odd = (lax.axis_index("rep") & 1) == 1
    rows = jnp.concatenate([jnp.where(odd, theirs, mine), jnp.where(odd, mine, theirs)], axis=2)
    outs, start = [], 0
    for size in sizes:
        outs.append(rows[:, start : start + size].reshape(-1, rows.shape[2]))
        start += size
    if start < rows.shape[1]:
        tail = rows[:, start:]
        tail = jnp.concatenate([tail[..., :LANES], tail[..., LANES:]], axis=1)
        columns = rows.shape[2] // len(order)
        bias = tail[:, : LAYERS + 1, PAD_AT : PAD_AT + columns].astype(f32)
        outs += [tail.reshape(-1, LANES), jnp.swapaxes(bias, 0, 1).reshape(LAYERS + 1, rows.shape[2])]
    return outs


def plain_gradients(rounded, averaged, low_grad, features, means, low_self, low_mean, *rest, groups):
    *others, head = rest
    encoder = dot_rows(features, low_self) + dot_rows(means, low_mean)
    layer = jnp.concatenate([dot_rows(rounded, low_grad), dot_rows(averaged, low_grad)], axis=0)
    parts = [part.reshape(groups, -1, part.shape[1]) for part in (encoder, layer, *others, head)]
    half = parts[-1].shape[1] // 2
    parts[-1] = jnp.concatenate([parts[-1][:, :half], parts[-1][:, half:]], axis=2)
    rows = jnp.concatenate(parts, axis=1)
    odd = (lax.axis_index("rep") & 1) == 1
    low, high = rows[..., :LANES], rows[..., LANES:]
    return jnp.where(odd, low, high).astype(bf16), jnp.where(odd, high, low)


def plain_first_cut(kept, received):
    total = kept + received.astype(f32)
    half = total.shape[1] // 2
    total = total.reshape(total.shape[0] // 2, 2, 2, half, LANES)
    outs = []
    for mask in range(4):
        node = (lax.axis_index("nodes") & 1) ^ (mask & 1)
        rows = ((lax.axis_index("rep") >> 1) & 1) ^ (mask >> 1)
        part = lax.dynamic_slice(total, (0, node, rows, 0, 0), (total.shape[0], 1, 1, half, LANES))
        outs.append(part.reshape(-1, half, LANES).astype(bf16 if mask else f32))
    return outs


def plain_last(own, received, sums, other_sums):
    grad = own.astype(f32) + received.astype(f32)
    squares = jnp.pad(jnp.sum(grad * grad, axis=(0, 1))[None], ((0, 7), (0, 0)))
    mine = lax.axis_index("nodes") // (lax.axis_size("nodes") // own.shape[0])
    grad = lax.dynamic_index_in_dim(grad, mine, 0, keepdims=False)
    return jnp.concatenate([grad, squares, sums + other_sums], axis=0)


def plain_update(mine, theirs, *rest):
    params, firsts, seconds = rest[:5], rest[5:10], rest[10:15]
    quarter = (mine.shape[0] - 24) // 2
    tile = mine[2 * quarter :] + theirs[2 * quarter :]
    high, odd = (lax.axis_index("rep") >> 1) & 1 == 1, lax.axis_index("rep") & 1 == 1
    sides = []
    for part in (mine, theirs):
        one, other = part[:quarter], part[quarter : 2 * quarter]
        sides.append(jnp.concatenate([jnp.where(high, other, one), jnp.where(high, one, other)], axis=0))
    rows = jnp.concatenate([jnp.where(odd, *sides[::-1]), jnp.where(odd, *sides)], axis=1)
    classes = params[4].shape[1]
    class_grad = tile[8:9, :classes]
    biases = jnp.concatenate([tile[16:20], tile[20:24]], axis=1)
    norm = jnp.sqrt(jnp.sum(tile[:8]) + jnp.sum(class_grad * class_grad) + jnp.sum(biases * biases))
    scale = jnp.minimum(1.0, 1.0 / (norm + 1e-06))
    encoder_rows, layer_rows = params[0].shape[0], params[1].shape[1]
    ends = encoder_rows + LAYERS * layer_rows
    columns = params[3].shape[1]
    grads = (
        rows[:encoder_rows],
        rows[encoder_rows:ends].reshape(LAYERS, layer_rows, -1),
        jnp.concatenate([rows[ends:, :LANES], rows[ends:, LANES:]], axis=0)[:, :classes],
        lax.dynamic_slice_in_dim(biases, lax.axis_index("nodes") * columns, columns, axis=1),
        class_grad,
    )
    results = [adamw(params[at], firsts[at], seconds[at], grads[at], scale) for at in range(5)]
    new = [entry[0] for entry in results]
    scalars = (tile[8, classes], tile[8, classes + 1], norm)
    return (
        *new, *[entry[1] for entry in results], *[entry[2] for entry in results],
        *[entry.astype(bf16) for entry in new[:4]], *scalars,
    )


def per_device(
    features,
    node_count,
    neighbours,
    neighbour_count,
    label_mask,
    labels,
    encoder_weight,
    layer_weights,
    head_weight,
    biases,
    class_bias,
    mean_encoder,
    mean_layers,
    mean_head,
    mean_biases,
    mean_class,
    square_encoder,
    square_layers,
    square_head,
    square_biases,
    square_class,
):
    node_rows = features.shape[0]
    fan = neighbours.shape[1]
    width = encoder_weight.shape[1]
    classes = class_bias.shape[0]
    groups = lax.axis_size("nodes")
    copies = lax.axis_size("rep")
    here_node = lax.axis_index("nodes")
    member = lax.axis_index("rep")
    encoder_rows, layer_rows, bias_columns = (
        encoder_weight.shape[0],
        layer_weights.shape[1],
        biases.shape[1],
    )

    owner = jnp.floor_divide(neighbours, node_rows)
    group = jnp.floor_divide(owner, copies)
    offset = jnp.where(group == here_node, 1, jnp.where(group == here_node ^ 1, 0, 2))
    codes = (offset * copies + jnp.mod(owner, copies)) * node_rows + jnp.mod(neighbours, node_rows)
    edge_live = lax.broadcasted_iota(jnp.int32, neighbours.shape, 1) < neighbour_count[:, None]
    codes = jnp.where(edge_live, codes, -1).reshape(node_rows * fan // BATCH, BATCH)
    codes = split_codes(codes)
    to_around = jnp.concatenate([features, codes], axis=0)
    partner, _, other = around_of(to_around)
    blocks = [codes]
    for bit in bits_of("rep"):
        blocks = blocks + [swap(block, "rep", bit) for block in blocks]
    second = build_table(blocks[1], None, node_rows, copies, fan)
    partner, other, second, *blocks[2:] = tied(partner, other, second, *blocks[2:])
    column_tables = [
        second if block is blocks[1] else build_table(block, None, node_rows, copies, fan) for block in blocks
    ]

    head_rows = head_weight.shape[0]
    aligned = encoder_rows % 16 == 0 and layer_rows % 16 == 0 and head_rows % 32 == 0
    rows = encoder_rows + LAYERS * layer_rows + head_rows // 2
    weights = (encoder_weight, layer_weights, head_weight, biases)
    in_hbm = [pltpu.with_memory_space_constraint(weight, pltpu.HBM) for weight in weights] if aligned else []
    own_weights = plain_pack(*weights) if not aligned else kernel_call(
        pack_kernel,
        "pack_weights",
        jax.ShapeDtypeStruct((rows, LANES), bf16),
        (*in_hbm, codes),
        (
            pltpu.VMEM((head_rows, LANES), f32),
            *[pltpu.VMEM(weight.shape, f32) for weight in weights],
            pltpu.SemaphoreType.DMA((4,)),
        ),
        pl.BlockSpec(memory_space=pltpu.HBM),
    )
    def over_nodes(part, beside):
        part, order = part[None], [0]
        for bit in bits_of("nodes")[::-1]:
            part = jnp.concatenate([part, swap(part, "nodes", bit)], axis=0)
            order = order + [node ^ bit for node in order]
            if beside:
                part, beside[0] = tied(part, beside[0])
                done.append(beside.pop(0))
        return part, order

    done = []
    own_weights, order = over_nodes(own_weights, column_tables)
    column_tables = done + column_tables
    *feature_products, sent = nodes_first_products(
        column_tables, None, (partner[:node_rows], features, other[:node_rows]), copies, False
    )
    local_rows = lax.broadcasted_iota(jnp.int32, (node_rows,), 0)
    valid_node = (local_rows < node_count[0]).astype(f32)[:, None]
    inverse_count = (1.0 / neighbour_count.astype(f32))[:, None]
    weight_mask = label_mask.astype(f32)[:, None] * valid_node

    def meanwhile(partner, own, other, held):
        return (
            build_table(partner, 0, node_rows, copies, fan),
            build_table(own, 1, node_rows, copies, fan),
            build_table(other, 2, node_rows, copies, fan),
            held,
            swap(held, "rep", 1),
        )

    feature_sums, (*row_tables, mine, theirs) = added_over_group(
        *feature_products, sent, (meanwhile, partner[node_rows:], codes, other[node_rows:], own_weights)
    )
    gathered = (mine, theirs)
    sizes = (encoder_rows,) + (layer_rows,) * LAYERS
    encoder, *layers, head, bias_rows = plain_assemble(*gathered, order, sizes) if not aligned else kernel_call(
        functools.partial(assemble_kernel, sizes=sizes, order=order),
        "assemble_weights",
        tuple(jax.ShapeDtypeStruct((groups * size, width), bf16) for size in sizes)
        + (
            jax.ShapeDtypeStruct((groups * head_rows, LANES), bf16),
            jax.ShapeDtypeStruct((min(8, head_rows), width), f32),
        ),
        gathered,
    )
    feature_mean = (feature_sums * inverse_count).astype(bf16)

    rounded = ((dot(features, encoder) + bias_rows[0:1]) * valid_node).astype(bf16)
    averaged = (dot(feature_mean, encoder) + bias_rows[0:1]).astype(bf16)
    low_self_input = (rounded, averaged)
    kept_joined = []
    kept_before = []
    for layer in range(LAYERS):
        if layer > 0:
            sums, _ = exchanged(rounded, column_tables, row_tables, False)
            averaged = (sums * inverse_count).astype(bf16)
        joined = jnp.concatenate([rounded, averaged], axis=1)
        before = dot(joined, layers[layer]) + bias_rows[layer + 1 : layer + 2]
        kept_joined.append(joined)
        kept_before.append(before)
        rounded = act_norm(before).astype(bf16)

    class_ids = lax.broadcasted_iota(jnp.int32, (1, LANES), 1)
    padded_bias = jnp.pad(class_bias, (0, LANES - classes))
    logits = jnp.where(class_ids < classes, dot(rounded, head) + padded_bias, -1e30)
    total_exp = jax.nn.logsumexp(logits, axis=1, keepdims=True)
    target = (class_ids == labels[:, None]).astype(f32)
    picked = jnp.sum(logits * target, axis=1, keepdims=True)
    grad_logits = (jnp.exp(logits - total_exp) - target) * weight_mask
    sums = jnp.where(class_ids == classes, weight_mask * (total_exp - picked), grad_logits)
    sums = jnp.where(class_ids == classes + 1, weight_mask, sums)
    class_tile = jnp.sum(sums, axis=0, keepdims=True)
    low_logits = grad_logits.astype(bf16)
    grad_head = dot_rows(rounded, low_logits)
    grad_hidden = dot_columns(low_logits, head)

    grad_weights = [None] * LAYERS
    grad_bias_rows = [None] * (LAYERS + 1)
    for layer in reversed(range(LAYERS)):
        _, pullback = jax.vjp(act_norm, kept_before[layer])
        grad_before = pullback(grad_hidden)[0]
        grad_bias_rows[layer + 1] = jnp.sum(grad_before, axis=0, keepdims=True)
        low_grad = grad_before.astype(bf16)
        grad_joined = dot_columns(low_grad, layers[layer])
        grad_self, grad_mean = halves(grad_joined)
        if layer > 0:
            low_grad_sum = (grad_mean * inverse_count).astype(bf16)
            received, (grad_weights[layer],) = exchanged(
                low_grad_sum, column_tables, row_tables, True, (kept_joined[layer], low_grad)
            )
            grad_hidden = grad_self + received
            grad_hidden, class_tile = tied(grad_hidden, class_tile)
    grad_self = grad_self * valid_node
    grad_bias_rows[0] = jnp.sum(grad_self + grad_mean, axis=0, keepdims=True)
    inputs = (
        *low_self_input,
        low_grad,
        features,
        feature_mean,
        grad_self.astype(bf16),
        grad_mean.astype(bf16),
        *grad_weights[1:],
        grad_head,
    )
    away, grads = plain_gradients(*inputs, groups=groups) if not aligned else kernel_call(
        functools.partial(gradient_kernel, groups=groups),
        "gradients",
        (
            jax.ShapeDtypeStruct((groups, rows, LANES), bf16),
            jax.ShapeDtypeStruct((groups, rows, LANES), f32),
        ),
        inputs,
        (pltpu.VMEM((features.shape[1], width), f32), pltpu.VMEM((2 * width, width), f32)),
    )

    received = swap(away, "rep", 1)
    half = rows // 2
    own, *sent = plain_first_cut(grads, received) if not aligned else kernel_call(
        first_cut_kernel,
        "first_cut",
        tuple(jax.ShapeDtypeStruct((groups // 2, half, LANES), kind) for kind in (f32, bf16, bf16, bf16)),
        (grads, received),
    )
    received = [swap_both(part, mask & 1, (mask >> 1) * 2) for mask, part in enumerate(sent, 1)]
    *steps, last_step = bits_of("nodes")[1:]
    for bit in steps:
        parts = (own, *received)
        kinds = (f32, bf16)
        own, sent = kernel_call(
            functools.partial(cut_kernel, count=len(parts), bit=bit, ways=2),
            "cut",
            tuple(jax.ShapeDtypeStruct((own.shape[0] // 2, half, LANES), kind) for kind in kinds),
            parts,
        )
        received = (swap(sent, "nodes", bit),)
    own = total_at((own, *received), slice(None)).astype(bf16)
    bias_grads = [row[:, side * LANES : (side + 1) * LANES] for side in range(2) for row in grad_bias_rows]
    sums = jnp.concatenate([jnp.broadcast_to(class_tile, (8, LANES)), *bias_grads], axis=0)
    received = swap(own, "nodes", last_step), sums, swap(sums, "nodes", last_step)
    inputs = (own, *received)
    grads = plain_last(*inputs) if not aligned else pl.pallas_call(
        last_kernel,
        out_shape=jax.ShapeDtypeStruct((half + 24, LANES), f32),
        in_specs=[VMEM] * 4,
        out_specs=VMEM,
        compiler_params=pltpu.CompilerParams(vmem_limit_bytes=VMEM_LIMIT),
        name="last_sum",
    )(*inputs)

    tile = grads[half:]
    for bit in steps:
        tile = tile + swap(tile, "nodes", bit)
    across, other, both = (
        swap_both(tile, 1, 0),
        swap(jnp.concatenate([grads[:half], tile], axis=0), "rep", 2),
        swap_both(tile, 1, 2),
    )
    tile = total_at((tile, across, other[half:], both), slice(None))
    grads = jnp.concatenate([grads[:half], other[:half], tile], axis=0)
    received = swap(grads, "rep", 1)

    params = (encoder_weight, layer_weights, head_weight, biases, class_bias[None])
    firsts = (mean_encoder, mean_layers, mean_head, mean_biases, mean_class[None])
    seconds = (square_encoder, square_layers, square_head, square_biases, square_class[None])
    shapes = tuple(jax.ShapeDtypeStruct(param.shape, f32) for param in params)
    lows = tuple(jax.ShapeDtypeStruct(param.shape, bf16) for param in params[:4])
    inputs = (grads, received, *params, *firsts, *seconds)
    results = plain_update(*inputs) if not aligned else pl.pallas_call(
        update_kernel,
        out_shape=shapes * 3 + lows + (jax.ShapeDtypeStruct((1, 1), f32),) * 3,
        in_specs=[VMEM] * 17,
        out_specs=(VMEM,) * 22,
        scratch_shapes=[pltpu.VMEM((rows, width), f32)],
        compiler_params=pltpu.CompilerParams(vmem_limit_bytes=VMEM_LIMIT),
        name="adamw",
    )(*inputs)
    results, scalars = list(results[:19]), results[19:]
    for index in (4, 9, 14):
        results[index] = results[index][0]
    return tuple(results) + tuple(scalar.reshape(()) for scalar in scalars)


def solution(mesh):
    node_arrays = (
        P(("nodes", "rep"), None),
        P(("nodes", "rep")),
        P(("nodes", "rep"), None),
        P(("nodes", "rep")),
        P(("nodes", "rep")),
        P(("nodes", "rep")),
    )
    weights = (P("nodes", None), P(None, "nodes", None), P("nodes", None), P(None, "nodes"), P())
    return jax.shard_map(
        per_device,
        mesh=mesh,
        in_specs=node_arrays + weights * 3,
        out_specs=weights * 3 + weights[:4] + (P(), P(), P()),
        check_vma=False,
    )
```

```python
import functools

import jax
import jax.numpy as jnp
from jax import lax
from jax.experimental import pallas as pl
from jax.experimental.pallas import tpu as pltpu
from jax.sharding import PartitionSpec as P

LAYERS = 3
STEP = 5

beta_one = 0.5
beta_two = 0.5
rate = 0.05
decay = 0.01
epsilon = 1e-08

LANES = 128
LANE_BITS = 7
BATCH = 256
PAD_AT = 64
VMEM_LIMIT = 14 << 20

bf16 = jnp.bfloat16
f32 = jnp.float32
VMEM = pl.BlockSpec(memory_space=pltpu.VMEM)


def swap(array, axis, mask):
    return lax.ppermute(array, axis, [(i, i ^ mask) for i in range(lax.axis_size(axis))])


def swap_both(array, node_mask, rep_mask):
    copies = lax.axis_size("rep")
    count = lax.axis_size("nodes") * copies
    mask = node_mask * copies + rep_mask
    return lax.ppermute(array, ("nodes", "rep"), [(i, i ^ mask) for i in range(count)])


def other_side(array):
    count = lax.axis_size("nodes")
    return lax.ppermute(array, "nodes", [(i, (i + (1 if i % 2 else -1)) % count) for i in range(count)])


def around_of(array):
    other = other_side(array)
    return swap(array, "nodes", 1), array, other


def bits_of(axis):
    return [1 << b for b in range(lax.axis_size(axis).bit_length() - 1)]


def masks_of(bits):
    masks = [0]
    for bit in bits:
        masks = masks + [mask | bit for mask in masks]
    return masks


def paired(bits):
    return [bits[at : at + 2] for at in range(0, len(bits), 2)]


def act_norm(before):
    active = jax.nn.gelu(before)
    return active * lax.rsqrt(jnp.mean(active * active, axis=-1, keepdims=True) + 1e-06)


def dot(left, right):
    return jnp.dot(left, right, preferred_element_type=f32)


def dot_rows(left, right):
    return lax.dot_general(left, right, (((0,), (0,)), ((), ())), preferred_element_type=f32)


def dot_columns(left, right):
    return lax.dot_general(left, right, (((1,), (1,)), ((), ())), preferred_element_type=f32)


def split_codes(codes):
    parts = jnp.concatenate([codes >> LANE_BITS, codes & (LANES - 1)], axis=0).astype(bf16)
    return jnp.concatenate([parts[:, :LANES], parts[:, LANES:]], axis=0)


def table_kernel(codes_ref, table_ref, keys, lows, *, fan, slot_bits, member_bits, by_rows):
    batch_rows = BATCH // fan
    batches = keys.shape[0]
    groups = table_ref.shape[1] // LANES
    mine = lax.axis_index("rep")
    row_id = lax.broadcasted_iota(jnp.int32, (groups * batch_rows, BATCH), 0).astype(bf16)
    lane_id = lax.broadcasted_iota(jnp.int32, (LANES, BATCH), 0).astype(bf16)
    one, zero = jnp.ones((), bf16), jnp.zeros((), bf16)
    group_bits = slot_bits - LANE_BITS
    for half in range(2):
        columns = slice(half * LANES, (half + 1) * LANES)
        start = half * 2 * batches
        upper = codes_ref[start : start + batches].astype(f32).astype(jnp.int32)
        if by_rows is not None:
            inside = (upper >> (member_bits + group_bits)) == by_rows
            group = (upper & ((1 << (member_bits + group_bits)) - 1)) ^ (mine << group_bits)
        else:
            inside = ((upper >> group_bits) & ((1 << member_bits) - 1)) == mine
            group = ((upper >> (member_bits + group_bits)) << group_bits) | (upper & ((1 << group_bits) - 1))
        row = (lax.broadcasted_iota(jnp.int32, upper.shape, 1) + half * LANES) // fan
        keys[:, columns] = jnp.where(inside & (upper >= 0), group * batch_rows + row, -1).astype(f32)
        lows[:, columns] = codes_ref[start + batches : start + 2 * batches].astype(f32)

    def step(batch, carry):
        left = jnp.where(keys[pl.ds(batch, 1), :].astype(bf16) == row_id, one, zero)
        right = jnp.where(lows[pl.ds(batch, 1), :].astype(bf16) == lane_id, one, zero)
        counts = dot_columns(left, right).astype(bf16)
        at = pl.ds(pl.multiple_of(batch * batch_rows, batch_rows), batch_rows)
        for group in range(groups):
            table_ref[at, group * LANES : (group + 1) * LANES] = counts[
                group * batch_rows : (group + 1) * batch_rows
            ]
        return carry

    lax.fori_loop(0, batches, step, 0, unroll=min(16, batches))


def build_table(codes, by_rows, slots, members, fan):
    batches = codes.shape[0] // 4
    columns = (3 if by_rows is None else members) * slots
    return kernel_call(
        functools.partial(
            table_kernel,
            fan=fan,
            slot_bits=slots.bit_length() - 1,
            member_bits=members.bit_length() - 1,
            by_rows=by_rows,
        ),
        "column_table" if by_rows is None else "row_table",
        jax.ShapeDtypeStruct((batches * (BATCH // fan), columns), bf16),
        (codes,),
        (pltpu.VMEM((batches, BATCH), f32), pltpu.VMEM((batches, BATCH), f32)),
    )


def products_kernel(*refs, tables, plan, transposed):
    outs = {entry[0] for entry in plan}
    given, outs = refs[: -len(outs)], refs[-len(outs) :]
    multiply = dot_rows if transposed else dot
    rows = given[-1].shape[0]
    for out, place, terms in plan:
        total = None
        for table, columns, operand in terms:
            one = multiply(given[table][:, columns * rows : (columns + 1) * rows], given[tables + operand][...])
            total = one if total is None else total + one
        outs[out][place * rows : (place + 1) * rows] = total.astype(outs[out].dtype)


def products(name, tables, operands, plan, kinds, transposed):
    rows, width = operands[0].shape
    sizes = [1 + max(place for out, place, _ in plan if out == at) for at in range(len(kinds))]
    outs = kernel_call(
        functools.partial(products_kernel, tables=len(tables), plan=plan, transposed=transposed),
        name,
        tuple(jax.ShapeDtypeStruct((size * rows, width), kind) for size, kind in zip(sizes, kinds)),
        (*tables, *operands),
    )
    return outs if len(kinds) > 1 else outs[0]


def nodes_first_products(column_tables, row_tables, around, members, transposed, after=()):
    sums = []
    for odd, kinds in ((1, (bf16,)), (0, (f32, f32))):
        if not odd and after:
            around = tied(*around, *after)[: len(around)]
        blocks = range(odd, members, 2)
        put = [(0, at) if odd or at == 0 else (1, at - 1) for at in range(len(blocks))]
        if transposed:
            tables = row_tables
            plan = [(*to, [(p, block, p) for p in range(3)]) for to, block in zip(put, blocks)]
        else:
            tables = [column_tables[block] for block in blocks]
            plan = [(*to, [(at, p, p) for p in range(3)]) for at, to in enumerate(put)]
        sums.append(products("nodes_first", tables, around, plan, kinds, transposed))
    return sums[1][0], sums[1][1], sums[0]


def rep_first_products(column_tables, row_tables, blocks, transposed):
    def product(places, blocks):
        kinds = tuple(f32 if place == 1 else bf16 for place in places)
        if transposed:
            tables = column_tables
            plan = [(out, 0, [(at, place, at) for at in range(len(blocks))]) for out, place in enumerate(places)]
        else:
            tables = [row_tables[place] for place in places]
            plan = [(out, 0, [(out, at, at) for at in range(len(blocks))]) for out in range(len(places))]
        return products("rep_first", tables, blocks, plan, kinds, transposed)

    to_far = product((2,), blocks)
    to_partner = product((0,), blocks)
    mine = product((1,), blocks)
    return to_partner, mine, to_far


def added_over_group(mine, kept, sent, later=None, after=None):
    rows = mine.shape[0]
    bits = bits_of("rep")
    terms = []
    for bit in bits[:-1]:
        received = swap(sent, "rep", bit)
        terms.append(received[:rows])
        left = kept.shape[0] // rows
        rest = [
            kept[i * rows : (i + 1) * rows] + received[(i + 1) * rows : (i + 2) * rows].astype(f32)
            for i in range(left)
        ]
        sent = jnp.concatenate(rest[0::2], axis=0).astype(bf16)
        kept = jnp.concatenate(rest[1::2], axis=0) if left > 1 else kept[:0]
    given = []
    if later is not None:
        work, *given = later
        given = work(*[tied(sent, array)[1] for array in given])
    if after is not None:
        given = [*given, *after(sent)]
    last, *given = tied(swap(sent, "rep", bits[-1]), *given)
    return sum([term.astype(f32) for term in terms + [last]], mine), given


def over_group(own):
    blocks = [own]
    for bit in reversed(bits_of("rep")):
        blocks = [part for block in blocks for part in (block, swap(block, "rep", bit))]
    return blocks


def exchanged(array, column_tables, row_tables, transposed, pair=None, early=False):
    one, other = halves(array)
    blocks = over_group(other)
    partner, own, far = around_of(one)
    far, partner = tied(far, partner)
    if early:
        partner, own_table = tied(partner, row_tables[1])
        row_tables = [row_tables[0], own_table, row_tables[2]]
    to_partner, mine, to_far = rep_first_products(column_tables, row_tables, blocks, transposed)
    from_far = other_side(to_far)
    from_partner = swap(to_partner, "nodes", 1)
    one = nodes_first_products(column_tables, row_tables, (partner, own, far), len(blocks), transposed)
    one, made = added_over_group(*one, after=lambda sent: (*(() if pair is None else (dot_rows(*tied(*pair, sent)[:2]),)),))
    other = mine + from_partner.astype(f32) + from_far.astype(f32)
    return jnp.concatenate([one, other], axis=1), made


def tied(*arrays):
    return lax.optimization_barrier(arrays)


def halves(array):
    half = array.shape[1] // 2
    return array[:, :half], array[:, half:]


def kernel_call(body, name, out_shape, operands, scratch=(), given=VMEM):
    many = isinstance(out_shape, tuple)
    return pl.pallas_call(
        body,
        out_shape=out_shape,
        in_specs=[given] * len(operands),
        out_specs=(VMEM,) * len(out_shape) if many else VMEM,
        scratch_shapes=list(scratch),
        compiler_params=pltpu.CompilerParams(vmem_limit_bytes=VMEM_LIMIT),
        name=name,
    )(*operands)


def pack_kernel(*refs):
    given, (packed, tail), held, done = refs[:4], refs[5:7], refs[7:11], refs[11]
    copies = [pltpu.make_async_copy(given[at], held[at], done.at[at]) for at in range(4)]
    for copy in copies:
        copy.start()
    for copy in copies:
        copy.wait()
    encoder, layers, head, biases = held
    encoder_rows, layer_rows, rows = encoder.shape[0], layers.shape[1], head.shape[0]
    tail[...] = jnp.zeros_like(tail)
    tail[:, : head.shape[1]] = head[...]
    tail[: biases.shape[0], PAD_AT : PAD_AT + biases.shape[1]] = biases[...]
    for odd in range(2):

        @pl.when((lax.axis_index("rep") & 1) == odd)
        def _(columns=slice(odd * LANES, (odd + 1) * LANES), half=slice(odd * rows // 2, (odd + 1) * rows // 2)):
            packed[:encoder_rows] = encoder[:, columns].astype(bf16)
            for layer in range(LAYERS):
                start = encoder_rows + layer * layer_rows
                packed[start : start + layer_rows] = layers[layer, :, columns].astype(bf16)
            packed[encoder_rows + LAYERS * layer_rows :] = tail[half].astype(bf16)


def assemble_kernel(mine, theirs, *outs, sizes, order):
    for odd in range(2):

        @pl.when((lax.axis_index("rep") & 1) == odd)
        def _(low=(mine, theirs)[odd], high=(theirs, mine)[odd]):
            bias_total = None
            for shard in range(mine.shape[0]):
                node = lax.axis_index("nodes") ^ order[shard]
                start = 0
                for out, rows in zip(outs, sizes):
                    at = pl.ds(pl.multiple_of(node * rows, rows), rows)
                    part = slice(start, start + rows)
                    out[at, :LANES] = low[shard, part]
                    out[at, LANES:] = high[shard, part]
                    start += rows
                if len(outs) == len(sizes):
                    continue
                head, bias_rows = outs[len(sizes) :]
                rows = head.shape[0] // mine.shape[0]
                half = rows // 2
                at = pl.multiple_of(node * rows, rows)
                head[pl.ds(at, half)] = low[shard, start:]
                head[pl.ds(pl.multiple_of(at + half, half), half)] = high[shard, start:]
                columns = bias_rows.shape[1] // mine.shape[0]
                bias = low[shard, start:].astype(f32)
                if half < 8:
                    bias = jnp.concatenate([bias, high[shard, start:].astype(f32)], axis=0)
                bias = bias[: bias_rows.shape[0]]
                lane = lax.broadcasted_iota(jnp.int32, bias.shape, 1)
                bias = jnp.where((lane >= PAD_AT) & (lane < PAD_AT + columns), bias, 0.0)
                wide = jnp.concatenate([bias, jnp.zeros_like(bias)], axis=1)
                wide = pltpu.roll(wide, (node * columns + bias_rows.shape[1] - PAD_AT) % bias_rows.shape[1], 1)
                bias_total = wide if bias_total is None else bias_total + wide
            if bias_total is not None:
                outs[-1][...] = bias_total


def gradient_kernel(
    rounded, averaged, low_grad, features, means, low_self, low_mean, *refs, groups
):
    *others, head, away, kept, encoder_grad, layer_grad = refs
    width = low_grad.shape[1]
    encoder_grad[...] = dot_rows(features[...], low_self[...]) + dot_rows(means[...], low_mean[...])
    layer_grad[:width] = dot_rows(rounded[...], low_grad[...])
    layer_grad[width:] = dot_rows(averaged[...], low_grad[...])
    sources = [encoder_grad, layer_grad] + list(others)
    for odd in range(2):

        @pl.when((lax.axis_index("rep") & 1) == odd)
        def _(odd=odd):
            mine = slice(odd * LANES, (odd + 1) * LANES)
            other = slice((1 - odd) * LANES, (2 - odd) * LANES)
            for node in range(groups):
                start = 0
                for source in sources:
                    rows = source.shape[0] // groups
                    at, put = slice(node * rows, (node + 1) * rows), slice(start, start + rows)
                    kept[node, put] = source[at, mine]
                    away[node, put] = source[at, other].astype(bf16)
                    start += rows
                half = head.shape[0] // groups // 2
                low, high = (2 * node + odd) * half, (2 * node + 1 - odd) * half
                kept[node, start:] = head[low : low + half]
                away[node, start:] = head[high : high + half].astype(bf16)


def total_at(parts, *index):
    sums = [part[index].astype(f32) for part in parts]
    while len(sums) > 1:
        sums = [one + other for one, other in zip(sums[0::2], sums[1::2])]
    return sums[0]


def first_cut_kernel(kept, received, own, *sent):
    half = own.shape[1]
    for place in range(own.shape[0]):
        for mask, out in enumerate((own, *sent)):
            node = 2 * place + ((lax.axis_index("nodes") & 1) ^ (mask & 1))
            rows = ((lax.axis_index("rep") >> 1) & 1) ^ (mask >> 1)
            rows = pl.ds(pl.multiple_of(rows * half, half), half)
            out[place] = total_at((kept, received), node, rows).astype(out.dtype)


def cut_kernel(*refs, count, bit, ways):
    parts, outs = refs[:count], refs[count:]
    mine = lax.axis_index("nodes") // bit & (ways - 1)
    for place in range(outs[0].shape[0]):
        for mask, out in enumerate(outs):
            out[place] = total_at(parts, ways * place + (mine ^ mask)).astype(out.dtype)


def last_kernel(own, received, sums, other_sums, out):
    owners, rows = own.shape[:2]
    mine = lax.axis_index("nodes") // (lax.axis_size("nodes") // owners)
    out[:rows] = total_at((own, received), mine)
    squares = None
    for owner in range(owners):
        grad = total_at((own, received), owner)
        one = jnp.sum((grad * grad).reshape(rows // 8, 8, LANES), axis=0)
        squares = one if squares is None else squares + one
    out[rows : rows + 8] = squares
    out[rows + 8 :] = sums[...] + other_sums[...]


def update_kernel(*refs):
    (mine_ref, theirs), rest = refs[:2], refs[2:]
    params, firsts, seconds = rest[:5], rest[5:10], rest[10:15]
    updated, drifts, spreads, copied = rest[15:20], rest[20:25], rest[25:30], rest[30:34]
    loss_ref, count_ref, norm_ref, grad = rest[34:]
    quarter = (mine_ref.shape[0] - 24) // 2
    tile = mine_ref[2 * quarter :] + theirs[2 * quarter :]
    high, odd = (lax.axis_index("rep") >> 1) & 1, lax.axis_index("rep") & 1
    upper = pl.multiple_of(high * quarter, quarter)
    lower = pl.multiple_of((1 - high) * quarter, quarter)
    mine = pl.ds(pl.multiple_of(odd * LANES, LANES), LANES)
    other = pl.ds(pl.multiple_of((1 - odd) * LANES, LANES), LANES)
    grad[pl.ds(upper, quarter), mine] = mine_ref[:quarter]
    grad[pl.ds(lower, quarter), mine] = mine_ref[quarter : 2 * quarter]
    grad[pl.ds(upper, quarter), other] = theirs[:quarter]
    grad[pl.ds(lower, quarter), other] = theirs[quarter : 2 * quarter]

    classes = params[4].shape[1]
    lane = lax.broadcasted_iota(jnp.int32, (1, LANES), 1)
    class_row = tile[8:9]
    class_grad = jnp.where(lane < classes, class_row, 0.0)
    bias_low, bias_high = tile[16:20], tile[20:24]
    squares = (
        jnp.sum(tile[:8], keepdims=True)
        + jnp.sum(class_grad * class_grad, keepdims=True)
        + jnp.sum(bias_low * bias_low, keepdims=True)
        + jnp.sum(bias_high * bias_high, keepdims=True)
    )
    norm = jnp.sqrt(squares)
    scale = jnp.minimum(1.0, 1.0 / (norm + 1e-06))
    loss_ref[...] = jnp.sum(jnp.where(lane == classes, class_row, 0.0), axis=1, keepdims=True)
    count_ref[...] = jnp.sum(jnp.where(lane == classes + 1, class_row, 0.0), axis=1, keepdims=True)
    norm_ref[...] = norm

    encoder_rows, layer_rows = params[0].shape[0], params[1].shape[1]
    ends = encoder_rows + LAYERS * layer_rows
    head_half = params[2].shape[0] // 2
    columns = params[3].shape[1]
    width = 2 * LANES
    biases = jnp.concatenate([bias_low, bias_high], axis=1)
    biases = pltpu.roll(biases, (width - lax.axis_index("nodes") * columns) % width, 1)[:, :columns]

    def step(index, at, gradient):
        new, drift, spread = adamw(params[index][at], firsts[index][at], seconds[index][at], gradient, scale)
        updated[index][at] = new
        drifts[index][at] = drift
        spreads[index][at] = spread
        if index < 4:
            copied[index][at] = new.astype(bf16)

    step(0, slice(None), grad[:encoder_rows])
    for layer in range(LAYERS):
        start = encoder_rows + layer * layer_rows
        step(1, layer, grad[start : start + layer_rows])
    step(2, slice(0, head_half), grad[ends:, :LANES][:, :classes])
    step(2, slice(head_half, 2 * head_half), grad[ends:, LANES:][:, :classes])
    step(3, slice(None), biases)
    step(4, slice(None), class_grad[:, :classes])


def adamw(weight, first, second, grad, scale):
    scaled = grad * scale
    drift = beta_one * first + (1.0 - beta_one) * scaled
    spread = beta_two * second + (1.0 - beta_two) * scaled * scaled
    corrected = drift / (1.0 - beta_one**STEP)
    denominator = jnp.sqrt(spread / (1.0 - beta_two**STEP)) + epsilon
    return (weight - rate * (corrected / denominator + decay * weight), drift, spread)


def plain_pack(encoder, layers, head, biases):
    head = jnp.pad(head, ((0, 0), (0, PAD_AT - head.shape[1])))
    bias = jnp.pad(biases, ((0, head.shape[0] - biases.shape[0]), (0, LANES - PAD_AT - biases.shape[1])))
    tail = jnp.concatenate([head, bias], axis=1)
    half = tail.shape[0] // 2
    tail = jnp.concatenate([tail[:half], tail[half:]], axis=1)
    odd = (lax.axis_index("rep") & 1) == 1
    rows = jnp.concatenate([encoder, *layers, tail], axis=0)
    return jnp.where(odd, rows[:, LANES:], rows[:, :LANES]).astype(bf16)


def plain_assemble(mine, theirs, order, sizes):
    places = [0] * len(order)
    for place, node in enumerate(order):
        places[node] = place
    places = jnp.asarray(places)[lax.axis_index("nodes") ^ jnp.arange(len(order))]
    mine, theirs = jnp.take(mine, places, axis=0), jnp.take(theirs, places, axis=0)
    odd = (lax.axis_index("rep") & 1) == 1
    rows = jnp.concatenate([jnp.where(odd, theirs, mine), jnp.where(odd, mine, theirs)], axis=2)
    outs, start = [], 0
    for size in sizes:
        outs.append(rows[:, start : start + size].reshape(-1, rows.shape[2]))
        start += size
    if start < rows.shape[1]:
        tail = rows[:, start:]
        tail = jnp.concatenate([tail[..., :LANES], tail[..., LANES:]], axis=1)
        columns = rows.shape[2] // len(order)
        bias = tail[:, : LAYERS + 1, PAD_AT : PAD_AT + columns].astype(f32)
        outs += [tail.reshape(-1, LANES), jnp.swapaxes(bias, 0, 1).reshape(LAYERS + 1, rows.shape[2])]
    return outs


def plain_gradients(rounded, averaged, low_grad, features, means, low_self, low_mean, *rest, groups):
    *others, head = rest
    encoder = dot_rows(features, low_self) + dot_rows(means, low_mean)
    layer = jnp.concatenate([dot_rows(rounded, low_grad), dot_rows(averaged, low_grad)], axis=0)
    parts = [part.reshape(groups, -1, part.shape[1]) for part in (encoder, layer, *others, head)]
    half = parts[-1].shape[1] // 2
    parts[-1] = jnp.concatenate([parts[-1][:, :half], parts[-1][:, half:]], axis=2)
    rows = jnp.concatenate(parts, axis=1)
    odd = (lax.axis_index("rep") & 1) == 1
    low, high = rows[..., :LANES], rows[..., LANES:]
    return jnp.where(odd, low, high).astype(bf16), jnp.where(odd, high, low)


def plain_first_cut(kept, received):
    total = kept + received.astype(f32)
    half = total.shape[1] // 2
    total = total.reshape(total.shape[0] // 2, 2, 2, half, LANES)
    outs = []
    for mask in range(4):
        node = (lax.axis_index("nodes") & 1) ^ (mask & 1)
        rows = ((lax.axis_index("rep") >> 1) & 1) ^ (mask >> 1)
        part = lax.dynamic_slice(total, (0, node, rows, 0, 0), (total.shape[0], 1, 1, half, LANES))
        outs.append(part.reshape(-1, half, LANES).astype(bf16 if mask else f32))
    return outs


def plain_last(own, received, sums, other_sums):
    grad = own.astype(f32) + received.astype(f32)
    squares = jnp.pad(jnp.sum(grad * grad, axis=(0, 1))[None], ((0, 7), (0, 0)))
    mine = lax.axis_index("nodes") // (lax.axis_size("nodes") // own.shape[0])
    grad = lax.dynamic_index_in_dim(grad, mine, 0, keepdims=False)
    return jnp.concatenate([grad, squares, sums + other_sums], axis=0)


def plain_update(mine, theirs, *rest):
    params, firsts, seconds = rest[:5], rest[5:10], rest[10:15]
    quarter = (mine.shape[0] - 24) // 2
    tile = mine[2 * quarter :] + theirs[2 * quarter :]
    high, odd = (lax.axis_index("rep") >> 1) & 1 == 1, lax.axis_index("rep") & 1 == 1
    sides = []
    for part in (mine, theirs):
        one, other = part[:quarter], part[quarter : 2 * quarter]
        sides.append(jnp.concatenate([jnp.where(high, other, one), jnp.where(high, one, other)], axis=0))
    rows = jnp.concatenate([jnp.where(odd, *sides[::-1]), jnp.where(odd, *sides)], axis=1)
    classes = params[4].shape[1]
    class_grad = tile[8:9, :classes]
    biases = jnp.concatenate([tile[16:20], tile[20:24]], axis=1)
    norm = jnp.sqrt(jnp.sum(tile[:8]) + jnp.sum(class_grad * class_grad) + jnp.sum(biases * biases))
    scale = jnp.minimum(1.0, 1.0 / (norm + 1e-06))
    encoder_rows, layer_rows = params[0].shape[0], params[1].shape[1]
    ends = encoder_rows + LAYERS * layer_rows
    columns = params[3].shape[1]
    grads = (
        rows[:encoder_rows],
        rows[encoder_rows:ends].reshape(LAYERS, layer_rows, -1),
        jnp.concatenate([rows[ends:, :LANES], rows[ends:, LANES:]], axis=0)[:, :classes],
        lax.dynamic_slice_in_dim(biases, lax.axis_index("nodes") * columns, columns, axis=1),
        class_grad,
    )
    results = [adamw(params[at], firsts[at], seconds[at], grads[at], scale) for at in range(5)]
    new = [entry[0] for entry in results]
    scalars = (tile[8, classes], tile[8, classes + 1], norm)
    return (
        *new, *[entry[1] for entry in results], *[entry[2] for entry in results],
        *[entry.astype(bf16) for entry in new[:4]], *scalars,
    )


def per_device(
    features,
    node_count,
    neighbours,
    neighbour_count,
    label_mask,
    labels,
    encoder_weight,
    layer_weights,
    head_weight,
    biases,
    class_bias,
    mean_encoder,
    mean_layers,
    mean_head,
    mean_biases,
    mean_class,
    square_encoder,
    square_layers,
    square_head,
    square_biases,
    square_class,
):
    node_rows = features.shape[0]
    fan = neighbours.shape[1]
    width = encoder_weight.shape[1]
    classes = class_bias.shape[0]
    groups = lax.axis_size("nodes")
    copies = lax.axis_size("rep")
    here_node = lax.axis_index("nodes")
    member = lax.axis_index("rep")
    encoder_rows, layer_rows, bias_columns = (
        encoder_weight.shape[0],
        layer_weights.shape[1],
        biases.shape[1],
    )

    owner = jnp.floor_divide(neighbours, node_rows)
    group = jnp.floor_divide(owner, copies)
    offset = jnp.where(group == here_node, 1, jnp.where(group == here_node ^ 1, 0, 2))
    codes = (offset * copies + jnp.mod(owner, copies)) * node_rows + jnp.mod(neighbours, node_rows)
    edge_live = lax.broadcasted_iota(jnp.int32, neighbours.shape, 1) < neighbour_count[:, None]
    codes = jnp.where(edge_live, codes, -1).reshape(node_rows * fan // BATCH, BATCH)
    codes = split_codes(codes)
    to_around = jnp.concatenate([features, codes], axis=0)
    partner, _, other = around_of(to_around)
    blocks = [codes]
    for bit in bits_of("rep"):
        blocks = blocks + [swap(block, "rep", bit) for block in blocks]
    second = build_table(blocks[1], None, node_rows, copies, fan)
    partner, other, second, *blocks[2:] = tied(partner, other, second, *blocks[2:])
    column_tables = [
        second if block is blocks[1] else build_table(block, None, node_rows, copies, fan) for block in blocks
    ]

    head_rows = head_weight.shape[0]
    aligned = encoder_rows % 16 == 0 and layer_rows % 16 == 0 and head_rows % 32 == 0
    rows = encoder_rows + LAYERS * layer_rows + head_rows // 2
    weights = (encoder_weight, layer_weights, head_weight, biases)
    in_hbm = [pltpu.with_memory_space_constraint(weight, pltpu.HBM) for weight in weights] if aligned else []
    own_weights = plain_pack(*weights) if not aligned else kernel_call(
        pack_kernel,
        "pack_weights",
        jax.ShapeDtypeStruct((rows, LANES), bf16),
        (*in_hbm, codes),
        (
            pltpu.VMEM((head_rows, LANES), f32),
            *[pltpu.VMEM(weight.shape, f32) for weight in weights],
            pltpu.SemaphoreType.DMA((4,)),
        ),
        pl.BlockSpec(memory_space=pltpu.HBM),
    )
    def over_nodes(part, beside):
        part, order = part[None], [0]
        for bit in bits_of("nodes")[::-1]:
            part = jnp.concatenate([part, swap(part, "nodes", bit)], axis=0)
            order = order + [node ^ bit for node in order]
            if beside:
                part, _ = tied(part, beside[0])
                beside = beside[1:]
        return part, order

    own_weights, order = over_nodes(own_weights, column_tables[:2])
    *feature_products, sent = nodes_first_products(
        column_tables, None, (partner[:node_rows], features, other[:node_rows]), copies, False
    )
    local_rows = lax.broadcasted_iota(jnp.int32, (node_rows,), 0)
    valid_node = (local_rows < node_count[0]).astype(f32)[:, None]
    inverse_count = (1.0 / neighbour_count.astype(f32))[:, None]
    weight_mask = label_mask.astype(f32)[:, None] * valid_node

    def meanwhile(partner, other, held):
        return (
            build_table(partner, 0, node_rows, copies, fan),
            build_table(other, 2, node_rows, copies, fan),
            held,
            swap(held, "rep", 1),
        )

    feature_sums, (*row_tables, mine, theirs) = added_over_group(
        *feature_products, sent, (meanwhile, partner[node_rows:], other[node_rows:], own_weights)
    )
    row_tables.insert(1, build_table(codes, 1, node_rows, copies, fan))
    gathered = (mine, theirs)
    sizes = (encoder_rows,) + (layer_rows,) * LAYERS
    encoder, *layers, head, bias_rows = plain_assemble(*gathered, order, sizes) if not aligned else kernel_call(
        functools.partial(assemble_kernel, sizes=sizes, order=order),
        "assemble_weights",
        tuple(jax.ShapeDtypeStruct((groups * size, width), bf16) for size in sizes)
        + (
            jax.ShapeDtypeStruct((groups * head_rows, LANES), bf16),
            jax.ShapeDtypeStruct((min(8, head_rows), width), f32),
        ),
        gathered,
    )
    feature_mean = (feature_sums * inverse_count).astype(bf16)

    rounded = ((dot(features, encoder) + bias_rows[0:1]) * valid_node).astype(bf16)
    averaged = (dot(feature_mean, encoder) + bias_rows[0:1]).astype(bf16)
    low_self_input = (rounded, averaged)
    kept_joined = []
    kept_before = []
    for layer in range(LAYERS):
        if layer > 0:
            sums, _ = exchanged(rounded, column_tables, row_tables, False, early=layer == 1)
            averaged = (sums * inverse_count).astype(bf16)
        joined = jnp.concatenate([rounded, averaged], axis=1)
        before = dot(joined, layers[layer]) + bias_rows[layer + 1 : layer + 2]
        kept_joined.append(joined)
        kept_before.append(before)
        rounded = act_norm(before).astype(bf16)

    class_ids = lax.broadcasted_iota(jnp.int32, (1, LANES), 1)
    padded_bias = jnp.pad(class_bias, (0, LANES - classes))
    logits = jnp.where(class_ids < classes, dot(rounded, head) + padded_bias, -1e30)
    total_exp = jax.nn.logsumexp(logits, axis=1, keepdims=True)
    target = (class_ids == labels[:, None]).astype(f32)
    picked = jnp.sum(logits * target, axis=1, keepdims=True)
    grad_logits = (jnp.exp(logits - total_exp) - target) * weight_mask
    sums = jnp.where(class_ids == classes, weight_mask * (total_exp - picked), grad_logits)
    sums = jnp.where(class_ids == classes + 1, weight_mask, sums)
    class_tile = jnp.sum(sums, axis=0, keepdims=True)
    low_logits = grad_logits.astype(bf16)
    grad_head = dot_rows(rounded, low_logits)
    grad_hidden = dot_columns(low_logits, head)

    grad_weights = [None] * LAYERS
    grad_bias_rows = [None] * (LAYERS + 1)
    for layer in reversed(range(LAYERS)):
        _, pullback = jax.vjp(act_norm, kept_before[layer])
        grad_before = pullback(grad_hidden)[0]
        grad_bias_rows[layer + 1] = jnp.sum(grad_before, axis=0, keepdims=True)
        low_grad = grad_before.astype(bf16)
        grad_joined = dot_columns(low_grad, layers[layer])
        grad_self, grad_mean = halves(grad_joined)
        if layer > 0:
            low_grad_sum = (grad_mean * inverse_count).astype(bf16)
            received, (grad_weights[layer],) = exchanged(
                low_grad_sum, column_tables, row_tables, True, (kept_joined[layer], low_grad)
            )
            grad_hidden = grad_self + received
            grad_hidden, class_tile = tied(grad_hidden, class_tile)
    grad_self = grad_self * valid_node
    grad_bias_rows[0] = jnp.sum(grad_self + grad_mean, axis=0, keepdims=True)
    inputs = (
        *low_self_input,
        low_grad,
        features,
        feature_mean,
        grad_self.astype(bf16),
        grad_mean.astype(bf16),
        *grad_weights[1:],
        grad_head,
    )
    away, grads = plain_gradients(*inputs, groups=groups) if not aligned else kernel_call(
        functools.partial(gradient_kernel, groups=groups),
        "gradients",
        (
            jax.ShapeDtypeStruct((groups, rows, LANES), bf16),
            jax.ShapeDtypeStruct((groups, rows, LANES), f32),
        ),
        inputs,
        (pltpu.VMEM((features.shape[1], width), f32), pltpu.VMEM((2 * width, width), f32)),
    )

    received = swap(away, "rep", 1)
    half = rows // 2
    own, *sent = plain_first_cut(grads, received) if not aligned else kernel_call(
        first_cut_kernel,
        "first_cut",
        tuple(jax.ShapeDtypeStruct((groups // 2, half, LANES), kind) for kind in (f32, bf16, bf16, bf16)),
        (grads, received),
    )
    received = [swap_both(part, mask & 1, (mask >> 1) * 2) for mask, part in enumerate(sent, 1)]
    *steps, last_step = bits_of("nodes")[1:]
    bias_grads = [row[:, side * LANES : (side + 1) * LANES] for side in range(2) for row in grad_bias_rows]
    sums = jnp.concatenate([jnp.broadcast_to(class_tile, (8, LANES)), *bias_grads], axis=0)
    other_sums = swap(sums, "nodes", last_step)
    received[0], other_sums = tied(received[0], other_sums)
    for bit in steps:
        parts = (own, *received)
        kinds = (f32, bf16)
        own, sent = kernel_call(
            functools.partial(cut_kernel, count=len(parts), bit=bit, ways=2),
            "cut",
            tuple(jax.ShapeDtypeStruct((own.shape[0] // 2, half, LANES), kind) for kind in kinds),
            parts,
        )
        received = (swap(sent, "nodes", bit),)
    own = total_at((own, *received), slice(None)).astype(bf16)
    received = swap(own, "nodes", last_step), sums, other_sums
    inputs = (own, *received)
    grads = plain_last(*inputs) if not aligned else pl.pallas_call(
        last_kernel,
        out_shape=jax.ShapeDtypeStruct((half + 24, LANES), f32),
        in_specs=[VMEM] * 4,
        out_specs=VMEM,
        compiler_params=pltpu.CompilerParams(vmem_limit_bytes=VMEM_LIMIT),
        name="last_sum",
    )(*inputs)

    tile = grads[half:]
    for bit in steps:
        tile = tile + swap(tile, "nodes", bit)
    across, other, both = (
        swap_both(tile, 1, 0),
        swap(jnp.concatenate([grads[:half], tile], axis=0), "rep", 2),
        swap_both(tile, 1, 2),
    )
    tile = total_at((tile, across, other[half:], both), slice(None))
    grads = jnp.concatenate([grads[:half], other[:half], tile], axis=0)
    received = swap(grads, "rep", 1)

    params = (encoder_weight, layer_weights, head_weight, biases, class_bias[None])
    firsts = (mean_encoder, mean_layers, mean_head, mean_biases, mean_class[None])
    seconds = (square_encoder, square_layers, square_head, square_biases, square_class[None])
    shapes = tuple(jax.ShapeDtypeStruct(param.shape, f32) for param in params)
    lows = tuple(jax.ShapeDtypeStruct(param.shape, bf16) for param in params[:4])
    inputs = (grads, received, *params, *firsts, *seconds)
    results = plain_update(*inputs) if not aligned else pl.pallas_call(
        update_kernel,
        out_shape=shapes * 3 + lows + (jax.ShapeDtypeStruct((1, 1), f32),) * 3,
        in_specs=[VMEM] * 17,
        out_specs=(VMEM,) * 22,
        scratch_shapes=[pltpu.VMEM((rows, width), f32)],
        compiler_params=pltpu.CompilerParams(vmem_limit_bytes=VMEM_LIMIT),
        name="adamw",
    )(*inputs)
    results, scalars = list(results[:19]), results[19:]
    for index in (4, 9, 14):
        results[index] = results[index][0]
    return tuple(results) + tuple(scalar.reshape(()) for scalar in scalars)


def solution(mesh):
    node_arrays = (
        P(("nodes", "rep"), None),
        P(("nodes", "rep")),
        P(("nodes", "rep"), None),
        P(("nodes", "rep")),
        P(("nodes", "rep")),
        P(("nodes", "rep")),
    )
    weights = (P("nodes", None), P(None, "nodes", None), P("nodes", None), P(None, "nodes"), P())
    return jax.shard_map(
        per_device,
        mesh=mesh,
        in_specs=node_arrays + weights * 3,
        out_specs=weights * 3 + weights[:4] + (P(), P(), P()),
        check_vma=False,
    )
```

```python
import functools

import jax
import jax.numpy as jnp
from jax import lax
from jax.experimental import pallas as pl
from jax.experimental.pallas import tpu as pltpu
from jax.sharding import PartitionSpec as P

LAYERS = 3
STEP = 5

beta_one = 0.5
beta_two = 0.5
rate = 0.05
decay = 0.01
epsilon = 1e-08

LANES = 128
LANE_BITS = 7
BATCH = 256
PAD_AT = 64
VMEM_LIMIT = 14 << 20

bf16 = jnp.bfloat16
f32 = jnp.float32
VMEM = pl.BlockSpec(memory_space=pltpu.VMEM)


def swap(array, axis, mask):
    return lax.ppermute(array, axis, [(i, i ^ mask) for i in range(lax.axis_size(axis))])


def swap_both(array, node_mask, rep_mask):
    copies = lax.axis_size("rep")
    count = lax.axis_size("nodes") * copies
    mask = node_mask * copies + rep_mask
    return lax.ppermute(array, ("nodes", "rep"), [(i, i ^ mask) for i in range(count)])


def other_side(array):
    count = lax.axis_size("nodes")
    return lax.ppermute(array, "nodes", [(i, (i + (1 if i % 2 else -1)) % count) for i in range(count)])


def around_of(array):
    other = other_side(array)
    return swap(array, "nodes", 1), array, other


def bits_of(axis):
    return [1 << b for b in range(lax.axis_size(axis).bit_length() - 1)]


def masks_of(bits):
    masks = [0]
    for bit in bits:
        masks = masks + [mask | bit for mask in masks]
    return masks


def paired(bits):
    return [bits[at : at + 2] for at in range(0, len(bits), 2)]


def act_norm(before):
    active = jax.nn.gelu(before)
    return active * lax.rsqrt(jnp.mean(active * active, axis=-1, keepdims=True) + 1e-06)


def dot(left, right):
    return jnp.dot(left, right, preferred_element_type=f32)


def dot_rows(left, right):
    return lax.dot_general(left, right, (((0,), (0,)), ((), ())), preferred_element_type=f32)


def dot_columns(left, right):
    return lax.dot_general(left, right, (((1,), (1,)), ((), ())), preferred_element_type=f32)


def split_codes(codes):
    parts = jnp.concatenate([codes >> LANE_BITS, codes & (LANES - 1)], axis=0).astype(bf16)
    return jnp.concatenate([parts[:, :LANES], parts[:, LANES:]], axis=0)


def table_kernel(codes_ref, table_ref, keys, lows, *, fan, slot_bits, member_bits, by_rows):
    batch_rows = BATCH // fan
    batches = keys.shape[0]
    groups = table_ref.shape[1] // LANES
    mine = lax.axis_index("rep")
    row_id = lax.broadcasted_iota(jnp.int32, (groups * batch_rows, BATCH), 0).astype(bf16)
    lane_id = lax.broadcasted_iota(jnp.int32, (LANES, BATCH), 0).astype(bf16)
    one, zero = jnp.ones((), bf16), jnp.zeros((), bf16)
    group_bits = slot_bits - LANE_BITS
    for half in range(2):
        columns = slice(half * LANES, (half + 1) * LANES)
        start = half * 2 * batches
        upper = codes_ref[start : start + batches].astype(f32).astype(jnp.int32)
        if by_rows is not None:
            inside = (upper >> (member_bits + group_bits)) == by_rows
            group = (upper & ((1 << (member_bits + group_bits)) - 1)) ^ (mine << group_bits)
        else:
            inside = ((upper >> group_bits) & ((1 << member_bits) - 1)) == mine
            group = ((upper >> (member_bits + group_bits)) << group_bits) | (upper & ((1 << group_bits) - 1))
        row = (lax.broadcasted_iota(jnp.int32, upper.shape, 1) + half * LANES) // fan
        keys[:, columns] = jnp.where(inside & (upper >= 0), group * batch_rows + row, -1).astype(f32)
        lows[:, columns] = codes_ref[start + batches : start + 2 * batches].astype(f32)

    def step(batch, carry):
        left = jnp.where(keys[pl.ds(batch, 1), :].astype(bf16) == row_id, one, zero)
        right = jnp.where(lows[pl.ds(batch, 1), :].astype(bf16) == lane_id, one, zero)
        counts = dot_columns(left, right).astype(bf16)
        at = pl.ds(pl.multiple_of(batch * batch_rows, batch_rows), batch_rows)
        for group in range(groups):
            table_ref[at, group * LANES : (group + 1) * LANES] = counts[
                group * batch_rows : (group + 1) * batch_rows
            ]
        return carry

    lax.fori_loop(0, batches, step, 0, unroll=min(16, batches))


def build_table(codes, by_rows, slots, members, fan):
    batches = codes.shape[0] // 4
    columns = (3 if by_rows is None else members) * slots
    return kernel_call(
        functools.partial(
            table_kernel,
            fan=fan,
            slot_bits=slots.bit_length() - 1,
            member_bits=members.bit_length() - 1,
            by_rows=by_rows,
        ),
        "column_table" if by_rows is None else "row_table",
        jax.ShapeDtypeStruct((batches * (BATCH // fan), columns), bf16),
        (codes,),
        (pltpu.VMEM((batches, BATCH), f32), pltpu.VMEM((batches, BATCH), f32)),
    )


def products_kernel(*refs, tables, plan, transposed):
    outs = {entry[0] for entry in plan}
    given, outs = refs[: -len(outs)], refs[-len(outs) :]
    multiply = dot_rows if transposed else dot
    rows = given[-1].shape[0]
    for out, place, terms in plan:
        total = None
        for table, columns, operand in terms:
            one = multiply(given[table][:, columns * rows : (columns + 1) * rows], given[tables + operand][...])
            total = one if total is None else total + one
        outs[out][place * rows : (place + 1) * rows] = total.astype(outs[out].dtype)


def products(name, tables, operands, plan, kinds, transposed):
    rows, width = operands[0].shape
    sizes = [1 + max(place for out, place, _ in plan if out == at) for at in range(len(kinds))]
    outs = kernel_call(
        functools.partial(products_kernel, tables=len(tables), plan=plan, transposed=transposed),
        name,
        tuple(jax.ShapeDtypeStruct((size * rows, width), kind) for size, kind in zip(sizes, kinds)),
        (*tables, *operands),
    )
    return outs if len(kinds) > 1 else outs[0]


def nodes_first_products(column_tables, row_tables, around, members, transposed, after=()):
    sums = []
    for odd, kinds in ((1, (bf16,)), (0, (f32, f32))):
        if not odd and after:
            around = tied(*around, *after)[: len(around)]
        blocks = range(odd, members, 2)
        put = [(0, at) if odd or at == 0 else (1, at - 1) for at in range(len(blocks))]
        if transposed:
            tables = row_tables
            plan = [(*to, [(p, block, p) for p in range(3)]) for to, block in zip(put, blocks)]
        else:
            tables = [column_tables[block] for block in blocks]
            plan = [(*to, [(at, p, p) for p in range(3)]) for at, to in enumerate(put)]
        sums.append(products("nodes_first", tables, around, plan, kinds, transposed))
    return sums[1][0], sums[1][1], sums[0]


def rep_first_products(column_tables, row_tables, blocks, transposed):
    def product(places, blocks):
        kinds = tuple(f32 if place == 1 else bf16 for place in places)
        if transposed:
            tables = column_tables
            plan = [(out, 0, [(at, place, at) for at in range(len(blocks))]) for out, place in enumerate(places)]
        else:
            tables = [row_tables[place] for place in places]
            plan = [(out, 0, [(out, at, at) for at in range(len(blocks))]) for out in range(len(places))]
        return products("rep_first", tables, blocks, plan, kinds, transposed)

    to_far = product((2,), blocks)
    to_partner = product((0,), blocks)
    mine = product((1,), blocks)
    return to_partner, mine, to_far


def added_over_group(mine, kept, sent, later=None, after=None):
    rows = mine.shape[0]
    bits = bits_of("rep")
    terms = []
    for bit in bits[:-1]:
        received = swap(sent, "rep", bit)
        terms.append(received[:rows])
        left = kept.shape[0] // rows
        rest = [
            kept[i * rows : (i + 1) * rows] + received[(i + 1) * rows : (i + 2) * rows].astype(f32)
            for i in range(left)
        ]
        sent = jnp.concatenate(rest[0::2], axis=0).astype(bf16)
        kept = jnp.concatenate(rest[1::2], axis=0) if left > 1 else kept[:0]
    given = []
    if later is not None:
        work, *given = later
        given = work(*[tied(sent, array)[1] for array in given])
    if after is not None:
        given = [*given, *after(sent)]
    last, *given = tied(swap(sent, "rep", bits[-1]), *given)
    return sum([term.astype(f32) for term in terms + [last]], mine), given


def over_group(own):
    blocks = [own]
    for bit in reversed(bits_of("rep")):
        blocks = [part for block in blocks for part in (block, swap(block, "rep", bit))]
    return blocks


def exchanged(array, column_tables, row_tables, transposed, pair=None, early=False):
    one, other = halves(array)
    blocks = over_group(other)
    partner, own, far = around_of(one)
    far, partner, blocks[1] = tied(far, partner, blocks[1])
    if early:
        partner, own_table, far_table = tied(partner, *row_tables[1:])
        row_tables = [row_tables[0], own_table, far_table]
    to_partner, mine, to_far = rep_first_products(column_tables, row_tables, blocks, transposed)
    from_far = other_side(to_far)
    from_partner = swap(to_partner, "nodes", 1)
    one = nodes_first_products(column_tables, row_tables, (partner, own, far), len(blocks), transposed)
    one, made = added_over_group(*one, after=lambda sent: (*(() if pair is None else (dot_rows(*tied(*pair, sent)[:2]),)),))
    other = mine + from_partner.astype(f32) + from_far.astype(f32)
    return jnp.concatenate([one, other], axis=1), made


def tied(*arrays):
    return lax.optimization_barrier(arrays)


def halves(array):
    half = array.shape[1] // 2
    return array[:, :half], array[:, half:]


def kernel_call(body, name, out_shape, operands, scratch=(), given=VMEM):
    many = isinstance(out_shape, tuple)
    return pl.pallas_call(
        body,
        out_shape=out_shape,
        in_specs=[given] * len(operands),
        out_specs=(VMEM,) * len(out_shape) if many else VMEM,
        scratch_shapes=list(scratch),
        compiler_params=pltpu.CompilerParams(vmem_limit_bytes=VMEM_LIMIT),
        name=name,
    )(*operands)


def pack_kernel(*refs):
    given, (packed, tail), held, done = refs[:4], refs[5:7], refs[7:11], refs[11]
    copies = [pltpu.make_async_copy(given[at], held[at], done.at[at]) for at in range(4)]
    for copy in copies:
        copy.start()
    for copy in copies:
        copy.wait()
    encoder, layers, head, biases = held
    encoder_rows, layer_rows, rows = encoder.shape[0], layers.shape[1], head.shape[0]
    tail[...] = jnp.zeros_like(tail)
    tail[:, : head.shape[1]] = head[...]
    tail[: biases.shape[0], PAD_AT : PAD_AT + biases.shape[1]] = biases[...]
    for odd in range(2):

        @pl.when((lax.axis_index("rep") & 1) == odd)
        def _(columns=slice(odd * LANES, (odd + 1) * LANES), half=slice(odd * rows // 2, (odd + 1) * rows // 2)):
            packed[:encoder_rows] = encoder[:, columns].astype(bf16)
            for layer in range(LAYERS):
                start = encoder_rows + layer * layer_rows
                packed[start : start + layer_rows] = layers[layer, :, columns].astype(bf16)
            packed[encoder_rows + LAYERS * layer_rows :] = tail[half].astype(bf16)


def assemble_kernel(mine, theirs, *outs, sizes, order):
    for odd in range(2):

        @pl.when((lax.axis_index("rep") & 1) == odd)
        def _(low=(mine, theirs)[odd], high=(theirs, mine)[odd]):
            bias_total = None
            for shard in range(mine.shape[0]):
                node = lax.axis_index("nodes") ^ order[shard]
                start = 0
                for out, rows in zip(outs, sizes):
                    at = pl.ds(pl.multiple_of(node * rows, rows), rows)
                    part = slice(start, start + rows)
                    out[at, :LANES] = low[shard, part]
                    out[at, LANES:] = high[shard, part]
                    start += rows
                if len(outs) == len(sizes):
                    continue
                head, bias_rows = outs[len(sizes) :]
                rows = head.shape[0] // mine.shape[0]
                half = rows // 2
                at = pl.multiple_of(node * rows, rows)
                head[pl.ds(at, half)] = low[shard, start:]
                head[pl.ds(pl.multiple_of(at + half, half), half)] = high[shard, start:]
                columns = bias_rows.shape[1] // mine.shape[0]
                bias = low[shard, start:].astype(f32)
                if half < 8:
                    bias = jnp.concatenate([bias, high[shard, start:].astype(f32)], axis=0)
                bias = bias[: bias_rows.shape[0]]
                lane = lax.broadcasted_iota(jnp.int32, bias.shape, 1)
                bias = jnp.where((lane >= PAD_AT) & (lane < PAD_AT + columns), bias, 0.0)
                wide = jnp.concatenate([bias, jnp.zeros_like(bias)], axis=1)
                wide = pltpu.roll(wide, (node * columns + bias_rows.shape[1] - PAD_AT) % bias_rows.shape[1], 1)
                bias_total = wide if bias_total is None else bias_total + wide
            if bias_total is not None:
                outs[-1][...] = bias_total


def gradient_kernel(
    rounded, averaged, low_grad, features, means, low_self, low_mean, *refs, groups
):
    *others, head, away, kept, encoder_grad, layer_grad = refs
    width = low_grad.shape[1]
    encoder_grad[...] = dot_rows(features[...], low_self[...]) + dot_rows(means[...], low_mean[...])
    layer_grad[:width] = dot_rows(rounded[...], low_grad[...])
    layer_grad[width:] = dot_rows(averaged[...], low_grad[...])
    sources = [encoder_grad, layer_grad] + list(others)
    for odd in range(2):

        @pl.when((lax.axis_index("rep") & 1) == odd)
        def _(odd=odd):
            mine = slice(odd * LANES, (odd + 1) * LANES)
            other = slice((1 - odd) * LANES, (2 - odd) * LANES)
            for node in range(groups):
                start = 0
                for source in sources:
                    rows = source.shape[0] // groups
                    at, put = slice(node * rows, (node + 1) * rows), slice(start, start + rows)
                    kept[node, put] = source[at, mine]
                    away[node, put] = source[at, other].astype(bf16)
                    start += rows
                half = head.shape[0] // groups // 2
                low, high = (2 * node + odd) * half, (2 * node + 1 - odd) * half
                kept[node, start:] = head[low : low + half]
                away[node, start:] = head[high : high + half].astype(bf16)


def total_at(parts, *index):
    sums = [part[index].astype(f32) for part in parts]
    while len(sums) > 1:
        sums = [one + other for one, other in zip(sums[0::2], sums[1::2])]
    return sums[0]


def first_cut_kernel(kept, received, own, *sent):
    half = own.shape[1]
    for place in range(own.shape[0]):
        for mask, out in enumerate((own, *sent)):
            node = 2 * place + ((lax.axis_index("nodes") & 1) ^ (mask & 1))
            rows = ((lax.axis_index("rep") >> 1) & 1) ^ (mask >> 1)
            rows = pl.ds(pl.multiple_of(rows * half, half), half)
            out[place] = total_at((kept, received), node, rows).astype(out.dtype)


def cut_kernel(*refs, count, bit, ways):
    parts, outs = refs[:count], refs[count:]
    mine = lax.axis_index("nodes") // bit & (ways - 1)
    for place in range(outs[0].shape[0]):
        for mask, out in enumerate(outs):
            out[place] = total_at(parts, ways * place + (mine ^ mask)).astype(out.dtype)


def last_kernel(own, received, sums, other_sums, out):
    owners, rows = own.shape[:2]
    mine = lax.axis_index("nodes") // (lax.axis_size("nodes") // owners)
    out[:rows] = total_at((own, received), mine)
    squares = None
    for owner in range(owners):
        grad = total_at((own, received), owner)
        one = jnp.sum((grad * grad).reshape(rows // 8, 8, LANES), axis=0)
        squares = one if squares is None else squares + one
    out[rows : rows + 8] = squares
    out[rows + 8 :] = sums[...] + other_sums[...]


def update_kernel(*refs):
    (mine_ref, theirs), rest = refs[:2], refs[2:]
    params, firsts, seconds = rest[:5], rest[5:10], rest[10:15]
    updated, drifts, spreads, copied = rest[15:20], rest[20:25], rest[25:30], rest[30:34]
    loss_ref, count_ref, norm_ref, grad = rest[34:]
    quarter = (mine_ref.shape[0] - 24) // 2
    tile = mine_ref[2 * quarter :] + theirs[2 * quarter :]
    high, odd = (lax.axis_index("rep") >> 1) & 1, lax.axis_index("rep") & 1
    upper = pl.multiple_of(high * quarter, quarter)
    lower = pl.multiple_of((1 - high) * quarter, quarter)
    mine = pl.ds(pl.multiple_of(odd * LANES, LANES), LANES)
    other = pl.ds(pl.multiple_of((1 - odd) * LANES, LANES), LANES)
    grad[pl.ds(upper, quarter), mine] = mine_ref[:quarter]
    grad[pl.ds(lower, quarter), mine] = mine_ref[quarter : 2 * quarter]
    grad[pl.ds(upper, quarter), other] = theirs[:quarter]
    grad[pl.ds(lower, quarter), other] = theirs[quarter : 2 * quarter]

    classes = params[4].shape[1]
    lane = lax.broadcasted_iota(jnp.int32, (1, LANES), 1)
    class_row = tile[8:9]
    class_grad = jnp.where(lane < classes, class_row, 0.0)
    bias_low, bias_high = tile[16:20], tile[20:24]
    squares = (
        jnp.sum(tile[:8], keepdims=True)
        + jnp.sum(class_grad * class_grad, keepdims=True)
        + jnp.sum(bias_low * bias_low, keepdims=True)
        + jnp.sum(bias_high * bias_high, keepdims=True)
    )
    norm = jnp.sqrt(squares)
    scale = jnp.minimum(1.0, 1.0 / (norm + 1e-06))
    loss_ref[...] = jnp.sum(jnp.where(lane == classes, class_row, 0.0), axis=1, keepdims=True)
    count_ref[...] = jnp.sum(jnp.where(lane == classes + 1, class_row, 0.0), axis=1, keepdims=True)
    norm_ref[...] = norm

    encoder_rows, layer_rows = params[0].shape[0], params[1].shape[1]
    ends = encoder_rows + LAYERS * layer_rows
    head_half = params[2].shape[0] // 2
    columns = params[3].shape[1]
    width = 2 * LANES
    biases = jnp.concatenate([bias_low, bias_high], axis=1)
    biases = pltpu.roll(biases, (width - lax.axis_index("nodes") * columns) % width, 1)[:, :columns]

    def step(index, at, gradient):
        new, drift, spread = adamw(params[index][at], firsts[index][at], seconds[index][at], gradient, scale)
        updated[index][at] = new
        drifts[index][at] = drift
        spreads[index][at] = spread
        if index < 4:
            copied[index][at] = new.astype(bf16)

    step(0, slice(None), grad[:encoder_rows])
    for layer in range(LAYERS):
        start = encoder_rows + layer * layer_rows
        step(1, layer, grad[start : start + layer_rows])
    step(2, slice(0, head_half), grad[ends:, :LANES][:, :classes])
    step(2, slice(head_half, 2 * head_half), grad[ends:, LANES:][:, :classes])
    step(3, slice(None), biases)
    step(4, slice(None), class_grad[:, :classes])


def adamw(weight, first, second, grad, scale):
    scaled = grad * scale
    drift = beta_one * first + (1.0 - beta_one) * scaled
    spread = beta_two * second + (1.0 - beta_two) * scaled * scaled
    corrected = drift / (1.0 - beta_one**STEP)
    denominator = jnp.sqrt(spread / (1.0 - beta_two**STEP)) + epsilon
    return (weight - rate * (corrected / denominator + decay * weight), drift, spread)


def plain_pack(encoder, layers, head, biases):
    head = jnp.pad(head, ((0, 0), (0, PAD_AT - head.shape[1])))
    bias = jnp.pad(biases, ((0, head.shape[0] - biases.shape[0]), (0, LANES - PAD_AT - biases.shape[1])))
    tail = jnp.concatenate([head, bias], axis=1)
    half = tail.shape[0] // 2
    tail = jnp.concatenate([tail[:half], tail[half:]], axis=1)
    odd = (lax.axis_index("rep") & 1) == 1
    rows = jnp.concatenate([encoder, *layers, tail], axis=0)
    return jnp.where(odd, rows[:, LANES:], rows[:, :LANES]).astype(bf16)


def plain_assemble(mine, theirs, order, sizes):
    places = [0] * len(order)
    for place, node in enumerate(order):
        places[node] = place
    places = jnp.asarray(places)[lax.axis_index("nodes") ^ jnp.arange(len(order))]
    mine, theirs = jnp.take(mine, places, axis=0), jnp.take(theirs, places, axis=0)
    odd = (lax.axis_index("rep") & 1) == 1
    rows = jnp.concatenate([jnp.where(odd, theirs, mine), jnp.where(odd, mine, theirs)], axis=2)
    outs, start = [], 0
    for size in sizes:
        outs.append(rows[:, start : start + size].reshape(-1, rows.shape[2]))
        start += size
    if start < rows.shape[1]:
        tail = rows[:, start:]
        tail = jnp.concatenate([tail[..., :LANES], tail[..., LANES:]], axis=1)
        columns = rows.shape[2] // len(order)
        bias = tail[:, : LAYERS + 1, PAD_AT : PAD_AT + columns].astype(f32)
        outs += [tail.reshape(-1, LANES), jnp.swapaxes(bias, 0, 1).reshape(LAYERS + 1, rows.shape[2])]
    return outs


def plain_gradients(rounded, averaged, low_grad, features, means, low_self, low_mean, *rest, groups):
    *others, head = rest
    encoder = dot_rows(features, low_self) + dot_rows(means, low_mean)
    layer = jnp.concatenate([dot_rows(rounded, low_grad), dot_rows(averaged, low_grad)], axis=0)
    parts = [part.reshape(groups, -1, part.shape[1]) for part in (encoder, layer, *others, head)]
    half = parts[-1].shape[1] // 2
    parts[-1] = jnp.concatenate([parts[-1][:, :half], parts[-1][:, half:]], axis=2)
    rows = jnp.concatenate(parts, axis=1)
    odd = (lax.axis_index("rep") & 1) == 1
    low, high = rows[..., :LANES], rows[..., LANES:]
    return jnp.where(odd, low, high).astype(bf16), jnp.where(odd, high, low)


def plain_first_cut(kept, received):
    total = kept + received.astype(f32)
    half = total.shape[1] // 2
    total = total.reshape(total.shape[0] // 2, 2, 2, half, LANES)
    outs = []
    for mask in range(4):
        node = (lax.axis_index("nodes") & 1) ^ (mask & 1)
        rows = ((lax.axis_index("rep") >> 1) & 1) ^ (mask >> 1)
        part = lax.dynamic_slice(total, (0, node, rows, 0, 0), (total.shape[0], 1, 1, half, LANES))
        outs.append(part.reshape(-1, half, LANES).astype(bf16 if mask else f32))
    return outs


def plain_last(own, received, sums, other_sums):
    grad = own.astype(f32) + received.astype(f32)
    squares = jnp.pad(jnp.sum(grad * grad, axis=(0, 1))[None], ((0, 7), (0, 0)))
    mine = lax.axis_index("nodes") // (lax.axis_size("nodes") // own.shape[0])
    grad = lax.dynamic_index_in_dim(grad, mine, 0, keepdims=False)
    return jnp.concatenate([grad, squares, sums + other_sums], axis=0)


def plain_update(mine, theirs, *rest):
    params, firsts, seconds = rest[:5], rest[5:10], rest[10:15]
    quarter = (mine.shape[0] - 24) // 2
    tile = mine[2 * quarter :] + theirs[2 * quarter :]
    high, odd = (lax.axis_index("rep") >> 1) & 1 == 1, lax.axis_index("rep") & 1 == 1
    sides = []
    for part in (mine, theirs):
        one, other = part[:quarter], part[quarter : 2 * quarter]
        sides.append(jnp.concatenate([jnp.where(high, other, one), jnp.where(high, one, other)], axis=0))
    rows = jnp.concatenate([jnp.where(odd, *sides[::-1]), jnp.where(odd, *sides)], axis=1)
    classes = params[4].shape[1]
    class_grad = tile[8:9, :classes]
    biases = jnp.concatenate([tile[16:20], tile[20:24]], axis=1)
    norm = jnp.sqrt(jnp.sum(tile[:8]) + jnp.sum(class_grad * class_grad) + jnp.sum(biases * biases))
    scale = jnp.minimum(1.0, 1.0 / (norm + 1e-06))
    encoder_rows, layer_rows = params[0].shape[0], params[1].shape[1]
    ends = encoder_rows + LAYERS * layer_rows
    columns = params[3].shape[1]
    grads = (
        rows[:encoder_rows],
        rows[encoder_rows:ends].reshape(LAYERS, layer_rows, -1),
        jnp.concatenate([rows[ends:, :LANES], rows[ends:, LANES:]], axis=0)[:, :classes],
        lax.dynamic_slice_in_dim(biases, lax.axis_index("nodes") * columns, columns, axis=1),
        class_grad,
    )
    results = [adamw(params[at], firsts[at], seconds[at], grads[at], scale) for at in range(5)]
    new = [entry[0] for entry in results]
    scalars = (tile[8, classes], tile[8, classes + 1], norm)
    return (
        *new, *[entry[1] for entry in results], *[entry[2] for entry in results],
        *[entry.astype(bf16) for entry in new[:4]], *scalars,
    )


def per_device(
    features,
    node_count,
    neighbours,
    neighbour_count,
    label_mask,
    labels,
    encoder_weight,
    layer_weights,
    head_weight,
    biases,
    class_bias,
    mean_encoder,
    mean_layers,
    mean_head,
    mean_biases,
    mean_class,
    square_encoder,
    square_layers,
    square_head,
    square_biases,
    square_class,
):
    node_rows = features.shape[0]
    fan = neighbours.shape[1]
    width = encoder_weight.shape[1]
    classes = class_bias.shape[0]
    groups = lax.axis_size("nodes")
    copies = lax.axis_size("rep")
    here_node = lax.axis_index("nodes")
    member = lax.axis_index("rep")
    encoder_rows, layer_rows, bias_columns = (
        encoder_weight.shape[0],
        layer_weights.shape[1],
        biases.shape[1],
    )

    owner = jnp.floor_divide(neighbours, node_rows)
    group = jnp.floor_divide(owner, copies)
    offset = jnp.where(group == here_node, 1, jnp.where(group == here_node ^ 1, 0, 2))
    codes = (offset * copies + jnp.mod(owner, copies)) * node_rows + jnp.mod(neighbours, node_rows)
    edge_live = lax.broadcasted_iota(jnp.int32, neighbours.shape, 1) < neighbour_count[:, None]
    codes = jnp.where(edge_live, codes, -1).reshape(node_rows * fan // BATCH, BATCH)
    codes = split_codes(codes)
    to_around = jnp.concatenate([features, codes], axis=0)
    partner, _, other = around_of(to_around)
    blocks = [codes]
    for bit in bits_of("rep"):
        blocks = blocks + [swap(block, "rep", bit) for block in blocks]
    second = build_table(blocks[1], None, node_rows, copies, fan)
    partner, other, second, *blocks[2:] = tied(partner, other, second, *blocks[2:])
    column_tables = [
        second if block is blocks[1] else build_table(block, None, node_rows, copies, fan) for block in blocks
    ]

    head_rows = head_weight.shape[0]
    aligned = encoder_rows % 16 == 0 and layer_rows % 16 == 0 and head_rows % 32 == 0
    rows = encoder_rows + LAYERS * layer_rows + head_rows // 2
    weights = (encoder_weight, layer_weights, head_weight, biases)
    in_hbm = [pltpu.with_memory_space_constraint(weight, pltpu.HBM) for weight in weights] if aligned else []
    own_weights = plain_pack(*weights) if not aligned else kernel_call(
        pack_kernel,
        "pack_weights",
        jax.ShapeDtypeStruct((rows, LANES), bf16),
        (*in_hbm, codes),
        (
            pltpu.VMEM((head_rows, LANES), f32),
            *[pltpu.VMEM(weight.shape, f32) for weight in weights],
            pltpu.SemaphoreType.DMA((4,)),
        ),
        pl.BlockSpec(memory_space=pltpu.HBM),
    )
    def over_nodes(part, beside):
        part, order = part[None], [0]
        for bit in bits_of("nodes")[::-1]:
            part = jnp.concatenate([part, swap(part, "nodes", bit)], axis=0)
            order = order + [node ^ bit for node in order]
            if beside:
                part, _ = tied(part, beside[0])
                beside = beside[1:]
        return part, order

    own_weights, order = over_nodes(own_weights, column_tables[:2])
    *feature_products, sent = nodes_first_products(
        column_tables, None, (partner[:node_rows], features, other[:node_rows]), copies, False
    )
    local_rows = lax.broadcasted_iota(jnp.int32, (node_rows,), 0)
    valid_node = (local_rows < node_count[0]).astype(f32)[:, None]
    inverse_count = (1.0 / neighbour_count.astype(f32))[:, None]
    weight_mask = label_mask.astype(f32)[:, None] * valid_node

    def meanwhile(partner, other, held):
        return (
            build_table(partner, 0, node_rows, copies, fan),
            other,
            held,
            swap(held, "rep", 1),
        )

    feature_sums, (*row_tables, mine, theirs) = added_over_group(
        *feature_products, sent, (meanwhile, partner[node_rows:], other[node_rows:], own_weights)
    )
    row_tables = [row_tables[0], *[build_table(block, place, node_rows, copies, fan) for place, block in ((1, codes), (2, row_tables[1]))]]
    gathered = (mine, theirs)
    sizes = (encoder_rows,) + (layer_rows,) * LAYERS
    encoder, *layers, head, bias_rows = plain_assemble(*gathered, order, sizes) if not aligned else kernel_call(
        functools.partial(assemble_kernel, sizes=sizes, order=order),
        "assemble_weights",
        tuple(jax.ShapeDtypeStruct((groups * size, width), bf16) for size in sizes)
        + (
            jax.ShapeDtypeStruct((groups * head_rows, LANES), bf16),
            jax.ShapeDtypeStruct((min(8, head_rows), width), f32),
        ),
        gathered,
    )
    feature_mean = (feature_sums * inverse_count).astype(bf16)

    rounded = ((dot(features, encoder) + bias_rows[0:1]) * valid_node).astype(bf16)
    averaged = (dot(feature_mean, encoder) + bias_rows[0:1]).astype(bf16)
    low_self_input = (rounded, averaged)
    kept_joined = []
    kept_before = []
    for layer in range(LAYERS):
        if layer > 0:
            sums, _ = exchanged(rounded, column_tables, row_tables, False, early=layer == 1)
            averaged = (sums * inverse_count).astype(bf16)
        joined = jnp.concatenate([rounded, averaged], axis=1)
        before = dot(joined, layers[layer]) + bias_rows[layer + 1 : layer + 2]
        kept_joined.append(joined)
        kept_before.append(before)
        rounded = act_norm(before).astype(bf16)

    class_ids = lax.broadcasted_iota(jnp.int32, (1, LANES), 1)
    padded_bias = jnp.pad(class_bias, (0, LANES - classes))
    logits = jnp.where(class_ids < classes, dot(rounded, head) + padded_bias, -1e30)
    total_exp = jax.nn.logsumexp(logits, axis=1, keepdims=True)
    target = (class_ids == labels[:, None]).astype(f32)
    picked = jnp.sum(logits * target, axis=1, keepdims=True)
    grad_logits = (jnp.exp(logits - total_exp) - target) * weight_mask
    sums = jnp.where(class_ids == classes, weight_mask * (total_exp - picked), grad_logits)
    sums = jnp.where(class_ids == classes + 1, weight_mask, sums)
    class_tile = jnp.sum(sums, axis=0, keepdims=True)
    low_logits = grad_logits.astype(bf16)
    grad_head = dot_rows(rounded, low_logits)
    grad_hidden = dot_columns(low_logits, head)

    grad_weights = [None] * LAYERS
    grad_bias_rows = [None] * (LAYERS + 1)
    for layer in reversed(range(LAYERS)):
        _, pullback = jax.vjp(act_norm, kept_before[layer])
        grad_before = pullback(grad_hidden)[0]
        grad_bias_rows[layer + 1] = jnp.sum(grad_before, axis=0, keepdims=True)
        low_grad = grad_before.astype(bf16)
        grad_joined = dot_columns(low_grad, layers[layer])
        grad_self, grad_mean = halves(grad_joined)
        if layer > 0:
            low_grad_sum = (grad_mean * inverse_count).astype(bf16)
            received, (grad_weights[layer],) = exchanged(
                low_grad_sum, column_tables, row_tables, True, (kept_joined[layer], low_grad)
            )
            grad_hidden = grad_self + received
    grad_self = grad_self * valid_node
    grad_bias_rows[0] = jnp.sum(grad_self + grad_mean, axis=0, keepdims=True)
    inputs = (
        *low_self_input,
        low_grad,
        features,
        feature_mean,
        grad_self.astype(bf16),
        grad_mean.astype(bf16),
        *grad_weights[1:],
        grad_head,
    )
    away, grads = plain_gradients(*inputs, groups=groups) if not aligned else kernel_call(
        functools.partial(gradient_kernel, groups=groups),
        "gradients",
        (
            jax.ShapeDtypeStruct((groups, rows, LANES), bf16),
            jax.ShapeDtypeStruct((groups, rows, LANES), f32),
        ),
        inputs,
        (pltpu.VMEM((features.shape[1], width), f32), pltpu.VMEM((2 * width, width), f32)),
    )

    received = swap(away, "rep", 1)
    half = rows // 2
    own, *sent = plain_first_cut(grads, received) if not aligned else kernel_call(
        first_cut_kernel,
        "first_cut",
        tuple(jax.ShapeDtypeStruct((groups // 2, half, LANES), kind) for kind in (f32, bf16, bf16, bf16)),
        (grads, received),
    )
    received = [swap_both(part, mask & 1, (mask >> 1) * 2) for mask, part in enumerate(sent, 1)]
    *steps, last_step = bits_of("nodes")[1:]
    bias_grads = [row[:, side * LANES : (side + 1) * LANES] for side in range(2) for row in grad_bias_rows]
    sums = jnp.concatenate([jnp.broadcast_to(class_tile, (8, LANES)), *bias_grads], axis=0)
    other_sums = swap(sums, "nodes", last_step)
    received[0], other_sums = tied(received[0], other_sums)
    for bit in steps:
        parts = (own, *received)
        kinds = (f32, bf16)
        own, sent = kernel_call(
            functools.partial(cut_kernel, count=len(parts), bit=bit, ways=2),
            "cut",
            tuple(jax.ShapeDtypeStruct((own.shape[0] // 2, half, LANES), kind) for kind in kinds),
            parts,
        )
        received = (swap(sent, "nodes", bit),)
    own = total_at((own, *received), slice(None)).astype(bf16)
    received = swap(own, "nodes", last_step), sums, other_sums
    inputs = (own, *received)
    grads = plain_last(*inputs) if not aligned else pl.pallas_call(
        last_kernel,
        out_shape=jax.ShapeDtypeStruct((half + 24, LANES), f32),
        in_specs=[VMEM] * 4,
        out_specs=VMEM,
        compiler_params=pltpu.CompilerParams(vmem_limit_bytes=VMEM_LIMIT),
        name="last_sum",
    )(*inputs)

    tile = grads[half:]
    for bit in steps:
        tile = tile + swap(tile, "nodes", bit)
    across, other, both = (
        swap_both(tile, 1, 0),
        swap(jnp.concatenate([grads[:half], tile], axis=0), "rep", 2),
        swap_both(tile, 1, 2),
    )
    tile = total_at((tile, across, other[half:], both), slice(None))
    grads = jnp.concatenate([grads[:half], other[:half], tile], axis=0)
    received = swap(grads, "rep", 1)

    params = (encoder_weight, layer_weights, head_weight, biases, class_bias[None])
    firsts = (mean_encoder, mean_layers, mean_head, mean_biases, mean_class[None])
    seconds = (square_encoder, square_layers, square_head, square_biases, square_class[None])
    shapes = tuple(jax.ShapeDtypeStruct(param.shape, f32) for param in params)
    lows = tuple(jax.ShapeDtypeStruct(param.shape, bf16) for param in params[:4])
    inputs = (grads, received, *params, *firsts, *seconds)
    results = plain_update(*inputs) if not aligned else pl.pallas_call(
        update_kernel,
        out_shape=shapes * 3 + lows + (jax.ShapeDtypeStruct((1, 1), f32),) * 3,
        in_specs=[VMEM] * 17,
        out_specs=(VMEM,) * 22,
        scratch_shapes=[pltpu.VMEM((rows, width), f32)],
        compiler_params=pltpu.CompilerParams(vmem_limit_bytes=VMEM_LIMIT),
        name="adamw",
    )(*inputs)
    results, scalars = list(results[:19]), results[19:]
    for index in (4, 9, 14):
        results[index] = results[index][0]
    return tuple(results) + tuple(scalar.reshape(()) for scalar in scalars)


def solution(mesh):
    node_arrays = (
        P(("nodes", "rep"), None),
        P(("nodes", "rep")),
        P(("nodes", "rep"), None),
        P(("nodes", "rep")),
        P(("nodes", "rep")),
        P(("nodes", "rep")),
    )
    weights = (P("nodes", None), P(None, "nodes", None), P("nodes", None), P(None, "nodes"), P())
    return jax.shard_map(
        per_device,
        mesh=mesh,
        in_specs=node_arrays + weights * 3,
        out_specs=weights * 3 + weights[:4] + (P(), P(), P()),
        check_vma=False,
    )
```

```python
import functools

import jax
import jax.numpy as jnp
from jax import lax
from jax.experimental import pallas as pl
from jax.experimental.pallas import tpu as pltpu
from jax.sharding import PartitionSpec as P

LAYERS = 3
STEP = 5

beta_one = 0.5
beta_two = 0.5
rate = 0.05
decay = 0.01
epsilon = 1e-08

LANES = 128
LANE_BITS = 7
BATCH = 256
PAD_AT = 64
VMEM_LIMIT = 14 << 20

bf16 = jnp.bfloat16
f32 = jnp.float32
VMEM = pl.BlockSpec(memory_space=pltpu.VMEM)


def swap(array, axis, mask):
    return lax.ppermute(array, axis, [(i, i ^ mask) for i in range(lax.axis_size(axis))])


def swap_both(array, node_mask, rep_mask):
    copies = lax.axis_size("rep")
    count = lax.axis_size("nodes") * copies
    mask = node_mask * copies + rep_mask
    return lax.ppermute(array, ("nodes", "rep"), [(i, i ^ mask) for i in range(count)])


def other_side(array):
    count = lax.axis_size("nodes")
    return lax.ppermute(array, "nodes", [(i, (i + (1 if i % 2 else -1)) % count) for i in range(count)])


def around_of(array):
    other = other_side(array)
    return swap(array, "nodes", 1), array, other


def bits_of(axis):
    return [1 << b for b in range(lax.axis_size(axis).bit_length() - 1)]


def masks_of(bits):
    masks = [0]
    for bit in bits:
        masks = masks + [mask | bit for mask in masks]
    return masks


def paired(bits):
    return [bits[at : at + 2] for at in range(0, len(bits), 2)]


def act_norm(before):
    active = jax.nn.gelu(before)
    return active * lax.rsqrt(jnp.mean(active * active, axis=-1, keepdims=True) + 1e-06)


def dot(left, right):
    return jnp.dot(left, right, preferred_element_type=f32)


def dot_rows(left, right):
    return lax.dot_general(left, right, (((0,), (0,)), ((), ())), preferred_element_type=f32)


def dot_columns(left, right):
    return lax.dot_general(left, right, (((1,), (1,)), ((), ())), preferred_element_type=f32)


def split_codes(codes):
    parts = jnp.concatenate([codes >> LANE_BITS, codes & (LANES - 1)], axis=0).astype(bf16)
    return jnp.concatenate([parts[:, :LANES], parts[:, LANES:]], axis=0)


def table_kernel(codes_ref, table_ref, keys, lows, *, fan, slot_bits, member_bits, by_rows):
    batch_rows = BATCH // fan
    batches = keys.shape[0]
    groups = table_ref.shape[1] // LANES
    mine = lax.axis_index("rep")
    row_id = lax.broadcasted_iota(jnp.int32, (groups * batch_rows, BATCH), 0).astype(bf16)
    lane_id = lax.broadcasted_iota(jnp.int32, (LANES, BATCH), 0).astype(bf16)
    one, zero = jnp.ones((), bf16), jnp.zeros((), bf16)
    group_bits = slot_bits - LANE_BITS
    for half in range(2):
        columns = slice(half * LANES, (half + 1) * LANES)
        start = half * 2 * batches
        upper = codes_ref[start : start + batches].astype(f32).astype(jnp.int32)
        if by_rows is not None:
            inside = (upper >> (member_bits + group_bits)) == by_rows
            group = (upper & ((1 << (member_bits + group_bits)) - 1)) ^ (mine << group_bits)
        else:
            inside = ((upper >> group_bits) & ((1 << member_bits) - 1)) == mine
            group = ((upper >> (member_bits + group_bits)) << group_bits) | (upper & ((1 << group_bits) - 1))
        row = (lax.broadcasted_iota(jnp.int32, upper.shape, 1) + half * LANES) // fan
        keys[:, columns] = jnp.where(inside & (upper >= 0), group * batch_rows + row, -1).astype(f32)
        lows[:, columns] = codes_ref[start + batches : start + 2 * batches].astype(f32)

    def step(batch, carry):
        left = jnp.where(keys[pl.ds(batch, 1), :].astype(bf16) == row_id, one, zero)
        right = jnp.where(lows[pl.ds(batch, 1), :].astype(bf16) == lane_id, one, zero)
        counts = dot_columns(left, right).astype(bf16)
        at = pl.ds(pl.multiple_of(batch * batch_rows, batch_rows), batch_rows)
        for group in range(groups):
            table_ref[at, group * LANES : (group + 1) * LANES] = counts[
                group * batch_rows : (group + 1) * batch_rows
            ]
        return carry

    lax.fori_loop(0, batches, step, 0, unroll=min(16, batches))


def build_table(codes, by_rows, slots, members, fan):
    batches = codes.shape[0] // 4
    columns = (3 if by_rows is None else members) * slots
    return kernel_call(
        functools.partial(
            table_kernel,
            fan=fan,
            slot_bits=slots.bit_length() - 1,
            member_bits=members.bit_length() - 1,
            by_rows=by_rows,
        ),
        "column_table" if by_rows is None else "row_table",
        jax.ShapeDtypeStruct((batches * (BATCH // fan), columns), bf16),
        (codes,),
        (pltpu.VMEM((batches, BATCH), f32), pltpu.VMEM((batches, BATCH), f32)),
    )


def products_kernel(*refs, tables, plan, transposed):
    outs = {entry[0] for entry in plan}
    given, outs = refs[: -len(outs)], refs[-len(outs) :]
    multiply = dot_rows if transposed else dot
    rows = given[-1].shape[0]
    for out, place, terms in plan:
        total = None
        for table, columns, operand in terms:
            one = multiply(given[table][:, columns * rows : (columns + 1) * rows], given[tables + operand][...])
            total = one if total is None else total + one
        outs[out][place * rows : (place + 1) * rows] = total.astype(outs[out].dtype)


def products(name, tables, operands, plan, kinds, transposed):
    rows, width = operands[0].shape
    sizes = [1 + max(place for out, place, _ in plan if out == at) for at in range(len(kinds))]
    outs = kernel_call(
        functools.partial(products_kernel, tables=len(tables), plan=plan, transposed=transposed),
        name,
        tuple(jax.ShapeDtypeStruct((size * rows, width), kind) for size, kind in zip(sizes, kinds)),
        (*tables, *operands),
    )
    return outs if len(kinds) > 1 else outs[0]


def nodes_first_products(column_tables, row_tables, around, members, transposed, after=()):
    sums = []
    for odd, kinds in ((1, (bf16,)), (0, (f32, f32))):
        if not odd and after:
            around = tied(*around, *after)[: len(around)]
        blocks = range(odd, members, 2)
        put = [(0, at) if odd or at == 0 else (1, at - 1) for at in range(len(blocks))]
        if transposed:
            tables = row_tables
            plan = [(*to, [(p, block, p) for p in range(3)]) for to, block in zip(put, blocks)]
        else:
            tables = [column_tables[block] for block in blocks]
            plan = [(*to, [(at, p, p) for p in range(3)]) for at, to in enumerate(put)]
        sums.append(products("nodes_first", tables, around, plan, kinds, transposed))
    return sums[1][0], sums[1][1], sums[0]


def rep_first_products(column_tables, row_tables, blocks, transposed):
    def product(places, blocks):
        kinds = tuple(f32 if place == 1 else bf16 for place in places)
        if transposed:
            tables = column_tables
            plan = [(out, 0, [(at, place, at) for at in range(len(blocks))]) for out, place in enumerate(places)]
        else:
            tables = [row_tables[place] for place in places]
            plan = [(out, 0, [(out, at, at) for at in range(len(blocks))]) for out in range(len(places))]
        return products("rep_first", tables, blocks, plan, kinds, transposed)

    to_far = product((2,), blocks)
    to_partner = product((0,), blocks)
    mine = product((1,), blocks)
    return to_partner, mine, to_far


def added_over_group(mine, kept, sent, later=None, after=None):
    rows = mine.shape[0]
    bits = bits_of("rep")
    terms = []
    for bit in bits[:-1]:
        received = swap(sent, "rep", bit)
        terms.append(received[:rows])
        left = kept.shape[0] // rows
        rest = [
            kept[i * rows : (i + 1) * rows] + received[(i + 1) * rows : (i + 2) * rows].astype(f32)
            for i in range(left)
        ]
        sent = jnp.concatenate(rest[0::2], axis=0).astype(bf16)
        kept = jnp.concatenate(rest[1::2], axis=0) if left > 1 else kept[:0]
    given = []
    if later is not None:
        work, *given = later
        given = work(*[tied(sent, array)[1] for array in given])
    if after is not None:
        given = [*given, *after(sent)]
    last, *given = tied(swap(sent, "rep", bits[-1]), *given)
    return sum([term.astype(f32) for term in terms + [last]], mine), given


def over_group(own):
    blocks = [own]
    for bit in reversed(bits_of("rep")):
        blocks = [part for block in blocks for part in (block, swap(block, "rep", bit))]
    return blocks


def exchanged(array, column_tables, row_tables, transposed, pair=None, early=()):
    one, other = halves(array)
    blocks = over_group(other)
    partner, own, far = around_of(one)
    far, partner, blocks[1] = tied(far, partner, blocks[1])
    if early:
        partner, own_table, far_table, *early = tied(partner, *row_tables[1:], *early)
        row_tables = [row_tables[0], own_table, far_table]
    to_partner, mine, to_far = rep_first_products(column_tables, row_tables, blocks, transposed)
    from_far = other_side(to_far)
    from_partner = swap(to_partner, "nodes", 1)
    one = nodes_first_products(column_tables, row_tables, (partner, own, far), len(blocks), transposed)
    one, made = added_over_group(*one, after=lambda sent: (*(() if pair is None else (dot_rows(*tied(*pair, sent)[:2]),)),))
    other = mine + from_partner.astype(f32) + from_far.astype(f32)
    return jnp.concatenate([one, other], axis=1), early or made


def tied(*arrays):
    return lax.optimization_barrier(arrays)


def halves(array):
    half = array.shape[1] // 2
    return array[:, :half], array[:, half:]


def kernel_call(body, name, out_shape, operands, scratch=(), given=VMEM):
    many = isinstance(out_shape, tuple)
    return pl.pallas_call(
        body,
        out_shape=out_shape,
        in_specs=[given] * len(operands),
        out_specs=(VMEM,) * len(out_shape) if many else VMEM,
        scratch_shapes=list(scratch),
        compiler_params=pltpu.CompilerParams(vmem_limit_bytes=VMEM_LIMIT),
        name=name,
    )(*operands)


def pack_kernel(*refs):
    given, (packed, tail), held, done = refs[:4], refs[5:7], refs[7:11], refs[11]
    copies = [pltpu.make_async_copy(given[at], held[at], done.at[at]) for at in range(4)]
    for copy in copies:
        copy.start()
    for copy in copies:
        copy.wait()
    encoder, layers, head, biases = held
    encoder_rows, layer_rows, rows = encoder.shape[0], layers.shape[1], head.shape[0]
    tail[...] = jnp.zeros_like(tail)
    tail[:, : head.shape[1]] = head[...]
    tail[: biases.shape[0], PAD_AT : PAD_AT + biases.shape[1]] = biases[...]
    for odd in range(2):

        @pl.when((lax.axis_index("rep") & 1) == odd)
        def _(columns=slice(odd * LANES, (odd + 1) * LANES), half=slice(odd * rows // 2, (odd + 1) * rows // 2)):
            packed[:encoder_rows] = encoder[:, columns].astype(bf16)
            for layer in range(LAYERS):
                start = encoder_rows + layer * layer_rows
                packed[start : start + layer_rows] = layers[layer, :, columns].astype(bf16)
            packed[encoder_rows + LAYERS * layer_rows :] = tail[half].astype(bf16)


def assemble_kernel(mine, theirs, *outs, sizes, order):
    for odd in range(2):

        @pl.when((lax.axis_index("rep") & 1) == odd)
        def _(low=(mine, theirs)[odd], high=(theirs, mine)[odd]):
            bias_total = None
            for shard in range(mine.shape[0]):
                node = lax.axis_index("nodes") ^ order[shard]
                start = 0
                for out, rows in zip(outs, sizes):
                    at = pl.ds(pl.multiple_of(node * rows, rows), rows)
                    part = slice(start, start + rows)
                    out[at, :LANES] = low[shard, part]
                    out[at, LANES:] = high[shard, part]
                    start += rows
                if len(outs) == len(sizes):
                    continue
                head, bias_rows = outs[len(sizes) :]
                rows = head.shape[0] // mine.shape[0]
                half = rows // 2
                at = pl.multiple_of(node * rows, rows)
                head[pl.ds(at, half)] = low[shard, start:]
                head[pl.ds(pl.multiple_of(at + half, half), half)] = high[shard, start:]
                columns = bias_rows.shape[1] // mine.shape[0]
                bias = low[shard, start:].astype(f32)
                if half < 8:
                    bias = jnp.concatenate([bias, high[shard, start:].astype(f32)], axis=0)
                bias = bias[: bias_rows.shape[0]]
                lane = lax.broadcasted_iota(jnp.int32, bias.shape, 1)
                bias = jnp.where((lane >= PAD_AT) & (lane < PAD_AT + columns), bias, 0.0)
                wide = jnp.concatenate([bias, jnp.zeros_like(bias)], axis=1)
                wide = pltpu.roll(wide, (node * columns + bias_rows.shape[1] - PAD_AT) % bias_rows.shape[1], 1)
                bias_total = wide if bias_total is None else bias_total + wide
            if bias_total is not None:
                outs[-1][...] = bias_total


def gradient_kernel(
    rounded, averaged, low_grad, features, means, low_self, low_mean, *refs, groups
):
    *others, head, away, kept, encoder_grad, layer_grad = refs
    width = low_grad.shape[1]
    encoder_grad[...] = dot_rows(features[...], low_self[...]) + dot_rows(means[...], low_mean[...])
    layer_grad[:width] = dot_rows(rounded[...], low_grad[...])
    layer_grad[width:] = dot_rows(averaged[...], low_grad[...])
    sources = [encoder_grad, layer_grad] + list(others)
    for odd in range(2):

        @pl.when((lax.axis_index("rep") & 1) == odd)
        def _(odd=odd):
            mine = slice(odd * LANES, (odd + 1) * LANES)
            other = slice((1 - odd) * LANES, (2 - odd) * LANES)
            for node in range(groups):
                start = 0
                for source in sources:
                    rows = source.shape[0] // groups
                    at, put = slice(node * rows, (node + 1) * rows), slice(start, start + rows)
                    kept[node, put] = source[at, mine]
                    away[node, put] = source[at, other].astype(bf16)
                    start += rows
                half = head.shape[0] // groups // 2
                low, high = (2 * node + odd) * half, (2 * node + 1 - odd) * half
                kept[node, start:] = head[low : low + half]
                away[node, start:] = head[high : high + half].astype(bf16)


def total_at(parts, *index):
    sums = [part[index].astype(f32) for part in parts]
    while len(sums) > 1:
        sums = [one + other for one, other in zip(sums[0::2], sums[1::2])]
    return sums[0]


def first_cut_kernel(kept, received, own, *sent):
    half = own.shape[1]
    for place in range(own.shape[0]):
        for mask, out in enumerate((own, *sent)):
            node = 2 * place + ((lax.axis_index("nodes") & 1) ^ (mask & 1))
            rows = ((lax.axis_index("rep") >> 1) & 1) ^ (mask >> 1)
            rows = pl.ds(pl.multiple_of(rows * half, half), half)
            out[place] = total_at((kept, received), node, rows).astype(out.dtype)


def cut_kernel(*refs, count, bit, ways):
    parts, outs = refs[:count], refs[count:]
    mine = lax.axis_index("nodes") // bit & (ways - 1)
    for place in range(outs[0].shape[0]):
        for mask, out in enumerate(outs):
            out[place] = total_at(parts, ways * place + (mine ^ mask)).astype(out.dtype)


def last_kernel(own, received, sums, other_sums, out):
    owners, rows = own.shape[:2]
    mine = lax.axis_index("nodes") // (lax.axis_size("nodes") // owners)
    out[:rows] = total_at((own, received), mine)
    squares = None
    for owner in range(owners):
        grad = total_at((own, received), owner)
        one = jnp.sum((grad * grad).reshape(rows // 8, 8, LANES), axis=0)
        squares = one if squares is None else squares + one
    out[rows : rows + 8] = squares
    out[rows + 8 :] = sums[...] + other_sums[...]


def update_kernel(*refs):
    (mine_ref, theirs), rest = refs[:2], refs[2:]
    params, firsts, seconds = rest[:5], rest[5:10], rest[10:15]
    updated, drifts, spreads, copied = rest[15:20], rest[20:25], rest[25:30], rest[30:34]
    loss_ref, count_ref, norm_ref, grad = rest[34:]
    quarter = (mine_ref.shape[0] - 24) // 2
    tile = mine_ref[2 * quarter :] + theirs[2 * quarter :]
    high, odd = (lax.axis_index("rep") >> 1) & 1, lax.axis_index("rep") & 1
    upper = pl.multiple_of(high * quarter, quarter)
    lower = pl.multiple_of((1 - high) * quarter, quarter)
    mine = pl.ds(pl.multiple_of(odd * LANES, LANES), LANES)
    other = pl.ds(pl.multiple_of((1 - odd) * LANES, LANES), LANES)
    grad[pl.ds(upper, quarter), mine] = mine_ref[:quarter]
    grad[pl.ds(lower, quarter), mine] = mine_ref[quarter : 2 * quarter]
    grad[pl.ds(upper, quarter), other] = theirs[:quarter]
    grad[pl.ds(lower, quarter), other] = theirs[quarter : 2 * quarter]

    classes = params[4].shape[1]
    lane = lax.broadcasted_iota(jnp.int32, (1, LANES), 1)
    class_row = tile[8:9]
    class_grad = jnp.where(lane < classes, class_row, 0.0)
    bias_low, bias_high = tile[16:20], tile[20:24]
    squares = (
        jnp.sum(tile[:8], keepdims=True)
        + jnp.sum(class_grad * class_grad, keepdims=True)
        + jnp.sum(bias_low * bias_low, keepdims=True)
        + jnp.sum(bias_high * bias_high, keepdims=True)
    )
    norm = jnp.sqrt(squares)
    scale = jnp.minimum(1.0, 1.0 / (norm + 1e-06))
    loss_ref[...] = jnp.sum(jnp.where(lane == classes, class_row, 0.0), axis=1, keepdims=True)
    count_ref[...] = jnp.sum(jnp.where(lane == classes + 1, class_row, 0.0), axis=1, keepdims=True)
    norm_ref[...] = norm

    encoder_rows, layer_rows = params[0].shape[0], params[1].shape[1]
    ends = encoder_rows + LAYERS * layer_rows
    head_half = params[2].shape[0] // 2
    columns = params[3].shape[1]
    width = 2 * LANES
    biases = jnp.concatenate([bias_low, bias_high], axis=1)
    biases = pltpu.roll(biases, (width - lax.axis_index("nodes") * columns) % width, 1)[:, :columns]

    def step(index, at, gradient):
        new, drift, spread = adamw(params[index][at], firsts[index][at], seconds[index][at], gradient, scale)
        updated[index][at] = new
        drifts[index][at] = drift
        spreads[index][at] = spread
        if index < 4:
            copied[index][at] = new.astype(bf16)

    step(0, slice(None), grad[:encoder_rows])
    for layer in range(LAYERS):
        start = encoder_rows + layer * layer_rows
        step(1, layer, grad[start : start + layer_rows])
    step(2, slice(0, head_half), grad[ends:, :LANES][:, :classes])
    step(2, slice(head_half, 2 * head_half), grad[ends:, LANES:][:, :classes])
    step(3, slice(None), biases)
    step(4, slice(None), class_grad[:, :classes])


def adamw(weight, first, second, grad, scale):
    scaled = grad * scale
    drift = beta_one * first + (1.0 - beta_one) * scaled
    spread = beta_two * second + (1.0 - beta_two) * scaled * scaled
    corrected = drift / (1.0 - beta_one**STEP)
    denominator = jnp.sqrt(spread / (1.0 - beta_two**STEP)) + epsilon
    return (weight - rate * (corrected / denominator + decay * weight), drift, spread)


def plain_pack(encoder, layers, head, biases):
    head = jnp.pad(head, ((0, 0), (0, PAD_AT - head.shape[1])))
    bias = jnp.pad(biases, ((0, head.shape[0] - biases.shape[0]), (0, LANES - PAD_AT - biases.shape[1])))
    tail = jnp.concatenate([head, bias], axis=1)
    half = tail.shape[0] // 2
    tail = jnp.concatenate([tail[:half], tail[half:]], axis=1)
    odd = (lax.axis_index("rep") & 1) == 1
    rows = jnp.concatenate([encoder, *layers, tail], axis=0)
    return jnp.where(odd, rows[:, LANES:], rows[:, :LANES]).astype(bf16)


def plain_assemble(mine, theirs, order, sizes):
    places = [0] * len(order)
    for place, node in enumerate(order):
        places[node] = place
    places = jnp.asarray(places)[lax.axis_index("nodes") ^ jnp.arange(len(order))]
    mine, theirs = jnp.take(mine, places, axis=0), jnp.take(theirs, places, axis=0)
    odd = (lax.axis_index("rep") & 1) == 1
    rows = jnp.concatenate([jnp.where(odd, theirs, mine), jnp.where(odd, mine, theirs)], axis=2)
    outs, start = [], 0
    for size in sizes:
        outs.append(rows[:, start : start + size].reshape(-1, rows.shape[2]))
        start += size
    if start < rows.shape[1]:
        tail = rows[:, start:]
        tail = jnp.concatenate([tail[..., :LANES], tail[..., LANES:]], axis=1)
        columns = rows.shape[2] // len(order)
        bias = tail[:, : LAYERS + 1, PAD_AT : PAD_AT + columns].astype(f32)
        outs += [tail.reshape(-1, LANES), jnp.swapaxes(bias, 0, 1).reshape(LAYERS + 1, rows.shape[2])]
    return outs


def plain_gradients(rounded, averaged, low_grad, features, means, low_self, low_mean, *rest, groups):
    *others, head = rest
    encoder = dot_rows(features, low_self) + dot_rows(means, low_mean)
    layer = jnp.concatenate([dot_rows(rounded, low_grad), dot_rows(averaged, low_grad)], axis=0)
    parts = [part.reshape(groups, -1, part.shape[1]) for part in (encoder, layer, *others, head)]
    half = parts[-1].shape[1] // 2
    parts[-1] = jnp.concatenate([parts[-1][:, :half], parts[-1][:, half:]], axis=2)
    rows = jnp.concatenate(parts, axis=1)
    odd = (lax.axis_index("rep") & 1) == 1
    low, high = rows[..., :LANES], rows[..., LANES:]
    return jnp.where(odd, low, high).astype(bf16), jnp.where(odd, high, low)


def plain_first_cut(kept, received):
    total = kept + received.astype(f32)
    half = total.shape[1] // 2
    total = total.reshape(total.shape[0] // 2, 2, 2, half, LANES)
    outs = []
    for mask in range(4):
        node = (lax.axis_index("nodes") & 1) ^ (mask & 1)
        rows = ((lax.axis_index("rep") >> 1) & 1) ^ (mask >> 1)
        part = lax.dynamic_slice(total, (0, node, rows, 0, 0), (total.shape[0], 1, 1, half, LANES))
        outs.append(part.reshape(-1, half, LANES).astype(bf16 if mask else f32))
    return outs


def plain_last(own, received, sums, other_sums):
    grad = own.astype(f32) + received.astype(f32)
    squares = jnp.pad(jnp.sum(grad * grad, axis=(0, 1))[None], ((0, 7), (0, 0)))
    mine = lax.axis_index("nodes") // (lax.axis_size("nodes") // own.shape[0])
    grad = lax.dynamic_index_in_dim(grad, mine, 0, keepdims=False)
    return jnp.concatenate([grad, squares, sums + other_sums], axis=0)


def plain_update(mine, theirs, *rest):
    params, firsts, seconds = rest[:5], rest[5:10], rest[10:15]
    quarter = (mine.shape[0] - 24) // 2
    tile = mine[2 * quarter :] + theirs[2 * quarter :]
    high, odd = (lax.axis_index("rep") >> 1) & 1 == 1, lax.axis_index("rep") & 1 == 1
    sides = []
    for part in (mine, theirs):
        one, other = part[:quarter], part[quarter : 2 * quarter]
        sides.append(jnp.concatenate([jnp.where(high, other, one), jnp.where(high, one, other)], axis=0))
    rows = jnp.concatenate([jnp.where(odd, *sides[::-1]), jnp.where(odd, *sides)], axis=1)
    classes = params[4].shape[1]
    class_grad = tile[8:9, :classes]
    biases = jnp.concatenate([tile[16:20], tile[20:24]], axis=1)
    norm = jnp.sqrt(jnp.sum(tile[:8]) + jnp.sum(class_grad * class_grad) + jnp.sum(biases * biases))
    scale = jnp.minimum(1.0, 1.0 / (norm + 1e-06))
    encoder_rows, layer_rows = params[0].shape[0], params[1].shape[1]
    ends = encoder_rows + LAYERS * layer_rows
    columns = params[3].shape[1]
    grads = (
        rows[:encoder_rows],
        rows[encoder_rows:ends].reshape(LAYERS, layer_rows, -1),
        jnp.concatenate([rows[ends:, :LANES], rows[ends:, LANES:]], axis=0)[:, :classes],
        lax.dynamic_slice_in_dim(biases, lax.axis_index("nodes") * columns, columns, axis=1),
        class_grad,
    )
    results = [adamw(params[at], firsts[at], seconds[at], grads[at], scale) for at in range(5)]
    new = [entry[0] for entry in results]
    scalars = (tile[8, classes], tile[8, classes + 1], norm)
    return (
        *new, *[entry[1] for entry in results], *[entry[2] for entry in results],
        *[entry.astype(bf16) for entry in new[:4]], *scalars,
    )


def per_device(
    features,
    node_count,
    neighbours,
    neighbour_count,
    label_mask,
    labels,
    encoder_weight,
    layer_weights,
    head_weight,
    biases,
    class_bias,
    mean_encoder,
    mean_layers,
    mean_head,
    mean_biases,
    mean_class,
    square_encoder,
    square_layers,
    square_head,
    square_biases,
    square_class,
):
    node_rows = features.shape[0]
    fan = neighbours.shape[1]
    width = encoder_weight.shape[1]
    classes = class_bias.shape[0]
    groups = lax.axis_size("nodes")
    copies = lax.axis_size("rep")
    here_node = lax.axis_index("nodes")
    member = lax.axis_index("rep")
    encoder_rows, layer_rows, bias_columns = (
        encoder_weight.shape[0],
        layer_weights.shape[1],
        biases.shape[1],
    )

    owner = jnp.floor_divide(neighbours, node_rows)
    group = jnp.floor_divide(owner, copies)
    offset = jnp.where(group == here_node, 1, jnp.where(group == here_node ^ 1, 0, 2))
    codes = (offset * copies + jnp.mod(owner, copies)) * node_rows + jnp.mod(neighbours, node_rows)
    edge_live = lax.broadcasted_iota(jnp.int32, neighbours.shape, 1) < neighbour_count[:, None]
    codes = jnp.where(edge_live, codes, -1).reshape(node_rows * fan // BATCH, BATCH)
    codes = split_codes(codes)
    to_around = jnp.concatenate([features, codes], axis=0)
    partner, _, other = around_of(to_around)
    blocks = [codes]
    for bit in bits_of("rep"):
        blocks = blocks + [swap(block, "rep", bit) for block in blocks]
    second = build_table(blocks[1], None, node_rows, copies, fan)
    partner, other, second, *blocks[2:] = tied(partner, other, second, *blocks[2:])
    column_tables = [
        second if block is blocks[1] else build_table(block, None, node_rows, copies, fan) for block in blocks
    ]

    head_rows = head_weight.shape[0]
    aligned = encoder_rows % 16 == 0 and layer_rows % 16 == 0 and head_rows % 32 == 0
    rows = encoder_rows + LAYERS * layer_rows + head_rows // 2
    weights = (encoder_weight, layer_weights, head_weight, biases)
    in_hbm = [pltpu.with_memory_space_constraint(weight, pltpu.HBM) for weight in weights] if aligned else []
    own_weights = plain_pack(*weights) if not aligned else kernel_call(
        pack_kernel,
        "pack_weights",
        jax.ShapeDtypeStruct((rows, LANES), bf16),
        (*in_hbm, codes),
        (
            pltpu.VMEM((head_rows, LANES), f32),
            *[pltpu.VMEM(weight.shape, f32) for weight in weights],
            pltpu.SemaphoreType.DMA((4,)),
        ),
        pl.BlockSpec(memory_space=pltpu.HBM),
    )
    def over_nodes(part, beside):
        part, order = part[None], [0]
        for bit in bits_of("nodes")[::-1]:
            part = jnp.concatenate([part, swap(part, "nodes", bit)], axis=0)
            order = order + [node ^ bit for node in order]
            if beside:
                part, _ = tied(part, beside[0])
                beside = beside[1:]
        return part, order

    own_weights, order = over_nodes(own_weights, column_tables[:2])
    *feature_products, sent = nodes_first_products(
        column_tables, None, (partner[:node_rows], features, other[:node_rows]), copies, False
    )
    local_rows = lax.broadcasted_iota(jnp.int32, (node_rows,), 0)
    valid_node = (local_rows < node_count[0]).astype(f32)[:, None]
    inverse_count = (1.0 / neighbour_count.astype(f32))[:, None]
    weight_mask = label_mask.astype(f32)[:, None] * valid_node
    low_labels = labels.astype(f32)

    def meanwhile(partner, other, held):
        return (
            build_table(partner, 0, node_rows, copies, fan),
            other,
            held,
            swap(held, "rep", 1),
        )

    feature_sums, (*row_tables, mine, theirs) = added_over_group(
        *feature_products, sent, (meanwhile, partner[node_rows:], other[node_rows:], own_weights)
    )
    row_tables = [row_tables[0], *[build_table(block, place, node_rows, copies, fan) for place, block in ((1, codes), (2, row_tables[1]))]]
    gathered = (mine, theirs)
    sizes = (encoder_rows,) + (layer_rows,) * LAYERS
    encoder, *layers, head, bias_rows = plain_assemble(*gathered, order, sizes) if not aligned else kernel_call(
        functools.partial(assemble_kernel, sizes=sizes, order=order),
        "assemble_weights",
        tuple(jax.ShapeDtypeStruct((groups * size, width), bf16) for size in sizes)
        + (
            jax.ShapeDtypeStruct((groups * head_rows, LANES), bf16),
            jax.ShapeDtypeStruct((min(8, head_rows), width), f32),
        ),
        gathered,
    )
    feature_mean = (feature_sums * inverse_count).astype(bf16)

    rounded = ((dot(features, encoder) + bias_rows[0:1]) * valid_node).astype(bf16)
    averaged = (dot(feature_mean, encoder) + bias_rows[0:1]).astype(bf16)
    low_self_input = (rounded, averaged)
    kept_joined = []
    kept_before = []
    for layer in range(LAYERS):
        if layer > 0:
            sums, kept_early = exchanged(
                rounded, column_tables, row_tables, False, early=(low_labels, weight_mask) if layer == 1 else ()
            )
            if layer == 1:
                low_labels, weight_mask = kept_early
            averaged = (sums * inverse_count).astype(bf16)
        joined = jnp.concatenate([rounded, averaged], axis=1)
        before = dot(joined, layers[layer]) + bias_rows[layer + 1 : layer + 2]
        kept_joined.append(joined)
        kept_before.append(before)
        rounded = act_norm(before).astype(bf16)

    class_ids = lax.broadcasted_iota(jnp.int32, (1, LANES), 1)
    padded_bias = jnp.pad(class_bias, (0, LANES - classes))
    logits = jnp.where(class_ids < classes, dot(rounded, head) + padded_bias, -1e30)
    total_exp = jax.nn.logsumexp(logits, axis=1, keepdims=True)
    target = (class_ids.astype(f32) == low_labels[:, None]).astype(f32)
    picked = jnp.sum(logits * target, axis=1, keepdims=True)
    grad_logits = (jnp.exp(logits - total_exp) - target) * weight_mask
    sums = jnp.where(class_ids == classes, weight_mask * (total_exp - picked), grad_logits)
    sums = jnp.where(class_ids == classes + 1, weight_mask, sums)
    class_tile = jnp.sum(sums, axis=0, keepdims=True)
    low_logits = grad_logits.astype(bf16)
    grad_head = dot_rows(rounded, low_logits)
    grad_hidden = dot_columns(low_logits, head)

    grad_weights = [None] * LAYERS
    grad_bias_rows = [None] * (LAYERS + 1)
    for layer in reversed(range(LAYERS)):
        _, pullback = jax.vjp(act_norm, kept_before[layer])
        grad_before = pullback(grad_hidden)[0]
        grad_bias_rows[layer + 1] = jnp.sum(grad_before, axis=0, keepdims=True)
        low_grad = grad_before.astype(bf16)
        grad_joined = dot_columns(low_grad, layers[layer])
        grad_self, grad_mean = halves(grad_joined)
        if layer > 0:
            low_grad_sum = (grad_mean * inverse_count).astype(bf16)
            received, (grad_weights[layer],) = exchanged(
                low_grad_sum, column_tables, row_tables, True, (kept_joined[layer], low_grad)
            )
            grad_hidden = grad_self + received
    grad_self = grad_self * valid_node
    grad_bias_rows[0] = jnp.sum(grad_self + grad_mean, axis=0, keepdims=True)
    inputs = (
        *low_self_input,
        low_grad,
        features,
        feature_mean,
        grad_self.astype(bf16),
        grad_mean.astype(bf16),
        *grad_weights[1:],
        grad_head,
    )
    away, grads = plain_gradients(*inputs, groups=groups) if not aligned else kernel_call(
        functools.partial(gradient_kernel, groups=groups),
        "gradients",
        (
            jax.ShapeDtypeStruct((groups, rows, LANES), bf16),
            jax.ShapeDtypeStruct((groups, rows, LANES), f32),
        ),
        inputs,
        (pltpu.VMEM((features.shape[1], width), f32), pltpu.VMEM((2 * width, width), f32)),
    )

    received = swap(away, "rep", 1)
    half = rows // 2
    own, *sent = plain_first_cut(grads, received) if not aligned else kernel_call(
        first_cut_kernel,
        "first_cut",
        tuple(jax.ShapeDtypeStruct((groups // 2, half, LANES), kind) for kind in (f32, bf16, bf16, bf16)),
        (grads, received),
    )
    received = [swap_both(part, mask & 1, (mask >> 1) * 2) for mask, part in enumerate(sent, 1)]
    *steps, last_step = bits_of("nodes")[1:]
    bias_grads = [row[:, side * LANES : (side + 1) * LANES] for side in range(2) for row in grad_bias_rows]
    sums = jnp.concatenate([jnp.broadcast_to(class_tile, (8, LANES)), *bias_grads], axis=0)
    other_sums = swap(sums, "nodes", last_step)
    received[0], other_sums = tied(received[0], other_sums)
    for bit in steps:
        parts = (own, *received)
        kinds = (f32, bf16)
        own, sent = kernel_call(
            functools.partial(cut_kernel, count=len(parts), bit=bit, ways=2),
            "cut",
            tuple(jax.ShapeDtypeStruct((own.shape[0] // 2, half, LANES), kind) for kind in kinds),
            parts,
        )
        received = (swap(sent, "nodes", bit),)
    own = total_at((own, *received), slice(None)).astype(bf16)
    received = swap(own, "nodes", last_step), sums, other_sums
    inputs = (own, *received)
    grads = plain_last(*inputs) if not aligned else pl.pallas_call(
        last_kernel,
        out_shape=jax.ShapeDtypeStruct((half + 24, LANES), f32),
        in_specs=[VMEM] * 4,
        out_specs=VMEM,
        compiler_params=pltpu.CompilerParams(vmem_limit_bytes=VMEM_LIMIT),
        name="last_sum",
    )(*inputs)

    tile = grads[half:]
    for bit in steps:
        tile = tile + swap(tile, "nodes", bit)
    across, other, both = (
        swap_both(tile, 1, 0),
        swap(jnp.concatenate([grads[:half], tile], axis=0), "rep", 2),
        swap_both(tile, 1, 2),
    )
    tile = total_at((tile, across, other[half:], both), slice(None))
    grads = jnp.concatenate([grads[:half], other[:half], tile], axis=0)
    received = swap(grads, "rep", 1)

    params = (encoder_weight, layer_weights, head_weight, biases, class_bias[None])
    firsts = (mean_encoder, mean_layers, mean_head, mean_biases, mean_class[None])
    seconds = (square_encoder, square_layers, square_head, square_biases, square_class[None])
    shapes = tuple(jax.ShapeDtypeStruct(param.shape, f32) for param in params)
    lows = tuple(jax.ShapeDtypeStruct(param.shape, bf16) for param in params[:4])
    inputs = (grads, received, *params, *firsts, *seconds)
    results = plain_update(*inputs) if not aligned else pl.pallas_call(
        update_kernel,
        out_shape=shapes * 3 + lows + (jax.ShapeDtypeStruct((1, 1), f32),) * 3,
        in_specs=[VMEM] * 17,
        out_specs=(VMEM,) * 22,
        scratch_shapes=[pltpu.VMEM((rows, width), f32)],
        compiler_params=pltpu.CompilerParams(vmem_limit_bytes=VMEM_LIMIT),
        name="adamw",
    )(*inputs)
    results, scalars = list(results[:19]), results[19:]
    for index in (4, 9, 14):
        results[index] = results[index][0]
    return tuple(results) + tuple(scalar.reshape(()) for scalar in scalars)


def solution(mesh):
    node_arrays = (
        P(("nodes", "rep"), None),
        P(("nodes", "rep")),
        P(("nodes", "rep"), None),
        P(("nodes", "rep")),
        P(("nodes", "rep")),
        P(("nodes", "rep")),
    )
    weights = (P("nodes", None), P(None, "nodes", None), P("nodes", None), P(None, "nodes"), P())
    return jax.shard_map(
        per_device,
        mesh=mesh,
        in_specs=node_arrays + weights * 3,
        out_specs=weights * 3 + weights[:4] + (P(), P(), P()),
        check_vma=False,
    )
```
